32 devices in a mesh: section: 8 (over z, x), head: 4 (over y, core).
Axes of the slice: x: 2, y: 2, z: 4, core: 2. Of those that a mesh axis runs over, the one named last changes fastest.
Arguments:
- entering: bfloat16 [8, 128, 4096], P('section', None, 'head'), may hold values from -6 to 6, as said below
- fresh_slice: bfloat16 [128, 4096], P(None, 'head'), may hold values from -6 to 6
- norm_gain: float32 [8, 4096], P('section'), may hold values from 0.5 to 1.5
- w_query: bfloat16 [8, 4096, 4096], P('section', None, 'head'), may hold values from -18.8125 to 18.8125
- w_key_value: bfloat16 [8, 4096, 1024], P('section', None, 'head'), may hold values from -0.0625 to 0.0625
- doc_lengths: int32 [9], replicated, may hold values from 1 to 512, 1152 in all
Outputs:
- leaving: bfloat16 [8, 128, 4096], P('section', None, 'head')
The draws below stay inside these ranges and needn't reach their ends.
Inputs may be any that keep to these rules, and one draw needn't show every extreme that they name: `entering`: entries of the activations that enter.
All inputs are finite; a program needn't handle non-finite values.
Results may differ from the reference program's by a relative error of at most 0.01.
Values may be sent and summed in bfloat16 or wider, within the bound.
No kernel may reach another device: no remote copies, remote signals or barrier semaphores. Data moves between devices by JAX's collectives and lax.ppermute only.
A program may use at most 64 MiB of HBM per device.

```python
import math
import jax
import jax.numpy as jnp
import numpy as np
from jax import lax

HD = 128
HQ = 32
KVH = 4
SLICE = 128
GROUP = 8
DW = 4096
PACK = 1152
NDOC = 9
MOST = 512
N_SECTION = 8


def draw_entering(key, part):
    columns = jnp.arange(DW, dtype=jnp.float32) / DW
    raw_values = jax.random.truncated_normal(key, -6.0, 6.0, (N_SECTION, SLICE, DW), jnp.float32)
    return (raw_values * jnp.exp(columns * math.log(3.0))[None, None, :] / 3.0).astype(jnp.bfloat16)


def joint_weights(key):
    base_key = jax.random.fold_in(key, 101)
    kv_rows = jax.random.truncated_normal(jax.random.fold_in(base_key, 1), -4.0, 4.0, (N_SECTION, DW, 2 * KVH * HD), jnp.float32) / math.sqrt(DW)
    noise_part = jax.random.truncated_normal(jax.random.fold_in(base_key, 2), -4.0, 4.0, (N_SECTION, DW, HQ * HD), jnp.float32) / math.sqrt(DW)
    query_rows = noise_part
    return (query_rows, kv_rows)


def draw_w_query(key, part):
    return joint_weights(key)[0].astype(jnp.bfloat16)


def draw_w_key_value(key, part):
    return joint_weights(key)[1].astype(jnp.bfloat16)


def steps_of(rng, extent, shards, smallest, high):
    gain = 1.0
    for dim, shards_of in shards:
        heights = jax.random.uniform(jax.random.fold_in(jax.random.fold_in(rng, 6), dim), (shards_of,), jnp.float32, smallest / len(shards), high / len(shards))
        gain = gain * jnp.repeat(jnp.exp(heights), extent[dim] // shards_of).reshape((-1,) + (1,) * (len(extent) - 1 - dim))
    return gain


def profile(count, total, bound, slope):
    weights = [(1 << 20) // math.isqrt(rank ** slope) + 1 for rank in range(2, count + 1)]
    spare, holding = total - bound - (count - 1), [1] * (count - 1)
    while spare > 0:
        free = [i for i in range(count - 1) if holding[i] < bound]
        whole, left = sum([weights[i] for i in free]), spare
        for i in free:
            extra = min(bound - holding[i], max(1, left * weights[i] // whole), spare)
            holding[i] = holding[i] + extra
            spare = spare - extra
    return np.array([bound] + holding)


def ragged(key, amount, total, reach, slope):
    if amount == 2:
        one = jax.random.randint(key, (), max(1, total - reach), min(reach, total - 1) + 1)
        return jnp.stack([one, total - one])
    lengths = jnp.asarray(profile(amount, total, reach, slope), jnp.int32)
    couples = (amount - 1) // 2
    donor, receiver = lengths[1:1 + 2 * couples:2], lengths[2:2 + 2 * couples:2]
    slack = jnp.minimum(donor - 1, reach - receiver)
    shifted = jax.random.randint(jax.random.fold_in(key, 1), (couples,), 0, 1 << 20) % (slack + 1)
    lengths = lengths.at[1:1 + 2 * couples:2].set(donor - shifted).at[2:2 + 2 * couples:2].set(receiver + shifted)
    return lengths[jax.random.permutation(jax.random.fold_in(key, 2), amount)]


def scatter_about(key, dims, scale, bound, pieces=(), kind=jnp.bfloat16):
    drawn = scale * jax.random.normal(key, dims, jnp.float32)
    if pieces:
        drawn = drawn * steps_of(key, dims, pieces, -0.22, 0.18)
    return jnp.clip(drawn, -bound, bound).astype(kind)


def setup_inputs(seed: int = 0) -> dict:
    key_of = jax.random.split(jax.random.key(seed), 7)
    entering = draw_entering(jax.random.fold_in(key_of[6], 71), 0)
    fresh_slice = scatter_about(key_of[1], (SLICE, DW), 1.0, 6.0, ((1, 4),))
    norm_gain = jnp.clip(1.0 + 0.1 * jax.random.normal(key_of[2], (N_SECTION, DW), jnp.float32), 0.5, 1.5)
    w_query = draw_w_query(jax.random.fold_in(key_of[6], 71), 0)
    w_key_value = draw_w_key_value(jax.random.fold_in(key_of[6], 71), 0)
    doc_lengths = ragged(key_of[5], NDOC, PACK, MOST, 2).astype(jnp.int32)
    return {"entering": entering, "fresh_slice": fresh_slice, "norm_gain": norm_gain, "w_query": w_query, "w_key_value": w_key_value, "doc_lengths": doc_lengths}


epsilon = 1e-05
masked_score = -1e+30

def doc_index(position, doc_ends):
    return lax.optimization_barrier(jnp.sum((doc_ends[None, :] <= position[:, None]).astype(jnp.int32), axis=1))

def attend_block(query_block, query_pos, query_doc, all_keys, all_values, key_pos, key_doc):
    scores = jnp.einsum('qghd,kgd->ghqk', query_block.astype(jnp.float32), all_keys.astype(jnp.float32)) / math.sqrt(HD)
    allowed = (key_pos[None, :] <= query_pos[:, None]) & (key_doc[None, :] == query_doc[:, None])
    scores = jnp.where(allowed[None, None], scores, masked_score)
    row_max = lax.optimization_barrier(jnp.max(scores, axis=-1, keepdims=True))
    expon = jnp.exp(scores - row_max)
    weights = (expon / lax.optimization_barrier(jnp.sum(expon, axis=-1, keepdims=True))).astype(jnp.bfloat16)
    mixed = jnp.einsum('ghqk,kgd->qghd', weights.astype(jnp.float32), all_values.astype(jnp.float32))
    return mixed.astype(jnp.bfloat16)

def section_layer(row_data, gain_row, w_q, w_kv, start, doc_ends, resident):
    slice_len = row_data.shape[0]
    widened = row_data.astype(jnp.float32)
    mean_sq = lax.optimization_barrier(jnp.mean(widened * widened, axis=1, keepdims=True))
    normed = (widened * lax.rsqrt(mean_sq + epsilon) * gain_row[None, :]).astype(jnp.bfloat16)
    queries = jnp.dot(normed, w_q, preferred_element_type=jnp.float32).astype(jnp.bfloat16)
    packed = jnp.dot(normed, w_kv, preferred_element_type=jnp.float32).astype(jnp.bfloat16)
    packed = packed.reshape(slice_len, HD, KVH, 2)
    new_keys = jnp.transpose(packed[:, :, :, 0], (0, 2, 1))
    new_values = jnp.transpose(packed[:, :, :, 1], (0, 2, 1))
    position = start + jnp.arange(slice_len, dtype=jnp.int32)
    if resident is None:
        all_keys, all_values, key_pos = (new_keys, new_values, position)
    else:
        all_keys = jnp.concatenate([resident[0], new_keys], axis=0)
        all_values = jnp.concatenate([resident[1], new_values], axis=0)
        key_pos = jnp.concatenate([resident[2], position], axis=0)
    key_doc = doc_index(key_pos, doc_ends)
    query_doc = doc_index(position, doc_ends)
    block_len = min(512, slice_len)
    count = slice_len // block_len
    query_groups = queries.reshape(count, block_len, KVH, GROUP, HD)

    def one_block(block_args):
        return attend_block(block_args[0], block_args[1], block_args[2], all_keys, all_values, key_pos, key_doc)
    attended = lax.map(one_block, (query_groups, position.reshape(count, block_len), query_doc.reshape(count, block_len)))
    attended = attended.reshape(slice_len, HQ * HD).astype(jnp.float32)
    return ((widened + attended).astype(jnp.bfloat16), new_keys, new_values, position)

def reference(entering, fresh_slice, norm_gain, w_query, w_key_value, doc_lengths):
    doc_ends = jnp.cumsum(doc_lengths).astype(jnp.int32)
    sections = entering.shape[0]
    slice_len = entering.shape[1]
    section_ids = jnp.arange(sections, dtype=jnp.int32)

    def first_tick(packed_args):
        section_index, row_data, gain_row, w_q, w_kv = packed_args
        start = (sections - 1 - section_index) * slice_len
        return section_layer(row_data, gain_row, w_q, w_kv, start, doc_ends, None)
    first_out, keys_first, values_first, pos_first = lax.map(first_tick, (section_ids, entering, norm_gain, w_query, w_key_value))
    second_in = jnp.concatenate([fresh_slice[None], first_out[:-1]], axis=0)

    def second_tick(packed_args):
        section_index, row_data, gain_row, w_q, w_kv, old_keys, old_values, old_pos = packed_args
        start = (sections - section_index) * slice_len
        result = section_layer(row_data, gain_row, w_q, w_kv, start, doc_ends, (old_keys, old_values, old_pos))
        return result[0]
    return lax.map(second_tick, (section_ids, second_in, norm_gain, w_query, w_key_value, keys_first, values_first, pos_first))
```

```python
import functools
import math

import jax
import jax.numpy as jnp
from jax import lax
from jax.experimental import pallas as pl
from jax.experimental.pallas import tpu as pltpu
from jax.sharding import PartitionSpec as P

HD = 128
KVH = 4
GROUP = 8

epsilon = 1e-05
masked_score = -1e30

VMEM = pltpu.VMEM
SMEM = pltpu.SMEM
f32 = jnp.float32
bf16 = jnp.bfloat16
vmem = pl.BlockSpec(memory_space=VMEM)
smem = pl.BlockSpec(memory_space=SMEM)
in_hbm = pl.BlockSpec(memory_space=pltpu.HBM)


params = pltpu.CompilerParams(vmem_limit_bytes=16 * 1024 * 1024)


def resident_in(*arrays):
    return [pltpu.with_memory_space_constraint(a, VMEM) for a in arrays]


def cost(flops, moved):
    return pl.CostEstimate(flops=flops, bytes_accessed=moved, transcendentals=0)


def rows_of(block, width):
    return pl.ds(pl.multiple_of(block * width, width), width)


def gained(x, gain_ref, block):
    width = x.shape[1]
    wide = x.astype(f32)
    squares = wide * wide
    ssq = squares[:, :HD]
    for c in range(HD, width, HD):
        ssq = ssq + squares[:, c : c + HD]
    return (wide * gain_ref[:, rows_of(block, width)]).astype(bf16), ssq


def first_block_kernel(
    x_ref, gain_ref, wq_hbm, wkv_hbm, accq_ref, acckv_ref, ssq_ref, wq_ref, wkv_ref, sems
):
    n = wq_hbm.shape[0] // x_ref.shape[1]
    width = x_ref.shape[1]
    me = lax.axis_index("head")

    def copies(step):
        rows = rows_of(lax.rem(me + step, n), width)
        return (
            pltpu.make_async_copy(wkv_hbm.at[rows], wkv_ref.at[rows], sems.at[step, 0]),
            pltpu.make_async_copy(wq_hbm.at[rows], wq_ref.at[rows], sems.at[step, 1]),
        )

    for step in range(n):
        for copy in copies(step):
            copy.start()
    normed, ssq = gained(x_ref[...], gain_ref, me)
    ssq_ref[...] = ssq
    for copy in copies(0):
        copy.wait()
    rows = rows_of(me, width)
    acckv_ref[...] = jnp.dot(normed, wkv_ref[rows, :], preferred_element_type=f32)
    accq_ref[...] = jnp.dot(normed, wq_ref[rows, :], preferred_element_type=f32)
    for step in range(1, n):
        for copy in copies(step):
            copy.wait()


def first_block(x, gain, wq, wkv):
    tokens, width = x.shape
    n = wq.shape[0] // width
    return pl.pallas_call(
        first_block_kernel,
        out_shape=(
            VMEM((tokens, wq.shape[1]), f32),
            VMEM((tokens, wkv.shape[1]), f32),
            VMEM((tokens, HD), f32),
            VMEM(wq.shape, bf16),
            VMEM(wkv.shape, bf16),
        ),
        in_specs=[vmem, vmem, in_hbm, in_hbm],
        out_specs=(vmem,) * 5,
        scratch_shapes=[pltpu.SemaphoreType.DMA((n, 2))],
        cost_estimate=cost(2 * tokens * width * (wq.shape[1] + wkv.shape[1]), 2 * (wq.size + wkv.size)),
        compiler_params=params,
        name="load_and_first_block",
    )(x, gain, *(pltpu.with_memory_space_constraint(w, pltpu.HBM) for w in (wq, wkv)))


def blocks_kernel(count, fresh_start, places, *refs):
    xs, rest = refs[:count], refs[count:]
    if fresh_start:
        gain_ref, wq_ref, wkv_ref, accq_out, acckv_out, ssq_out = rest
    else:
        gain_ref, wq_ref, wkv_ref, accq_ref, acckv_ref, ssq_ref, accq_out, acckv_out, ssq_out = rest
    width = xs[0].shape[1]
    me = lax.axis_index("head")
    for i, x_ref in enumerate(xs):
        block = places[i](me)
        normed, ssq = gained(x_ref[...], gain_ref, block)
        rows = rows_of(block, width)
        kv = jnp.dot(normed, wkv_ref[rows, :], preferred_element_type=f32)
        q = jnp.dot(normed, wq_ref[rows, :], preferred_element_type=f32)
        if i == 0 and fresh_start:
            accq_out[...], acckv_out[...], ssq_out[...] = q, kv, ssq
        elif i == 0:
            accq_out[...] = accq_ref[...] + q
            acckv_out[...] = acckv_ref[...] + kv
            ssq_out[...] = ssq_ref[...] + ssq
        else:
            accq_out[...] += q
            acckv_out[...] += kv
            ssq_out[...] += ssq


def more_blocks(xs, places, gain, wq, wkv, state):
    tokens, width = xs[0].shape
    operands = [*xs, *resident_in(gain, wq, wkv), *(state or ())]
    shapes = ((tokens, wq.shape[1]), (tokens, wkv.shape[1]), (tokens, HD))
    return pl.pallas_call(
        functools.partial(blocks_kernel, len(xs), state is None, places),
        out_shape=tuple(VMEM(s, f32) for s in shapes),
        in_specs=[vmem] * len(operands),
        out_specs=(vmem,) * 3,
        cost_estimate=cost(
            len(xs) * 2 * tokens * width * (wq.shape[1] + wkv.shape[1]), len(xs) * 2 * tokens * width
        ),
        compiler_params=params,
        name="more_blocks",
    )(*operands)


def last_kv_kernel(count, places, *refs):
    xs, rest = refs[:count], refs[count:]
    gain_ref, wkv_ref, acckv_ref, ssq_ref = rest[:4]
    scale_ref, pieces, turned = rest[4], rest[5:-1], rest[-1]
    width = xs[0].shape[1]
    n = lax.axis_size("head")
    me = lax.axis_index("head")
    total, ssq = acckv_ref[...], ssq_ref[...]
    for i, x_ref in enumerate(xs):
        block = places[i](me)
        normed, more = gained(x_ref[...], gain_ref, block)
        ssq = ssq + more
        total = total + jnp.dot(normed, wkv_ref[rows_of(block, width), :], preferred_element_type=f32)
    scale = lax.rsqrt(jnp.sum(ssq, axis=1, keepdims=True) / (n * width) + epsilon)
    scale_ref[...] = jnp.broadcast_to(scale, scale_ref.shape)
    kv = (total * scale).astype(bf16)
    columns = kv.shape[1]
    features = columns // (2 * KVH)
    row = lax.broadcasted_iota(jnp.int32, (columns, columns), 0)
    col = lax.broadcasted_iota(jnp.int32, (columns, columns), 1)
    group, which, feature = row // (2 * features), (row // features) % 2, row % features
    choose = jnp.where(col == (feature * KVH + group) * 2 + which, 1.0, 0.0).astype(bf16)
    turned[...] = lax.dot_general(choose, kv, (((1,), (1,)), ((), ())), preferred_element_type=f32)
    for k in range(n):
        group_there = group_of(lax.rem(me + k, n), n)
        rows = pl.ds(pl.multiple_of(group_there * 2 * features, 2 * features), 2 * features)
        pieces[k][...] = turned[rows, :].astype(bf16)


def group_of(head_index, n):
    return head_index * KVH // n


def last_kv(xs, places, gain, wkv, acckv, ssq, n):
    tokens, width = xs[0].shape
    columns = wkv.shape[1]
    operands = [*xs, *resident_in(gain, wkv), acckv, ssq]
    return pl.pallas_call(
        functools.partial(last_kv_kernel, len(xs), places),
        out_shape=(VMEM((tokens, HD), f32),) + tuple(VMEM((columns // KVH, tokens), bf16) for _ in range(n)),
        in_specs=[vmem] * len(operands),
        out_specs=(vmem,) * (1 + n),
        scratch_shapes=[VMEM((columns, tokens), f32)],
        cost_estimate=cost(len(xs) * 2 * tokens * width * columns, 2 * tokens * width),
        compiler_params=params,
        name="last_block_key_value",
    )(*operands)


def last_q_kernel(count, places, *refs):
    xs, rest = refs[:count], refs[count:]
    gain_ref, wq_ref, accq_ref, scale_ref, q_ref = rest
    width = xs[0].shape[1]
    me = lax.axis_index("head")
    total = accq_ref[...]
    for i, x_ref in enumerate(xs):
        block = places[i](me)
        normed, _ = gained(x_ref[...], gain_ref, block)
        total = total + jnp.dot(normed, wq_ref[rows_of(block, width), :], preferred_element_type=f32)
    q_ref[...] = (total * scale_ref[:, 0:1]).astype(bf16)


def last_q(xs, places, gain, wq, accq, scale):
    tokens, width = xs[0].shape
    operands = [*xs, *resident_in(gain, wq), accq, scale]
    return pl.pallas_call(
        functools.partial(last_q_kernel, len(xs), places),
        out_shape=VMEM((tokens, wq.shape[1]), bf16),
        in_specs=[vmem] * len(operands),
        out_specs=vmem,
        cost_estimate=cost(len(xs) * 2 * tokens * width * wq.shape[1], 2 * tokens * width),
        compiler_params=params,
        name="last_block_queries",
    )(*operands)


def attend_kernel(n, sections, turn, doc_ref, q_ref, x_ref, *refs):
    pieces, rest = refs[:n], refs[n:]
    tokens = q_ref.shape[0]
    me = lax.axis_index("head")
    section = lax.axis_index("section")
    first_start = (sections - 1 - section) * tokens
    features = pieces[0].shape[0] // 2
    if turn == 1:
        fresh_ref, out_ref, keys_ref, values_ref, gather = rest
        start, base = first_start, first_start
    else:
        old_keys, old_values, out_ref, gather = rest
        start, base = first_start + tokens, first_start
    for k in range(n):
        source = lax.rem(me + n - k, n)
        piece = pieces[k][...].astype(f32)
        rows = pl.ds(pl.multiple_of(source * features, features), features)
        gather[0, rows, :] = piece[:features]
        gather[1, rows, :] = piece[features:]
    keys, values = gather[0].astype(bf16), gather[1].astype(bf16)
    if turn == 1:
        keys_ref[...], values_ref[...] = keys, values
    else:
        keys = jnp.concatenate([old_keys[...], keys], axis=1)
        values = jnp.concatenate([old_values[...], values], axis=1)
    here = start + lax.broadcasted_iota(jnp.int32, (tokens, 1), 0)
    there = base + lax.broadcasted_iota(jnp.int32, (1, keys.shape[1]), 1)
    opened = jnp.zeros((tokens, 1), jnp.int32)
    end = jnp.int32(0)
    for d in range(doc_ref.shape[0]):
        end = end + doc_ref[d]
        opened = jnp.where(end <= here, end, opened)
    allowed = (there >= opened) & (there <= here)
    for h in range(q_ref.shape[1] // HD):
        columns = slice(h * HD, (h + 1) * HD)
        scores = jnp.dot(q_ref[:, columns], keys, preferred_element_type=f32) * (1.0 / math.sqrt(HD))
        scores = jnp.where(allowed, scores, masked_score)
        expon = jnp.exp(scores - jnp.max(scores, axis=1, keepdims=True))
        weights = (expon * (1.0 / jnp.sum(expon, axis=1, keepdims=True))).astype(bf16)
        mixed = lax.dot_general(weights, values, (((1,), (1,)), ((), ())), preferred_element_type=f32)
        out = (x_ref[:, columns].astype(f32) + mixed.astype(bf16).astype(f32)).astype(bf16)
        if turn == 1:
            out = jnp.where(section == sections - 1, fresh_ref[:, columns].astype(f32), out.astype(f32)).astype(bf16)
        out_ref[:, columns] = out


def attend(doc_lengths, q, x, pieces, turn, extra, sections):
    n = len(pieces)
    tokens = q.shape[0]
    out = (jax.ShapeDtypeStruct(q.shape, bf16),)
    if turn == 1:
        out = out + (VMEM((HD, tokens), bf16),) * 2
    operands = [doc_lengths, q, x, *pieces, *extra]
    return pl.pallas_call(
        functools.partial(attend_kernel, n, sections, turn),
        out_shape=out,
        in_specs=[smem] + [vmem] * (len(operands) - 1),
        out_specs=(vmem,) * len(out),
        scratch_shapes=[VMEM((2, HD, tokens), f32)],
        cost_estimate=cost(8 * tokens * tokens * q.shape[1], 2 * q.size),
        compiler_params=params,
        name="attend",
    )(*operands)


def shards(entering, fresh_slice, norm_gain, w_query, w_key_value, doc_lengths):
    n = lax.axis_size("head")
    sections = lax.axis_size("section")
    own = entering[0]
    w_q, w_kv = w_query[0], w_key_value[0]
    gain = norm_gain

    def moved(array, by, flip):
        pairs = [
            (s * n + h, ((s + by) % sections) * n + (h ^ flip)) for s in range(sections) for h in range(n)
        ]
        return lax.ppermute(array, ("section", "head"), pairs)

    def turned(array, by):
        return lax.ppermute(array, "head", [(h, (h + by) % n) for h in range(n)])

    def finish(xs, places, wq, wkv, state, x, turn, extra):
        accq, acckv, ssq = state
        scale, *pieces = last_kv(xs, places, gain, wkv, acckv, ssq, n)
        arrived = [pieces[0]] + [turned(pieces[k], k) for k in range(1, n)]
        q = last_q(xs, places, gain, wq, accq, scale)
        return attend(doc_lengths, q, x, arrived, turn, extra, sections)

    paired = n == 4
    xor = [functools.partial(lambda flip, me: lax.bitwise_xor(me, jnp.int32(flip)), flip) for flip in range(4)]
    others = [functools.partial(lambda k, me: lax.rem(me + k, jnp.int32(n)), k) for k in range(n)]

    def rest_of(array):
        every = lax.all_gather(array, "head", axis=0)
        me = lax.axis_index("head")
        return [lax.dynamic_index_in_dim(every, (me + k) % n, 0, False) for k in range(1, n)]

    if paired:
        over = moved(own, 0, 2)
        beside = moved(own, 0, 1)
    *state, wq, wkv = first_block(own, gain, w_q, w_kv)
    if paired:
        over, *state = lax.optimization_barrier((over, *state))
        passed = moved(over, 0, 1)
        state = more_blocks([beside, over], [xor[1], xor[2]], gain, wq, wkv, state)
        last, places = [passed], [xor[3]]
    else:
        last, places = rest_of(own), others[1:]
    sent, keys, values = finish(last, places, wq, wkv, state, own, 1, [fresh_slice])

    if paired:
        mine = moved(sent, 1, 0)
        over = moved(sent, 1, 2)
        beside = moved(mine, 0, 1)
        passed = moved(over, 0, 1)
        state = more_blocks([mine], [xor[0]], gain, wq, wkv, None)
        state = more_blocks([over, beside], [xor[2], xor[1]], gain, wq, wkv, state)
        last, places = [passed], [xor[3]]
    else:
        mine = moved(sent, 1, 0)
        state = more_blocks([mine], [others[0]], gain, wq, wkv, None)
        last, places = rest_of(mine), others[1:]
    return finish(last, places, wq, wkv, state, mine, 2, [keys, values])[0][None]


def solution(mesh):
    placed = (
        P("section", None, "head"),
        P(None, "head"),
        P("section", None),
        P("section", None, "head"),
        P("section", None, "head"),
        P(),
    )
    return jax.shard_map(
        shards, mesh=mesh, in_specs=placed, out_specs=P("section", None, "head"), check_vma=False
    )
```

```python
import functools
import math

import jax
import jax.numpy as jnp
from jax import lax
from jax.experimental import pallas as pl
from jax.experimental.pallas import tpu as pltpu
from jax.sharding import PartitionSpec as P

HD = 128
KVH = 4
GROUP = 8

epsilon = 1e-05
masked_score = -1e30

VMEM = pltpu.VMEM
SMEM = pltpu.SMEM
f32 = jnp.float32
bf16 = jnp.bfloat16
vmem = pl.BlockSpec(memory_space=VMEM)
smem = pl.BlockSpec(memory_space=SMEM)
in_hbm = pl.BlockSpec(memory_space=pltpu.HBM)


params = pltpu.CompilerParams(vmem_limit_bytes=16 * 1024 * 1024)


def resident_in(*arrays):
    return [pltpu.with_memory_space_constraint(a, VMEM) for a in arrays]


def cost(flops, moved):
    return pl.CostEstimate(flops=flops, bytes_accessed=moved, transcendentals=0)


def rows_of(block, width):
    return pl.ds(pl.multiple_of(block * width, width), width)


def gained(x, gain_ref, block):
    width = x.shape[1]
    wide = x.astype(f32)
    squares = wide * wide
    ssq = squares[:, :HD]
    for c in range(HD, width, HD):
        ssq = ssq + squares[:, c : c + HD]
    return (wide * gain_ref[:, rows_of(block, width)]).astype(bf16), ssq


def first_block_kernel(
    x_ref, gain_ref, wq_hbm, wkv_hbm, accq_ref, acckv_ref, ssq_ref, wq_ref, wkv_ref, sems
):
    n = wq_hbm.shape[0] // x_ref.shape[1]
    width = x_ref.shape[1]
    me = lax.axis_index("head")

    def copies(step):
        rows = rows_of(lax.rem(me + step, n), width)
        return (
            pltpu.make_async_copy(wkv_hbm.at[rows], wkv_ref.at[rows], sems.at[step, 0]),
            pltpu.make_async_copy(wq_hbm.at[rows], wq_ref.at[rows], sems.at[step, 1]),
        )

    for step in range(n):
        for copy in copies(step):
            copy.start()
    normed, ssq = gained(x_ref[...], gain_ref, me)
    ssq_ref[...] = ssq
    for copy in copies(0):
        copy.wait()
    rows = rows_of(me, width)
    acckv_ref[...] = jnp.dot(normed, wkv_ref[rows, :], preferred_element_type=f32)
    accq_ref[...] = jnp.dot(normed, wq_ref[rows, :], preferred_element_type=f32)
    for step in range(1, n):
        for copy in copies(step):
            copy.wait()


def first_block(x, gain, wq, wkv):
    tokens, width = x.shape
    n = wq.shape[0] // width
    return pl.pallas_call(
        first_block_kernel,
        out_shape=(
            VMEM((tokens, wq.shape[1]), f32),
            VMEM((tokens, wkv.shape[1]), f32),
            VMEM((tokens, HD), f32),
            VMEM(wq.shape, bf16),
            VMEM(wkv.shape, bf16),
        ),
        in_specs=[vmem, vmem, in_hbm, in_hbm],
        out_specs=(vmem,) * 5,
        scratch_shapes=[pltpu.SemaphoreType.DMA((n, 2))],
        cost_estimate=cost(2 * tokens * width * (wq.shape[1] + wkv.shape[1]), 2 * (wq.size + wkv.size)),
        compiler_params=params,
        name="load_and_first_block",
    )(x, gain, *(pltpu.with_memory_space_constraint(w, pltpu.HBM) for w in (wq, wkv)))


def blocks_kernel(count, fresh_start, places, *refs):
    xs, rest = refs[:count], refs[count:]
    if fresh_start:
        gain_ref, wq_ref, wkv_ref, accq_out, acckv_out, ssq_out = rest
    else:
        gain_ref, wq_ref, wkv_ref, accq_ref, acckv_ref, ssq_ref, accq_out, acckv_out, ssq_out = rest
    me = lax.axis_index("head")
    for i, x_ref in enumerate(xs):
        width = x_ref.shape[1]
        block = places[i](me)
        normed, ssq = gained(x_ref[...], gain_ref, block)
        rows = rows_of(block, width)
        kv = jnp.dot(normed, wkv_ref[rows, :], preferred_element_type=f32)
        q = jnp.dot(normed, wq_ref[rows, :], preferred_element_type=f32)
        if i == 0 and fresh_start:
            accq_out[...], acckv_out[...], ssq_out[...] = q, kv, ssq
        elif i == 0:
            accq_out[...] = accq_ref[...] + q
            acckv_out[...] = acckv_ref[...] + kv
            ssq_out[...] = ssq_ref[...] + ssq
        else:
            accq_out[...] += q
            acckv_out[...] += kv
            ssq_out[...] += ssq


def more_blocks(xs, places, gain, wq, wkv, state):
    tokens, width = xs[0].shape
    operands = [*xs, *resident_in(gain, wq, wkv), *(state or ())]
    shapes = ((tokens, wq.shape[1]), (tokens, wkv.shape[1]), (tokens, HD))
    return pl.pallas_call(
        functools.partial(blocks_kernel, len(xs), state is None, places),
        out_shape=tuple(VMEM(s, f32) for s in shapes),
        in_specs=[vmem] * len(operands),
        out_specs=(vmem,) * 3,
        cost_estimate=cost(
            len(xs) * 2 * tokens * width * (wq.shape[1] + wkv.shape[1]), len(xs) * 2 * tokens * width
        ),
        compiler_params=params,
        name="more_blocks",
    )(*operands)


def last_kv_kernel(count, places, *refs):
    xs, rest = refs[:count], refs[count:]
    gain_ref, wkv_ref, acckv_ref, ssq_ref = rest[:4]
    scale_ref, pieces, turned = rest[4], rest[5:-1], rest[-1]
    n = lax.axis_size("head")
    me = lax.axis_index("head")
    total, ssq = acckv_ref[...], ssq_ref[...]
    for i, x_ref in enumerate(xs):
        block = places[i](me)
        width = x_ref.shape[1]
        normed, more = gained(x_ref[...], gain_ref, block)
        ssq = ssq + more
        total = total + jnp.dot(normed, wkv_ref[rows_of(block, width), :], preferred_element_type=f32)
    scale = lax.rsqrt(jnp.sum(ssq, axis=1, keepdims=True) / gain_ref.shape[1] + epsilon)
    scale_ref[...] = jnp.broadcast_to(scale, scale_ref.shape)
    kv = (total * scale).astype(bf16)
    columns = kv.shape[1]
    features = columns // (2 * KVH)
    row = lax.broadcasted_iota(jnp.int32, (columns, columns), 0)
    col = lax.broadcasted_iota(jnp.int32, (columns, columns), 1)
    group, which, feature = row // (2 * features), (row // features) % 2, row % features
    choose = jnp.where(col == (feature * KVH + group) * 2 + which, 1.0, 0.0).astype(bf16)
    turned[...] = lax.dot_general(choose, kv, (((1,), (1,)), ((), ())), preferred_element_type=f32)
    size = 2 * features
    for flip in range(n):
        group_there = lax.bitwise_xor(me, jnp.int32(flip)) * KVH // n
        pieces[flip][...] = turned[pl.ds(pl.multiple_of(group_there * size, size), size), :].astype(bf16)


def last_kv(xs, places, gain, wkv, acckv, ssq, n):
    tokens, width = xs[0].shape
    columns = wkv.shape[1]
    operands = [*xs, *resident_in(gain, wkv), acckv, ssq]
    return pl.pallas_call(
        functools.partial(last_kv_kernel, len(xs), places),
        out_shape=(VMEM((tokens, HD), f32),) + tuple(VMEM((columns // KVH, tokens), bf16) for _ in range(n)),
        in_specs=[vmem] * len(operands),
        out_specs=(vmem,) * (1 + n),
        scratch_shapes=[VMEM((columns, tokens), f32)],
        cost_estimate=cost(len(xs) * 2 * tokens * width * columns, 2 * tokens * width),
        compiler_params=params,
        name="last_block_key_value",
    )(*operands)


def last_q_kernel(count, places, *refs):
    xs, rest = refs[:count], refs[count:]
    gain_ref, wq_ref, accq_ref, scale_ref, q_ref = rest
    width = xs[0].shape[1]
    me = lax.axis_index("head")
    total = accq_ref[...]
    for i, x_ref in enumerate(xs):
        block = places[i](me)
        normed, _ = gained(x_ref[...], gain_ref, block)
        total = total + jnp.dot(normed, wq_ref[rows_of(block, width), :], preferred_element_type=f32)
    q_ref[...] = (total * scale_ref[:, 0:1]).astype(bf16)


def last_q(xs, places, gain, wq, accq, scale):
    tokens, width = xs[0].shape
    operands = [*xs, *resident_in(gain, wq), accq, scale]
    return pl.pallas_call(
        functools.partial(last_q_kernel, len(xs), places),
        out_shape=VMEM((tokens, wq.shape[1]), bf16),
        in_specs=[vmem] * len(operands),
        out_specs=vmem,
        cost_estimate=cost(len(xs) * 2 * tokens * width * wq.shape[1], 2 * tokens * width),
        compiler_params=params,
        name="last_block_queries",
    )(*operands)


def openings_kernel(sections, doc_ref, first_ref, second_ref):
    tokens = first_ref.shape[0]
    for turn, out_ref in enumerate((first_ref, second_ref)):
        start = (sections - 1 + turn - lax.axis_index("section")) * tokens
        here = start + lax.broadcasted_iota(jnp.int32, out_ref.shape, 0)
        opened = jnp.zeros(out_ref.shape, jnp.int32)
        end = jnp.int32(0)
        for d in range(doc_ref.shape[0]):
            end = end + doc_ref[d]
            opened = jnp.where(end <= here, end, opened)
        out_ref[...] = opened


def openings(doc_lengths, tokens, sections):
    return pl.pallas_call(
        functools.partial(openings_kernel, sections),
        out_shape=(VMEM((tokens, HD), jnp.int32),) * 2,
        in_specs=[smem],
        out_specs=(vmem,) * 2,
        compiler_params=params,
        name="openings",
    )(doc_lengths)


def attend_kernel(n, sections, turn, heads, x_count, extra_count, gathered, *refs):
    opened_ref, q_ref = refs[:2]
    x_refs, rest = refs[2 : 2 + x_count], refs[2 + x_count :]
    extras, outs = rest[:extra_count], rest[extra_count:]
    if gathered:
        *outs, gather = outs
    out_ref = outs[0]
    tokens = q_ref.shape[0]
    section = lax.axis_index("section")
    base = (sections - 1 - section) * tokens
    start = base + (turn - 1) * tokens
    if gathered:
        features = extras[0].shape[0] // 2
        for flip in range(n):
            source = lax.bitwise_xor(lax.axis_index("head"), jnp.int32(flip))
            piece = extras[flip][...].astype(f32)
            rows = pl.ds(pl.multiple_of(source * features, features), features)
            gather[0, rows, :] = piece[:features]
            gather[1, rows, :] = piece[features:]
        keys, values = gather[0].astype(bf16), gather[1].astype(bf16)
        extras = extras[n:]
        if turn == 1:
            outs[1][...], outs[2][...] = keys, values
    else:
        keys, values, *extras = extras[0][...], extras[1][...], *extras[2:]
    if turn == 2:
        keys = jnp.concatenate([extras[0][...], keys], axis=1)
        values = jnp.concatenate([extras[1][...], values], axis=1)
    else:
        fresh_ref = extras[0]
    here = start + lax.broadcasted_iota(jnp.int32, (tokens, keys.shape[1]), 0)
    there = base + lax.broadcasted_iota(jnp.int32, (tokens, keys.shape[1]), 1)
    allowed = (there >= opened_ref[:, 0:1]) & (there <= here)
    count = heads[1] - heads[0]
    stacked = jnp.concatenate([q_ref[:, h * HD : (h + 1) * HD] for h in range(*heads)], axis=0)
    scores = jnp.dot(stacked, keys, preferred_element_type=f32) * (1.0 / math.sqrt(HD))
    scores = jnp.where(allowed[None], scores.reshape(count, tokens, -1), masked_score)
    expon = jnp.exp(scores - jnp.max(scores, axis=2, keepdims=True))
    weights = (expon * (1.0 / jnp.sum(expon, axis=2, keepdims=True))).astype(bf16)
    mixed = lax.dot_general(
        weights.reshape(count * tokens, -1), values, (((1,), (1,)), ((), ())), preferred_element_type=f32
    ).astype(bf16)
    for i in range(count):
        column = (heads[0] + i) * HD
        x_width = x_refs[0].shape[1]
        x_ref, inside = x_refs[column // x_width], column % x_width
        out = x_ref[:, inside : inside + HD].astype(f32) + mixed[i * tokens : (i + 1) * tokens].astype(f32)
        if turn == 1:
            out = out.astype(bf16).astype(f32)
            out = jnp.where(section == sections - 1, fresh_ref[:, column : column + HD].astype(f32), out)
        out_ref[:, i * HD : (i + 1) * HD] = out.astype(bf16)


def attend(opened, q, xs, extra, turn, heads, gathered, n, sections):
    tokens = q.shape[0]
    out = (jax.ShapeDtypeStruct((tokens, (heads[1] - heads[0]) * HD), bf16),)
    if turn == 1 and gathered:
        out = out + (VMEM((HD, tokens), bf16),) * 2
    operands = [opened, q, *xs, *extra]
    return pl.pallas_call(
        functools.partial(attend_kernel, n, sections, turn, heads, len(xs), len(extra), gathered),
        out_shape=out,
        in_specs=[vmem] * len(operands),
        out_specs=(vmem,) * len(out),
        scratch_shapes=[VMEM((2, HD, tokens), f32)] if gathered else [],
        cost_estimate=cost(8 * tokens * tokens * q.shape[1], 2 * q.size),
        compiler_params=params,
        name="attend",
    )(*operands)


def shards(entering, fresh_slice, norm_gain, w_query, w_key_value, doc_lengths):
    n = lax.axis_size("head")
    sections = lax.axis_size("section")
    own = entering[0]
    w_q, w_kv = w_query[0], w_key_value[0]
    gain = norm_gain
    tokens, width = own.shape
    heads = w_q.shape[1] // HD
    half = heads // 2

    def moved(array, by, flip):
        pairs = [
            (s * n + h, ((s + by) % sections) * n + (h ^ flip)) for s in range(sections) for h in range(n)
        ]
        return lax.ppermute(array, ("section", "head"), pairs)

    def exchanged(xs, places, wkv, state):
        _, acckv, ssq = state
        scale, *pieces = last_kv(xs, places, gain, wkv, acckv, ssq, n)
        crossing = {flip: moved(pieces[flip], 0, flip) for flip in range(n - 1, 0, -1)}
        return scale, [pieces[0]] + [crossing[flip] for flip in range(1, n)]

    def rest_of(array):
        every = lax.all_gather(array, "head", axis=0)
        me = lax.axis_index("head")
        return [lax.dynamic_index_in_dim(every, (me + k) % n, 0, False) for k in range(1, n)]

    paired = n == 4
    others = [functools.partial(lambda k, me: lax.rem(me + k, jnp.int32(n)), k) for k in range(n)]

    def place(flip, parts=1, part=0):
        return lambda me: lax.bitwise_xor(me, jnp.int32(flip)) * parts + part

    if paired:
        over = moved(own, 0, 2)
        beside = moved(own, 0, 1)
    *state, wq, wkv = first_block(own, gain, w_q, w_kv)
    opened = openings(doc_lengths, tokens, sections)
    if paired:
        over, opened, *state = lax.optimization_barrier((over, opened, *state))
        passed = moved(over, 0, 1)
        state = more_blocks([beside, over], [place(1), place(2)], gain, wq, wkv, state)
        last, places = [passed], [place(3)]
    else:
        last, places = rest_of(own), others[1:]
    scale, received = exchanged(last, places, wkv, state)
    q = last_q(last, places, gain, wq, state[0], scale)
    first_heads = (0, half) if paired else (0, heads)
    sent, keys, values = attend(
        opened[0], q, [own], [*received, fresh_slice], 1, first_heads, True, n, sections
    )

    if paired:
        mine_a = moved(sent, 1, 0)
        (sent,) = attend(
            opened[0], q, [own], [keys, values, fresh_slice], 1, (half, heads), False, n, sections
        )
        over_b = moved(sent, 1, 2)
        mine_b = moved(sent, 1, 0)
        mine_a, _ = lax.optimization_barrier((mine_a, sent))
        over_a = moved(mine_a, 0, 2)
        beside_a = moved(mine_a, 0, 1)
        state = more_blocks([mine_a], [place(0, 2, 0)], gain, wq, wkv, None)
        mine_b, over_b, *state = lax.optimization_barrier((mine_b, over_b, *state))
        beside_b = moved(mine_b, 0, 1)
        passed_b = moved(over_b, 0, 1)
        passed_a = moved(over_a, 0, 1)
        early = [beside_a, over_a, mine_b, over_b]
        places = [place(1, 2, 0), place(2, 2, 0), place(0, 2, 1), place(2, 2, 1)]
        state = more_blocks(early, places, gain, wq, wkv, state)
        last, places = [passed_a, beside_b, passed_b], [place(3, 2, 0), place(1, 2, 1), place(3, 2, 1)]
        mine = [mine_a, mine_b]
    else:
        mine = [moved(sent, 1, 0)]
        state = more_blocks(mine, others[:1], gain, wq, wkv, None)
        last, places = rest_of(mine[0]), others[1:]
    scale, received = exchanged(last, places, wkv, state)
    q = last_q(last, places, gain, wq, state[0], scale)
    out = attend(opened[1], q, mine, [*received, keys, values], 2, (0, heads), True, n, sections)
    return out[0][None]


def solution(mesh):
    placed = (
        P("section", None, "head"),
        P(None, "head"),
        P("section", None),
        P("section", None, "head"),
        P("section", None, "head"),
        P(),
    )
    return jax.shard_map(
        shards, mesh=mesh, in_specs=placed, out_specs=P("section", None, "head"), check_vma=False
    )
```

```python
import functools
import math

import jax
import jax.numpy as jnp
from jax import lax
from jax.experimental import pallas as pl
from jax.experimental.pallas import tpu as pltpu
from jax.sharding import PartitionSpec as P

HD = 128
KVH = 4
GROUP = 8

epsilon = 1e-05
masked_score = -1e30

VMEM = pltpu.VMEM
f32 = jnp.float32
bf16 = jnp.bfloat16
vmem = pl.BlockSpec(memory_space=VMEM)
smem = pl.BlockSpec(memory_space=pltpu.SMEM)
in_hbm = pl.BlockSpec(memory_space=pltpu.HBM)
params = pltpu.CompilerParams(vmem_limit_bytes=16 * 1024 * 1024)


def resident_in(*arrays):
    return [pltpu.with_memory_space_constraint(a, VMEM) for a in arrays]


def cost(flops, moved):
    return pl.CostEstimate(flops=flops, bytes_accessed=moved, transcendentals=0)


def rows_of(block, width):
    return pl.ds(pl.multiple_of(block * width, width), width)


def dot(a, b):
    return jnp.dot(a, b, preferred_element_type=f32)


def dot_turned(a, b):
    return lax.dot_general(a, b, (((1,), (1,)), ((), ())), preferred_element_type=f32)


def gained(x, gain_ref, block):
    width = x.shape[1]
    wide = x.astype(f32)
    squares = wide * wide
    ssq = squares[:, :HD]
    for c in range(HD, width, HD):
        ssq = ssq + squares[:, c : c + HD]
    return (wide * gain_ref[:, rows_of(block, width)]).astype(bf16), ssq


def load_kernel(x_hbm, gain_hbm, wq_hbm, wkv_hbm, accq_ref, x_ref, gain_ref, wq_ref, wkv_ref, sems):
    width = x_hbm.shape[1]
    n = wq_hbm.shape[0] // width
    me = lax.axis_index("head")

    def part(step):
        rows = rows_of(lax.rem(me + step, n), width)
        return pltpu.make_async_copy(wq_hbm.at[rows], wq_ref.at[rows], sems.at[step])

    small = (
        pltpu.make_async_copy(x_hbm, x_ref, sems.at[n]),
        pltpu.make_async_copy(gain_hbm, gain_ref, sems.at[n + 1]),
    )
    keys_values = pltpu.make_async_copy(wkv_hbm, wkv_ref, sems.at[n + 2])
    for copy in small:
        copy.start()
    for step in range(n):
        part(step).start()
    keys_values.start()
    for copy in small:
        copy.wait()
    normed, _ = gained(x_ref[...], gain_ref, me)
    part(0).wait()
    accq_ref[...] = dot(normed, wq_ref[rows_of(me, width), :])
    for step in range(1, n):
        part(step).wait()
    keys_values.wait()


def load(x, gain, wq, wkv):
    tokens, width = x.shape
    n = wq.shape[0] // width
    operands = [pltpu.with_memory_space_constraint(a, pltpu.HBM) for a in (x, gain, wq, wkv)]
    return pl.pallas_call(
        load_kernel,
        out_shape=(
            VMEM((tokens, wq.shape[1]), f32),
            VMEM(x.shape, bf16),
            VMEM(gain.shape, f32),
            VMEM(wq.shape, bf16),
            VMEM(wkv.shape, bf16),
        ),
        in_specs=[in_hbm] * 4,
        out_specs=(vmem,) * 5,
        scratch_shapes=[pltpu.SemaphoreType.DMA((n + 3,))],
        cost_estimate=cost(2 * tokens * width * wq.shape[1], 2 * (wq.size + wkv.size)),
        compiler_params=params,
        name="load_and_own_queries",
    )(*operands)


def blocks_kernel(count, wkv_count, carried, places, with_q, *refs):
    xs, refs = refs[:count], refs[count:]
    gain_ref, wq_ref = refs[:2]
    wkv_refs, refs = refs[2 : 2 + wkv_count], refs[2 + wkv_count :]
    old, outs = refs[:carried], refs[carried:]
    me = lax.axis_index("head")
    columns = wkv_refs[0].shape[1]
    q = old[0][...] if carried >= 1 else None
    kvs = [old[1][:, c * columns : (c + 1) * columns] if carried == 3 else None for c in range(wkv_count)]
    ssq = old[2][...] if carried == 3 else None

    def add(total, term):
        return term if total is None else total + term

    for i, x_ref in enumerate(xs):
        block, width = places[i](me), x_ref.shape[1]
        normed, squares = gained(x_ref[...], gain_ref, block)
        ssq = add(ssq, squares)
        rows = rows_of(block, width)
        kvs = [add(kv, dot(normed, w_ref[rows, :])) for kv, w_ref in zip(kvs, wkv_refs)]
        if with_q[i]:
            q = add(q, dot(normed, wq_ref[rows, :]))
    outs[0][...] = q
    for c, kv in enumerate(kvs):
        outs[1][:, c * columns : (c + 1) * columns] = kv
    outs[2][...] = ssq


def more_blocks(xs, places, gain, wq, wkvs, state, with_q=None):
    tokens = xs[0].shape[0]
    operands = [*xs, *resident_in(gain, wq, *wkvs), *state]
    columns = len(wkvs) * wkvs[0].shape[1]
    shapes = ((tokens, wq.shape[1]), (tokens, columns), (tokens, HD))
    return pl.pallas_call(
        functools.partial(
            blocks_kernel, len(xs), len(wkvs), len(state), places, with_q or [True] * len(xs)
        ),
        out_shape=tuple(VMEM(s, f32) for s in shapes),
        in_specs=[vmem] * len(operands),
        out_specs=(vmem,) * 3,
        cost_estimate=cost(sum(2 * x.size * (wq.shape[1] + columns) for x in xs), sum(2 * x.size for x in xs)),
        compiler_params=params,
        name="more_blocks",
    )(*operands)


def last_kv_kernel(count, wkv_count, n, flips, places, *refs):
    xs, refs = refs[:count], refs[count:]
    gain_ref, wkv_refs, refs = refs[0], refs[1 : 1 + wkv_count], refs[1 + wkv_count :]
    acckv_ref, ssq_ref, scale_ref, pieces = refs[0], refs[1], refs[2], refs[3:]
    me = lax.axis_index("head")
    columns = wkv_refs[0].shape[1]
    kvs = [acckv_ref[:, c * columns : (c + 1) * columns] for c in range(wkv_count)]
    ssq = ssq_ref[...]
    for i, x_ref in enumerate(xs):
        block, width = places[i](me), x_ref.shape[1]
        normed, squares = gained(x_ref[...], gain_ref, block)
        ssq = ssq + squares
        kvs = [kv + dot(normed, w_ref[rows_of(block, width), :]) for kv, w_ref in zip(kvs, wkv_refs)]
    scale = lax.rsqrt(jnp.sum(ssq, axis=1, keepdims=True) / gain_ref.shape[1] + epsilon)
    scale_ref[...] = jnp.broadcast_to(scale, scale_ref.shape)
    kv = jnp.concatenate([(kv * scale).astype(bf16) for kv in kvs], axis=1)
    features = columns // (2 * KVH)
    size = 2 * wkv_count * features
    row = lax.broadcasted_iota(jnp.int32, (size, wkv_count * columns), 0)
    col = lax.broadcasted_iota(jnp.int32, (size, wkv_count * columns), 1)
    which, core, feature = row // (wkv_count * features), (row // features) % wkv_count, row % features
    whose = (core != lax.rem(me, wkv_count)).astype(jnp.int32)
    first = col - (whose * columns + feature * (2 * KVH) + which)
    for flip, piece in zip(flips, pieces):
        group = lax.bitwise_xor(me, jnp.int32(flip)) * KVH // n
        choose = jnp.where(first == group * 2, 1.0, 0.0).astype(bf16)
        piece[...] = dot_turned(choose, kv).astype(bf16)


def last_kv(xs, places, gain, wkvs, acckv, ssq, n, flips):
    tokens = xs[0].shape[0]
    columns = len(wkvs) * wkvs[0].shape[1]
    operands = [*xs, *resident_in(gain, *wkvs), acckv, ssq]
    return pl.pallas_call(
        functools.partial(last_kv_kernel, len(xs), len(wkvs), n, flips, places),
        out_shape=(VMEM((tokens, HD), f32),) + (VMEM((columns // KVH, tokens), bf16),) * len(flips),
        in_specs=[vmem] * len(operands),
        out_specs=(vmem,) * (1 + len(flips)),
        cost_estimate=cost(sum(2 * x.size * columns for x in xs), sum(2 * x.size for x in xs)),
        compiler_params=params,
        name="last_keys_values",
    )(*operands)


def last_q_kernel(count, places, *refs):
    xs, rest = refs[:count], refs[count:]
    gain_ref, wq_ref, accq_ref, scale_ref, q_ref = rest
    me = lax.axis_index("head")
    total = accq_ref[...]
    for i, x_ref in enumerate(xs):
        block, width = places[i](me), x_ref.shape[1]
        normed, _ = gained(x_ref[...], gain_ref, block)
        total = total + dot(normed, wq_ref[rows_of(block, width), :])
    q_ref[...] = (total * scale_ref[:, 0:1]).astype(bf16)


def last_q(xs, places, gain, wq, accq, scale):
    operands = [*xs, *resident_in(gain, wq), accq, scale]
    return pl.pallas_call(
        functools.partial(last_q_kernel, len(xs), places),
        out_shape=VMEM((xs[0].shape[0], wq.shape[1]), bf16),
        in_specs=[vmem] * len(operands),
        out_specs=vmem,
        cost_estimate=cost(sum(2 * x.size * wq.shape[1] for x in xs), sum(2 * x.size for x in xs)),
        compiler_params=params,
        name="last_queries",
    )(*operands)


def openings_kernel(sections, doc_ref, first_ref, second_ref):
    tokens = first_ref.shape[0]
    for turn, out_ref in enumerate((first_ref, second_ref)):
        start = (sections - 1 + turn - lax.axis_index("section")) * tokens
        here = start + lax.broadcasted_iota(jnp.int32, out_ref.shape, 0)
        opened = jnp.zeros(out_ref.shape, jnp.int32)
        end = jnp.int32(0)
        for d in range(doc_ref.shape[0]):
            end = end + doc_ref[d]
            opened = jnp.where(end <= here, end, opened)
        out_ref[...] = opened


def openings(doc_lengths, tokens, sections):
    return pl.pallas_call(
        functools.partial(openings_kernel, sections),
        out_shape=(VMEM((tokens, HD), jnp.int32),) * 2,
        in_specs=[smem],
        out_specs=(vmem,) * 2,
        compiler_params=params,
        name="openings",
    )(doc_lengths)


def stacked_heads(q_ref, heads):
    return jnp.concatenate([q_ref[:, h * HD : (h + 1) * HD] for h in range(*heads)], axis=0)


def masked_scores(q, keys, opened_ref, query_start, key_start):
    tokens, count = opened_ref.shape[0], keys.shape[1]
    here = query_start + lax.broadcasted_iota(jnp.int32, (tokens, count), 0)
    there = key_start + lax.broadcasted_iota(jnp.int32, (tokens, count), 1)
    allowed = (there >= opened_ref[:, 0:1]) & (there <= here)
    scores = dot(q, keys) * (1.0 / math.sqrt(HD))
    scores = jnp.where(allowed[None], scores.reshape(-1, tokens, count), masked_score)
    return scores.reshape(-1, count)


def put_together(me, pieces, flips, parts, gather):
    features = pieces[0].shape[0] // 2
    for flip, piece_ref in zip(flips, pieces):
        source = lax.bitwise_xor(me, jnp.int32(flip)) // parts
        piece = piece_ref[...].astype(f32)
        gather[0, rows_of(source, features), :] = piece[:features]
        gather[1, rows_of(source, features), :] = piece[features:]
    return gather[0].astype(bf16), gather[1].astype(bf16)


def first_attend_kernel(sections, heads, flips, parts, opened_ref, q_ref, x_ref, fresh_ref, *refs):
    section = lax.axis_index("section")
    start = (sections - 1 - section) * q_ref.shape[0]
    if flips is None:
        keys_ref, values_ref, out_ref = refs
        keys, values = keys_ref[...], values_ref[...]
    else:
        pieces, (out_ref, keys_ref, values_ref, gather) = refs[: len(flips)], refs[len(flips) :]
        keys, values = put_together(lax.axis_index("head"), pieces, flips, parts, gather)
        keys_ref[...], values_ref[...] = keys, values
    tokens = q_ref.shape[0]
    scores = masked_scores(stacked_heads(q_ref, heads), keys, opened_ref, start, start)
    expon = jnp.exp(scores - jnp.max(scores, axis=1, keepdims=True))
    weights = (expon * (1.0 / jnp.sum(expon, axis=1, keepdims=True))).astype(bf16)
    mixed = dot_turned(weights, values).astype(bf16).astype(f32)
    for i, h in enumerate(range(*heads)):
        columns = slice(h * HD, (h + 1) * HD)
        out = (x_ref[:, columns].astype(f32) + mixed[i * tokens : (i + 1) * tokens]).astype(bf16)
        out = jnp.where(section == sections - 1, fresh_ref[:, columns].astype(f32), out.astype(f32))
        out_ref[:, i * HD : (i + 1) * HD] = out.astype(bf16)


def first_attend(opened, q, x, fresh, pieces, flips, parts, heads, sections):
    tokens = q.shape[0]
    out = (VMEM((tokens, (heads[1] - heads[0]) * HD), bf16),)
    scratch = []
    if flips is not None:
        out = out + (VMEM((HD, tokens), bf16),) * 2
        scratch = [VMEM((2, HD, tokens), f32)]
    operands = [opened, q, x, fresh, *pieces]
    return pl.pallas_call(
        functools.partial(first_attend_kernel, sections, heads, flips, parts),
        out_shape=out,
        in_specs=[vmem] * len(operands),
        out_specs=(vmem,) * len(out),
        scratch_shapes=scratch,
        cost_estimate=cost(1000, 1000),
        compiler_params=params,
        name="first_attend",
    )(*operands)


def resident_kernel(sections, opened_ref, q_ref, keys_ref, values_ref, max_ref, sum_ref, mixed_ref):
    tokens = q_ref.shape[0]
    key_start = (sections - 1 - lax.axis_index("section")) * tokens
    q = stacked_heads(q_ref, (0, q_ref.shape[1] // HD))
    scores = masked_scores(q, keys_ref[...], opened_ref, key_start + tokens, key_start)
    top = jnp.max(scores, axis=1, keepdims=True)
    expon = jnp.exp(scores - top)
    max_ref[...] = jnp.broadcast_to(top, max_ref.shape)
    sum_ref[...] = jnp.broadcast_to(jnp.sum(expon, axis=1, keepdims=True), sum_ref.shape)
    mixed_ref[...] = dot_turned(expon.astype(bf16), values_ref[...])


def resident_attend(opened, q, keys, values, sections):
    rows = q.shape[0] * (q.shape[1] // HD)
    return pl.pallas_call(
        functools.partial(resident_kernel, sections),
        out_shape=(VMEM((rows, HD), f32),) * 3,
        in_specs=[vmem] * 4,
        out_specs=(vmem,) * 3,
        cost_estimate=cost(1000, 1000),
        compiler_params=params,
        name="resident_attend",
    )(opened, q, keys, values)


def second_attend_kernel(sections, flips, parts, x_count, opened_ref, q_ref, max_ref, sum_ref, mixed_ref, *refs):
    x_refs, refs = refs[:x_count], refs[x_count:]
    pieces, (out_ref, gather) = refs[: len(flips)], refs[len(flips) :]
    tokens, heads = q_ref.shape[0], q_ref.shape[1] // HD
    start = (sections - lax.axis_index("section")) * tokens
    keys, values = put_together(lax.axis_index("head"), pieces, flips, parts, gather)
    scores = masked_scores(stacked_heads(q_ref, (0, heads)), keys, opened_ref, start, start)
    top = jnp.maximum(jnp.max(scores, axis=1, keepdims=True), max_ref[...])
    expon = jnp.exp(scores - top)
    shrink = jnp.exp(max_ref[...] - top)
    total = jnp.sum(expon, axis=1, keepdims=True) + shrink * sum_ref[...]
    mixed = dot_turned(expon.astype(bf16), values) + shrink * mixed_ref[...]
    mixed = (mixed * (1.0 / total)).astype(bf16).astype(f32)
    x_width = x_refs[0].shape[1]
    for h in range(heads):
        x_ref, inside = x_refs[h * HD // x_width], h * HD % x_width
        out = x_ref[:, inside : inside + HD].astype(f32) + mixed[h * tokens : (h + 1) * tokens]
        out_ref[:, h * HD : (h + 1) * HD] = out.astype(bf16)


def second_attend(opened, q, xs, resident, pieces, flips, parts, sections):
    tokens = q.shape[0]
    operands = [opened, q, *resident, *xs, *pieces]
    return pl.pallas_call(
        functools.partial(second_attend_kernel, sections, flips, parts, len(xs)),
        out_shape=jax.ShapeDtypeStruct(q.shape, bf16),
        in_specs=[vmem] * len(operands),
        out_specs=vmem,
        scratch_shapes=[VMEM((2, HD, tokens), f32)],
        cost_estimate=cost(1000, 1000),
        compiler_params=params,
        name="second_attend",
    )(*operands)


def shards(entering, fresh_slice, norm_gain, w_query, w_key_value, doc_lengths):
    n = lax.axis_size("head")
    sections = lax.axis_size("section")
    own = entering[0]
    w_q, w_kv = w_query[0], w_key_value[0]
    tokens = own.shape[0]
    heads = w_q.shape[1] // HD
    paired = n == 4
    parts = 2 if paired else 1
    flips = [0, 2] if paired else list(range(n))

    def moved(array, by, flip):
        pairs = [
            (s * n + h, ((s + by) % sections) * n + (h ^ flip)) for s in range(sections) for h in range(n)
        ]
        return lax.ppermute(array, ("section", "head"), pairs)

    def after(array, *others):
        return lax.optimization_barrier((array, *others))[0]

    def exchanged(xs, places, state):
        scale, *pieces = last_kv(xs, places, gain, wkvs, state[1], state[2], n, flips)
        received = [moved(piece, 0, flip) for piece, flip in zip(pieces[1:], flips[1:])]
        return scale, [pieces[0], *received]

    def rest_of(array):
        every = lax.all_gather(array, "head", axis=0)
        me = lax.axis_index("head")
        return [lax.dynamic_index_in_dim(every, (me + k) % n, 0, False) for k in range(1, n)]

    def place(flip, count=1, part=0):
        return lambda me: lax.bitwise_xor(me, jnp.int32(flip)) * count + part

    following = [functools.partial(lambda k, me: lax.rem(me + k, jnp.int32(n)), k) for k in range(n)]

    if paired:
        over = moved(own, 0, 2)
        beside = moved(own, 0, 1)
        w_kv_beside = moved(w_kv, 0, 1)
    accq, own, gain, wq, wkv = load(own, norm_gain, w_q, w_kv)
    if paired:
        wkvs = [wkv, w_kv_beside]
        over = after(over, accq)
        passed = moved(over, 0, 1)
        xs, places, with_q = [own, beside, over], [place(0), place(1), place(2)], [False, True, True]
        state = more_blocks(xs, places, gain, wq, wkvs, [accq], with_q)
        last, places = [passed], [place(3)]
    else:
        wkvs = [wkv]
        state = more_blocks([own], following[:1], gain, wq, wkvs, [accq], [False])
        last, places = rest_of(own), following[1:]
    scale, pieces = exchanged(last, places, state)
    opened = openings(after(doc_lengths, scale), tokens, sections)
    q = last_q(last, places, gain, wq, state[0], scale)
    half = heads // 2 if paired else heads
    sent, keys, values = first_attend(
        opened[0], q, own, fresh_slice, pieces, flips, parts, (0, half), sections
    )

    if paired:
        mine_a = moved(sent, 1, 0)
        (sent,) = first_attend(
            opened[0], q, own, fresh_slice, [keys, values], None, parts, (half, heads), sections
        )
        over_b = moved(sent, 1, 2)
        mine_b = moved(sent, 1, 0)
        mine_a = after(mine_a, sent)
        over_a = moved(mine_a, 0, 2)
        beside_a = moved(mine_a, 0, 1)
        state = more_blocks([mine_a], [place(0, 2, 0)], gain, wq, wkvs, [])
        mine_b, over_b, *state = lax.optimization_barrier((mine_b, over_b, *state))
        beside_b = moved(mine_b, 0, 1)
        passed_b = moved(over_b, 0, 1)
        passed_a = moved(over_a, 0, 1)
        early = [beside_a, over_a, mine_b, over_b]
        places = [place(1, 2, 0), place(2, 2, 0), place(0, 2, 1), place(2, 2, 1)]
        state = more_blocks(early, places, gain, wq, wkvs, state)
        last, places = [passed_a, beside_b, passed_b], [place(3, 2, 0), place(1, 2, 1), place(3, 2, 1)]
        mine = [mine_a, mine_b]
    else:
        mine = [moved(sent, 1, 0)]
        state = more_blocks(mine, following[:1], gain, wq, wkvs, [])
        last, places = rest_of(mine[0]), following[1:]
    scale, pieces = exchanged(last, places, state)
    q = last_q(last, places, gain, wq, state[0], scale)
    resident = resident_attend(opened[1], q, keys, values, sections)
    return second_attend(opened[1], q, mine, resident, pieces, flips, parts, sections)[None]


def solution(mesh):
    placed = (
        P("section", None, "head"),
        P(None, "head"),
        P("section", None),
        P("section", None, "head"),
        P("section", None, "head"),
        P(),
    )
    return jax.shard_map(
        shards, mesh=mesh, in_specs=placed, out_specs=P("section", None, "head"), check_vma=False
    )
```

```python
import functools
import math

import jax
import jax.numpy as jnp
from jax import lax
from jax.experimental import pallas as pl
from jax.experimental.pallas import tpu as pltpu
from jax.sharding import PartitionSpec as P

HD = 128
KVH = 4
GROUP = 8

epsilon = 1e-05
masked_score = -1e30

VMEM = pltpu.VMEM
f32 = jnp.float32
bf16 = jnp.bfloat16
vmem = pl.BlockSpec(memory_space=VMEM)
smem = pl.BlockSpec(memory_space=pltpu.SMEM)
in_hbm = pl.BlockSpec(memory_space=pltpu.HBM)
params = pltpu.CompilerParams(vmem_limit_bytes=16 * 1024 * 1024)


def resident_in(*arrays):
    return [pltpu.with_memory_space_constraint(a, VMEM) for a in arrays]


def cost(flops, moved):
    return pl.CostEstimate(flops=flops, bytes_accessed=moved, transcendentals=0)


def rows_of(block, width):
    return pl.ds(pl.multiple_of(block * width, width), width)


def dot(a, b):
    return jnp.dot(a, b, preferred_element_type=f32)


def dot_turned(a, b):
    return lax.dot_general(a, b, (((1,), (1,)), ((), ())), preferred_element_type=f32)


def gained(x, gain_ref, block):
    width = x.shape[1]
    wide = x.astype(f32)
    squares = wide * wide
    ssq = squares[:, :HD]
    for c in range(HD, width, HD):
        ssq = ssq + squares[:, c : c + HD]
    return (wide * gain_ref[:, rows_of(block, width)]).astype(bf16), ssq


def load_kernel(x_hbm, gain_hbm, wq_hbm, wkv_hbm, accq_ref, x_ref, gain_ref, wq_ref, wkv_ref, sems):
    width = x_hbm.shape[1]
    n = wq_hbm.shape[0] // width
    me = lax.axis_index("head")

    def part(step):
        rows = rows_of(lax.rem(me + step, n), width)
        return pltpu.make_async_copy(wq_hbm.at[rows], wq_ref.at[rows], sems.at[step])

    small = (
        pltpu.make_async_copy(x_hbm, x_ref, sems.at[n]),
        pltpu.make_async_copy(gain_hbm, gain_ref, sems.at[n + 1]),
    )
    keys_values = pltpu.make_async_copy(wkv_hbm, wkv_ref, sems.at[n + 2])
    for copy in small:
        copy.start()
    for step in range(n):
        part(step).start()
    keys_values.start()
    for copy in small:
        copy.wait()
    normed, _ = gained(x_ref[...], gain_ref, me)
    part(0).wait()
    accq_ref[...] = dot(normed, wq_ref[rows_of(me, width), :])
    for step in range(1, n):
        part(step).wait()
    keys_values.wait()


def load(x, gain, wq, wkv):
    tokens, width = x.shape
    n = wq.shape[0] // width
    operands = [pltpu.with_memory_space_constraint(a, pltpu.HBM) for a in (x, gain, wq, wkv)]
    return pl.pallas_call(
        load_kernel,
        out_shape=(
            VMEM((tokens, wq.shape[1]), f32),
            VMEM(x.shape, bf16),
            VMEM(gain.shape, f32),
            VMEM(wq.shape, bf16),
            VMEM(wkv.shape, bf16),
        ),
        in_specs=[in_hbm] * 4,
        out_specs=(vmem,) * 5,
        scratch_shapes=[pltpu.SemaphoreType.DMA((n + 3,))],
        cost_estimate=cost(2 * tokens * width * wq.shape[1], 2 * (wq.size + wkv.size)),
        compiler_params=params,
        name="load_and_own_queries",
    )(*operands)


def blocks_kernel(count, wkv_count, carried, places, with_q, *refs):
    xs, refs = refs[:count], refs[count:]
    gain_ref, wq_ref = refs[:2]
    wkv_refs, refs = refs[2 : 2 + wkv_count], refs[2 + wkv_count :]
    old, outs = refs[:carried], refs[carried:]
    me = lax.axis_index("head")
    columns = wkv_refs[0].shape[1]
    q = old[0][...] if carried >= 1 else None
    kvs = [old[1][:, c * columns : (c + 1) * columns] if carried == 3 else None for c in range(wkv_count)]
    ssq = old[2][...] if carried == 3 else None

    def add(total, term):
        return term if total is None else total + term

    for i, x_ref in enumerate(xs):
        block, width = places[i](me), x_ref.shape[1]
        normed, squares = gained(x_ref[...], gain_ref, block)
        ssq = add(ssq, squares)
        rows = rows_of(block, width)
        kvs = [add(kv, dot(normed, w_ref[rows, :])) for kv, w_ref in zip(kvs, wkv_refs)]
        if with_q[i]:
            q = add(q, dot(normed, wq_ref[rows, :]))
    outs[0][...] = q
    for c, kv in enumerate(kvs):
        outs[1][:, c * columns : (c + 1) * columns] = kv
    outs[2][...] = ssq


def more_blocks(xs, places, gain, wq, wkvs, state, with_q=None):
    tokens = xs[0].shape[0]
    operands = [*xs, *resident_in(gain, wq, *wkvs), *state]
    columns = len(wkvs) * wkvs[0].shape[1]
    shapes = ((tokens, wq.shape[1]), (tokens, columns), (tokens, HD))
    return pl.pallas_call(
        functools.partial(
            blocks_kernel, len(xs), len(wkvs), len(state), places, with_q or [True] * len(xs)
        ),
        out_shape=tuple(VMEM(s, f32) for s in shapes),
        in_specs=[vmem] * len(operands),
        out_specs=(vmem,) * 3,
        cost_estimate=cost(sum(2 * x.size * (wq.shape[1] + columns) for x in xs), sum(2 * x.size for x in xs)),
        compiler_params=params,
        name="more_blocks",
    )(*operands)


def last_kv_kernel(count, wkv_count, n, flips, places, *refs):
    xs, refs = refs[:count], refs[count:]
    gain_ref, wkv_refs, refs = refs[0], refs[1 : 1 + wkv_count], refs[1 + wkv_count :]
    acckv_ref, ssq_ref, scale_ref, pieces = refs[0], refs[1], refs[2], refs[3:]
    me = lax.axis_index("head")
    columns = wkv_refs[0].shape[1]
    kvs = [acckv_ref[:, c * columns : (c + 1) * columns] for c in range(wkv_count)]
    ssq = ssq_ref[...]
    for i, x_ref in enumerate(xs):
        block, width = places[i](me), x_ref.shape[1]
        normed, squares = gained(x_ref[...], gain_ref, block)
        ssq = ssq + squares
        kvs = [kv + dot(normed, w_ref[rows_of(block, width), :]) for kv, w_ref in zip(kvs, wkv_refs)]
    scale = lax.rsqrt(jnp.sum(ssq, axis=1, keepdims=True) / gain_ref.shape[1] + epsilon)
    scale_ref[...] = jnp.broadcast_to(scale, scale_ref.shape)
    kv = jnp.concatenate([(kv * scale).astype(bf16) for kv in kvs], axis=1)
    features = columns // (2 * KVH)
    size = 2 * wkv_count * features
    row = lax.broadcasted_iota(jnp.int32, (size, wkv_count * columns), 0)
    col = lax.broadcasted_iota(jnp.int32, (size, wkv_count * columns), 1)
    which, core, feature = row // (wkv_count * features), (row // features) % wkv_count, row % features
    whose = (core != lax.rem(me, wkv_count)).astype(jnp.int32)
    first = col - (whose * columns + feature * (2 * KVH) + which)
    for flip, piece in zip(flips, pieces):
        group = lax.bitwise_xor(me, jnp.int32(flip)) * KVH // n
        choose = jnp.where(first == group * 2, 1.0, 0.0).astype(bf16)
        piece[...] = dot_turned(choose, kv).astype(bf16)


def last_kv(xs, places, gain, wkvs, acckv, ssq, n, flips):
    tokens = xs[0].shape[0]
    columns = len(wkvs) * wkvs[0].shape[1]
    operands = [*xs, *resident_in(gain, *wkvs), acckv, ssq]
    return pl.pallas_call(
        functools.partial(last_kv_kernel, len(xs), len(wkvs), n, flips, places),
        out_shape=(VMEM((tokens, HD), f32),) + (VMEM((columns // KVH, tokens), bf16),) * len(flips),
        in_specs=[vmem] * len(operands),
        out_specs=(vmem,) * (1 + len(flips)),
        cost_estimate=cost(sum(2 * x.size * columns for x in xs), sum(2 * x.size for x in xs)),
        compiler_params=params,
        name="last_keys_values",
    )(*operands)


def last_q_kernel(count, places, *refs):
    xs, rest = refs[:count], refs[count:]
    gain_ref, wq_ref, accq_ref, scale_ref, q_ref = rest
    me = lax.axis_index("head")
    total = accq_ref[...]
    for i, x_ref in enumerate(xs):
        block, width = places[i](me), x_ref.shape[1]
        normed, _ = gained(x_ref[...], gain_ref, block)
        total = total + dot(normed, wq_ref[rows_of(block, width), :])
    q_ref[...] = (total * scale_ref[:, 0:1]).astype(bf16)


def last_q(xs, places, gain, wq, accq, scale):
    operands = [*xs, *resident_in(gain, wq), accq, scale]
    return pl.pallas_call(
        functools.partial(last_q_kernel, len(xs), places),
        out_shape=VMEM((xs[0].shape[0], wq.shape[1]), bf16),
        in_specs=[vmem] * len(operands),
        out_specs=vmem,
        cost_estimate=cost(sum(2 * x.size * wq.shape[1] for x in xs), sum(2 * x.size for x in xs)),
        compiler_params=params,
        name="last_queries",
    )(*operands)


def openings_kernel(sections, doc_ref, first_ref, second_ref):
    tokens = first_ref.shape[0]
    for turn, out_ref in enumerate((first_ref, second_ref)):
        start = (sections - 1 + turn - lax.axis_index("section")) * tokens
        here = start + lax.broadcasted_iota(jnp.int32, out_ref.shape, 0)
        opened = jnp.zeros(out_ref.shape, jnp.int32)
        end = jnp.int32(0)
        for d in range(doc_ref.shape[0]):
            end = end + doc_ref[d]
            opened = jnp.where(end <= here, end, opened)
        out_ref[...] = opened


def openings(doc_lengths, tokens, sections):
    return pl.pallas_call(
        functools.partial(openings_kernel, sections),
        out_shape=(VMEM((tokens, HD), jnp.int32),) * 2,
        in_specs=[smem],
        out_specs=(vmem,) * 2,
        compiler_params=params,
        name="openings",
    )(doc_lengths)


def stacked_heads(q_ref, heads):
    return jnp.concatenate([q_ref[:, h * HD : (h + 1) * HD] for h in range(*heads)], axis=0)


def masked_scores(q, keys, opened_ref, query_start, key_start):
    tokens, count = opened_ref.shape[0], keys.shape[1]
    here = query_start + lax.broadcasted_iota(jnp.int32, (tokens, count), 0)
    there = key_start + lax.broadcasted_iota(jnp.int32, (tokens, count), 1)
    allowed = (there >= opened_ref[:, 0:1]) & (there <= here)
    scores = dot(q, keys) * (1.0 / math.sqrt(HD))
    scores = jnp.where(allowed[None], scores.reshape(-1, tokens, count), masked_score)
    return scores.reshape(-1, count)


def put_together(me, pieces, flips, parts, gather):
    features = pieces[0].shape[0] // 2
    for flip, piece_ref in zip(flips, pieces):
        source = lax.bitwise_xor(me, jnp.int32(flip)) // parts
        piece = piece_ref[...].astype(f32)
        gather[0, rows_of(source, features), :] = piece[:features]
        gather[1, rows_of(source, features), :] = piece[features:]
    return gather[0].astype(bf16), gather[1].astype(bf16)


def first_attend_kernel(sections, heads, flips, parts, opened_ref, q_ref, x_ref, fresh_ref, *refs):
    section = lax.axis_index("section")
    start = (sections - 1 - section) * q_ref.shape[0]
    if flips is None:
        keys_ref, values_ref, out_ref = refs
        keys, values = keys_ref[...], values_ref[...]
    else:
        pieces, (out_ref, keys_ref, values_ref, gather) = refs[: len(flips)], refs[len(flips) :]
        keys, values = put_together(lax.axis_index("head"), pieces, flips, parts, gather)
        keys_ref[...], values_ref[...] = keys, values
    tokens = q_ref.shape[0]
    scores = masked_scores(stacked_heads(q_ref, heads), keys, opened_ref, start, start)
    expon = jnp.exp(scores - jnp.max(scores, axis=1, keepdims=True))
    weights = (expon * (1.0 / jnp.sum(expon, axis=1, keepdims=True))).astype(bf16)
    mixed = dot_turned(weights, values).astype(bf16).astype(f32)
    for i, h in enumerate(range(*heads)):
        columns = slice(h * HD, (h + 1) * HD)
        out = (x_ref[:, columns].astype(f32) + mixed[i * tokens : (i + 1) * tokens]).astype(bf16)
        out = jnp.where(section == sections - 1, fresh_ref[:, columns].astype(f32), out.astype(f32))
        out_ref[:, i * HD : (i + 1) * HD] = out.astype(bf16)


def first_attend(opened, q, x, fresh, pieces, flips, parts, heads, sections):
    tokens = q.shape[0]
    out = (VMEM((tokens, (heads[1] - heads[0]) * HD), bf16),)
    scratch = []
    if flips is not None:
        out = out + (VMEM((HD, tokens), bf16),) * 2
        scratch = [VMEM((2, HD, tokens), f32)]
    operands = [opened, q, x, fresh, *pieces]
    return pl.pallas_call(
        functools.partial(first_attend_kernel, sections, heads, flips, parts),
        out_shape=out,
        in_specs=[vmem] * len(operands),
        out_specs=(vmem,) * len(out),
        scratch_shapes=scratch,
        cost_estimate=cost(1000, 1000),
        compiler_params=params,
        name="first_attend",
    )(*operands)


def resident_kernel(sections, opened_ref, q_ref, keys_ref, values_ref, max_ref, sum_ref, mixed_ref):
    tokens = q_ref.shape[0]
    key_start = (sections - 1 - lax.axis_index("section")) * tokens
    q = stacked_heads(q_ref, (0, q_ref.shape[1] // HD))
    scores = masked_scores(q, keys_ref[...], opened_ref, key_start + tokens, key_start)
    top = jnp.max(scores, axis=1, keepdims=True)
    expon = jnp.exp(scores - top)
    max_ref[...] = jnp.broadcast_to(top, max_ref.shape)
    sum_ref[...] = jnp.broadcast_to(jnp.sum(expon, axis=1, keepdims=True), sum_ref.shape)
    mixed_ref[...] = dot_turned(expon.astype(bf16), values_ref[...])


def resident_attend(opened, q, keys, values, sections):
    rows = q.shape[0] * (q.shape[1] // HD)
    return pl.pallas_call(
        functools.partial(resident_kernel, sections),
        out_shape=(VMEM((rows, HD), f32),) * 3,
        in_specs=[vmem] * 4,
        out_specs=(vmem,) * 3,
        cost_estimate=cost(1000, 1000),
        compiler_params=params,
        name="resident_attend",
    )(opened, q, keys, values)


def second_attend_kernel(sections, flips, parts, x_count, opened_ref, q_ref, max_ref, sum_ref, mixed_ref, *refs):
    x_refs, refs = refs[:x_count], refs[x_count:]
    pieces, (out_ref, gather) = refs[: len(flips)], refs[len(flips) :]
    tokens, heads = q_ref.shape[0], q_ref.shape[1] // HD
    start = (sections - lax.axis_index("section")) * tokens
    keys, values = put_together(lax.axis_index("head"), pieces, flips, parts, gather)
    scores = masked_scores(stacked_heads(q_ref, (0, heads)), keys, opened_ref, start, start)
    top = jnp.maximum(jnp.max(scores, axis=1, keepdims=True), max_ref[...])
    expon = jnp.exp(scores - top)
    shrink = jnp.exp(max_ref[...] - top)
    total = jnp.sum(expon, axis=1, keepdims=True) + shrink * sum_ref[...]
    mixed = dot_turned(expon.astype(bf16), values) + shrink * mixed_ref[...]
    mixed = (mixed * (1.0 / total)).astype(bf16).astype(f32)
    x_width = x_refs[0].shape[1]
    for h in range(heads):
        x_ref, inside = x_refs[h * HD // x_width], h * HD % x_width
        out = x_ref[:, inside : inside + HD].astype(f32) + mixed[h * tokens : (h + 1) * tokens]
        out_ref[:, h * HD : (h + 1) * HD] = out.astype(bf16)


def second_attend(opened, q, xs, resident, pieces, flips, parts, sections):
    tokens = q.shape[0]
    operands = [opened, q, *resident, *xs, *pieces]
    return pl.pallas_call(
        functools.partial(second_attend_kernel, sections, flips, parts, len(xs)),
        out_shape=jax.ShapeDtypeStruct(q.shape, bf16),
        in_specs=[vmem] * len(operands),
        out_specs=vmem,
        scratch_shapes=[VMEM((2, HD, tokens), f32)],
        cost_estimate=cost(1000, 1000),
        compiler_params=params,
        name="second_attend",
    )(*operands)


def shards(entering, fresh_slice, norm_gain, w_query, w_key_value, doc_lengths):
    n = lax.axis_size("head")
    sections = lax.axis_size("section")
    own = entering[0]
    w_q, w_kv = w_query[0], w_key_value[0]
    tokens = own.shape[0]
    heads = w_q.shape[1] // HD
    paired = n == 4
    parts = 2 if paired else 1
    flips = [0, 3] if paired else list(range(n))

    def moved(array, by, flip):
        pairs = [
            (s * n + h, ((s + by) % sections) * n + (h ^ flip)) for s in range(sections) for h in range(n)
        ]
        return lax.ppermute(array, ("section", "head"), pairs)

    def after(array, *others):
        return lax.optimization_barrier((array, *others))[0]

    def exchanged(xs, places, state):
        scale, *pieces = last_kv(xs, places, gain, wkvs, state[1], state[2], n, flips)
        received = [moved(piece, 0, flip) for piece, flip in zip(pieces[1:], flips[1:])]
        return scale, [pieces[0], *received]

    def rest_of(array):
        every = lax.all_gather(array, "head", axis=0)
        me = lax.axis_index("head")
        return [lax.dynamic_index_in_dim(every, (me + k) % n, 0, False) for k in range(1, n)]

    def place(flip, count=1, part=0):
        return lambda me: lax.bitwise_xor(me, jnp.int32(flip)) * count + part

    following = [functools.partial(lambda k, me: lax.rem(me + k, jnp.int32(n)), k) for k in range(n)]

    if paired:
        over = moved(own, 0, 3)
        beside = moved(own, 0, 1)
        w_kv_beside = moved(w_kv, 0, 1)
    accq, own, gain, wq, wkv = load(own, norm_gain, w_q, w_kv)
    if paired:
        wkvs = [wkv, w_kv_beside]
        over = after(over, accq)
        passed = moved(over, 0, 1)
        xs, places, with_q = [own, beside, over], [place(0), place(1), place(3)], [False, True, True]
        state = more_blocks(xs, places, gain, wq, wkvs, [accq], with_q)
        last, places = [passed], [place(2)]
    else:
        wkvs = [wkv]
        state = more_blocks([own], following[:1], gain, wq, wkvs, [accq], [False])
        last, places = rest_of(own), following[1:]
    scale, pieces = exchanged(last, places, state)
    opened = openings(after(doc_lengths, scale), tokens, sections)
    q = last_q(last, places, gain, wq, state[0], scale)
    half = heads // 2 if paired else heads
    sent, keys, values = first_attend(
        opened[0], q, own, fresh_slice, pieces, flips, parts, (0, half), sections
    )

    if paired:
        a1 = moved(sent, 1, 1)
        (sent,) = first_attend(
            opened[0], q, own, fresh_slice, [keys, values], None, parts, (half, heads), sections
        )
        b3 = moved(sent, 1, 3)
        b1 = moved(sent, 1, 1)
        a1 = after(a1, sent)
        a2 = moved(a1, 0, 3)
        a0 = moved(a1, 0, 1)
        state = more_blocks([a1], [place(1, 2, 0)], gain, wq, wkvs, [])
        b1, b3, *state = lax.optimization_barrier((b1, b3, *state))
        b0 = moved(b1, 0, 1)
        b2 = moved(b3, 0, 1)
        a3 = moved(a2, 0, 1)
        places = [place(0, 2, 0), place(2, 2, 0), place(1, 2, 1), place(3, 2, 1)]
        state = more_blocks([a0, a2, b1, b3], places, gain, wq, wkvs, state)
        last, places = [a3, b0, b2], [place(3, 2, 0), place(0, 2, 1), place(2, 2, 1)]
        mine = [a0, b0]
    else:
        mine = [moved(sent, 1, 0)]
        state = more_blocks(mine, following[:1], gain, wq, wkvs, [])
        last, places = rest_of(mine[0]), following[1:]
    scale, pieces = exchanged(last, places, state)
    q = last_q(last, places, gain, wq, state[0], scale)
    resident = resident_attend(opened[1], q, keys, values, sections)
    return second_attend(opened[1], q, mine, resident, pieces, flips, parts, sections)[None]


def solution(mesh):
    placed = (
        P("section", None, "head"),
        P(None, "head"),
        P("section", None),
        P("section", None, "head"),
        P("section", None, "head"),
        P(),
    )
    return jax.shard_map(
        shards, mesh=mesh, in_specs=placed, out_specs=P("section", None, "head"), check_vma=False
    )
```

```python
import functools
import math

import jax
import jax.numpy as jnp
from jax import lax
from jax.experimental import pallas as pl
from jax.experimental.pallas import tpu as pltpu
from jax.sharding import PartitionSpec as P

HD = 128
KVH = 4
GROUP = 8

epsilon = 1e-05
masked_score = -1e30

VMEM = pltpu.VMEM
f32 = jnp.float32
bf16 = jnp.bfloat16
vmem = pl.BlockSpec(memory_space=VMEM)
smem = pl.BlockSpec(memory_space=pltpu.SMEM)
in_hbm = pl.BlockSpec(memory_space=pltpu.HBM)
params = pltpu.CompilerParams(vmem_limit_bytes=16 * 1024 * 1024)


def resident_in(*arrays):
    return [pltpu.with_memory_space_constraint(a, VMEM) for a in arrays]


def cost(flops, moved):
    return pl.CostEstimate(flops=flops, bytes_accessed=moved, transcendentals=0)


def rows_of(block, width):
    return pl.ds(pl.multiple_of(block * width, width), width)


def dot(a, b):
    return jnp.dot(a, b, preferred_element_type=f32)


def dot_turned(a, b):
    return lax.dot_general(a, b, (((1,), (1,)), ((), ())), preferred_element_type=f32)


def gained(x, gain_ref, block):
    width = x.shape[1]
    wide = x.astype(f32)
    squares = wide * wide
    ssq = squares[:, :HD]
    for c in range(HD, width, HD):
        ssq = ssq + squares[:, c : c + HD]
    return (wide * gain_ref[:, rows_of(block, width)]).astype(bf16), ssq


def choose_rows(choose_ref, me, n, flips, parts):
    size, columns = choose_ref.shape[1], choose_ref.shape[2] // parts
    features = size // (2 * parts)
    shape = (features, choose_ref.shape[2])
    row = lax.broadcasted_iota(jnp.int32, shape, 0)
    col = lax.broadcasted_iota(jnp.int32, shape, 1)
    offset = col - row * (2 * KVH)
    for i, flip in enumerate(flips):
        group = lax.bitwise_xor(me, jnp.int32(flip)) * KVH // n
        for which in range(2):
            for core in range(parts):
                whose = jnp.where(lax.rem(me, jnp.int32(parts)) == core, 0, 1)
                wanted = whose * columns + group * 2 + which
                first = (which * parts + core) * features
                choose_ref[i, first : first + features, :] = jnp.where(offset == wanted, 1.0, 0.0)


def load_kernel(
    n, flips, parts, x_hbm, gain_hbm, wq_hbm, wkv_hbm, accq_ref, x_ref, gain_ref, wq_ref, wkv_ref, choose_ref, sems
):
    width = x_hbm.shape[1]
    me = lax.axis_index("head")

    def part(step):
        rows = rows_of(lax.rem(me + step, n), width)
        return pltpu.make_async_copy(wq_hbm.at[rows], wq_ref.at[rows], sems.at[step])

    small = (
        pltpu.make_async_copy(x_hbm, x_ref, sems.at[n]),
        pltpu.make_async_copy(gain_hbm, gain_ref, sems.at[n + 1]),
    )
    keys_values = pltpu.make_async_copy(wkv_hbm, wkv_ref, sems.at[n + 2])
    for copy in small:
        copy.start()
    for step in range(n):
        part(step).start()
    keys_values.start()
    choose_rows(choose_ref, me, n, flips, parts)
    for copy in small:
        copy.wait()
    normed, _ = gained(x_ref[...], gain_ref, me)
    part(0).wait()
    accq_ref[...] = dot(normed, wq_ref[rows_of(me, width), :])
    for step in range(1, n):
        part(step).wait()
    keys_values.wait()


def load(x, gain, wq, wkv, n, flips, parts):
    tokens, width = x.shape
    columns = wkv.shape[1]
    operands = [pltpu.with_memory_space_constraint(a, pltpu.HBM) for a in (x, gain, wq, wkv)]
    return pl.pallas_call(
        functools.partial(load_kernel, n, flips, parts),
        out_shape=(
            VMEM((tokens, wq.shape[1]), f32),
            VMEM(x.shape, bf16),
            VMEM(gain.shape, f32),
            VMEM(wq.shape, bf16),
            VMEM(wkv.shape, bf16),
            VMEM((len(flips), parts * columns // KVH, parts * columns), f32),
        ),
        in_specs=[in_hbm] * 4,
        out_specs=(vmem,) * 6,
        scratch_shapes=[pltpu.SemaphoreType.DMA((n + 3,))],
        cost_estimate=cost(10**11, 10**9),
        compiler_params=params,
        name="load_and_own_queries",
    )(*operands)


def blocks_kernel(count, wkv_count, carried, places, with_q, *refs):
    xs, refs = refs[:count], refs[count:]
    gain_ref, wq_ref = refs[:2]
    wkv_refs, refs = refs[2 : 2 + wkv_count], refs[2 + wkv_count :]
    old, outs = refs[:carried], refs[carried:]
    me = lax.axis_index("head")
    columns = wkv_refs[0].shape[1]
    q = old[0][...] if carried >= 1 else None
    kvs = [old[1][:, c * columns : (c + 1) * columns] if carried == 3 else None for c in range(wkv_count)]
    ssq = old[2][...] if carried == 3 else None

    def add(total, term):
        return term if total is None else total + term

    for i, x_ref in enumerate(xs):
        block, width = places[i](me), x_ref.shape[1]
        normed, squares = gained(x_ref[...], gain_ref, block)
        ssq = add(ssq, squares)
        rows = rows_of(block, width)
        kvs = [add(kv, dot(normed, w_ref[rows, :])) for kv, w_ref in zip(kvs, wkv_refs)]
        if with_q[i]:
            q = add(q, dot(normed, wq_ref[rows, :]))
    outs[0][...] = q
    for c, kv in enumerate(kvs):
        outs[1][:, c * columns : (c + 1) * columns] = kv
    outs[2][...] = ssq


def more_blocks(xs, places, gain, wq, wkvs, state, with_q=None):
    tokens = xs[0].shape[0]
    operands = [*xs, *resident_in(gain, wq, *wkvs), *state]
    columns = len(wkvs) * wkvs[0].shape[1]
    shapes = ((tokens, wq.shape[1]), (tokens, columns), (tokens, HD))
    return pl.pallas_call(
        functools.partial(
            blocks_kernel, len(xs), len(wkvs), len(state), places, with_q or [True] * len(xs)
        ),
        out_shape=tuple(VMEM(s, f32) for s in shapes),
        in_specs=[vmem] * len(operands),
        out_specs=(vmem,) * 3,
        cost_estimate=cost(sum(2 * x.size * (wq.shape[1] + columns) for x in xs), sum(2 * x.size for x in xs)),
        compiler_params=params,
        name="more_blocks",
    )(*operands)


def last_kv_kernel(count, wkv_count, places, *refs):
    xs, refs = refs[:count], refs[count:]
    gain_ref, wkv_refs, refs = refs[0], refs[1 : 1 + wkv_count], refs[1 + wkv_count :]
    choose_ref, acckv_ref, ssq_ref, scale_ref, *pieces = refs
    me = lax.axis_index("head")
    columns = wkv_refs[0].shape[1]
    kvs = [acckv_ref[:, c * columns : (c + 1) * columns] for c in range(wkv_count)]
    ssq = ssq_ref[...]
    for i, x_ref in enumerate(xs):
        block, width = places[i](me), x_ref.shape[1]
        normed, squares = gained(x_ref[...], gain_ref, block)
        ssq = ssq + squares
        kvs = [kv + dot(normed, w_ref[rows_of(block, width), :]) for kv, w_ref in zip(kvs, wkv_refs)]
    scale = lax.rsqrt(jnp.sum(ssq, axis=1, keepdims=True) / gain_ref.shape[1] + epsilon)
    scale_ref[...] = jnp.broadcast_to(scale, scale_ref.shape)
    kv = jnp.concatenate([(kv * scale).astype(bf16) for kv in kvs], axis=1)
    for i, piece in enumerate(pieces):
        piece[...] = dot_turned(choose_ref[i].astype(bf16), kv).astype(bf16)


def last_kv(xs, places, gain, wkvs, choose, acckv, ssq):
    tokens = xs[0].shape[0]
    columns = len(wkvs) * wkvs[0].shape[1]
    operands = [*xs, *resident_in(gain, *wkvs, choose), acckv, ssq]
    count = choose.shape[0]
    return pl.pallas_call(
        functools.partial(last_kv_kernel, len(xs), len(wkvs), places),
        out_shape=(VMEM((tokens, HD), f32),) + (VMEM((columns // KVH, tokens), bf16),) * count,
        in_specs=[vmem] * len(operands),
        out_specs=(vmem,) * (1 + count),
        cost_estimate=cost(sum(2 * x.size * columns for x in xs), sum(2 * x.size for x in xs)),
        compiler_params=params,
        name="last_keys_values",
    )(*operands)


def last_q_kernel(count, places, *refs):
    xs, rest = refs[:count], refs[count:]
    gain_ref, wq_ref, accq_ref, scale_ref, q_ref = rest
    me = lax.axis_index("head")
    total = accq_ref[...]
    for i, x_ref in enumerate(xs):
        block, width = places[i](me), x_ref.shape[1]
        normed, _ = gained(x_ref[...], gain_ref, block)
        total = total + dot(normed, wq_ref[rows_of(block, width), :])
    q_ref[...] = (total * scale_ref[:, 0:1]).astype(bf16)


def last_q(xs, places, gain, wq, accq, scale):
    operands = [*xs, *resident_in(gain, wq), accq, scale]
    return pl.pallas_call(
        functools.partial(last_q_kernel, len(xs), places),
        out_shape=VMEM((xs[0].shape[0], wq.shape[1]), bf16),
        in_specs=[vmem] * len(operands),
        out_specs=vmem,
        cost_estimate=cost(sum(2 * x.size * wq.shape[1] for x in xs), sum(2 * x.size for x in xs)),
        compiler_params=params,
        name="last_queries",
    )(*operands)


def openings_kernel(sections, doc_ref, first_ref, second_ref):
    tokens = first_ref.shape[0]
    for turn, out_ref in enumerate((first_ref, second_ref)):
        start = (sections - 1 + turn - lax.axis_index("section")) * tokens
        here = start + lax.broadcasted_iota(jnp.int32, out_ref.shape, 0)
        opened = jnp.zeros(out_ref.shape, jnp.int32)
        end = jnp.int32(0)
        for d in range(doc_ref.shape[0]):
            end = end + doc_ref[d]
            opened = jnp.where(end <= here, end, opened)
        out_ref[...] = opened


def openings(doc_lengths, tokens, sections):
    return pl.pallas_call(
        functools.partial(openings_kernel, sections),
        out_shape=(VMEM((tokens, HD), jnp.int32),) * 2,
        in_specs=[smem],
        out_specs=(vmem,) * 2,
        compiler_params=params,
        name="openings",
    )(doc_lengths)


def stacked_heads(q_ref, heads):
    return jnp.concatenate([q_ref[:, h * HD : (h + 1) * HD] for h in range(*heads)], axis=0)


def masked_scores(q, keys, opened_ref, query_start, key_start):
    tokens, count = opened_ref.shape[0], keys.shape[1]
    here = query_start + lax.broadcasted_iota(jnp.int32, (tokens, count), 0)
    there = key_start + lax.broadcasted_iota(jnp.int32, (tokens, count), 1)
    allowed = (there >= opened_ref[:, 0:1]) & (there <= here)
    scores = dot(q, keys) * (1.0 / math.sqrt(HD))
    scores = jnp.where(allowed[None], scores.reshape(-1, tokens, count), masked_score)
    return scores.reshape(-1, count)


def put_together(me, pieces, flips, parts, gather):
    features = pieces[0].shape[0] // 2
    for flip, piece_ref in zip(flips, pieces):
        source = lax.bitwise_xor(me, jnp.int32(flip)) // parts
        piece = piece_ref[...].astype(f32)
        gather[0, rows_of(source, features), :] = piece[:features]
        gather[1, rows_of(source, features), :] = piece[features:]
    return gather[0].astype(bf16), gather[1].astype(bf16)


def first_attend_kernel(sections, heads, flips, parts, opened_ref, q_ref, x_ref, fresh_ref, *refs):
    section = lax.axis_index("section")
    start = (sections - 1 - section) * q_ref.shape[0]
    if flips is None:
        keys_ref, values_ref, out_ref = refs
        keys, values = keys_ref[...], values_ref[...]
    else:
        pieces, (out_ref, keys_ref, values_ref, gather) = refs[: len(flips)], refs[len(flips) :]
        keys, values = put_together(lax.axis_index("head"), pieces, flips, parts, gather)
        keys_ref[...], values_ref[...] = keys, values
    tokens = q_ref.shape[0]
    scores = masked_scores(stacked_heads(q_ref, heads), keys, opened_ref, start, start)
    expon = jnp.exp(scores - jnp.max(scores, axis=1, keepdims=True))
    weights = (expon * (1.0 / jnp.sum(expon, axis=1, keepdims=True))).astype(bf16)
    mixed = dot_turned(weights, values).astype(bf16).astype(f32)
    for i, h in enumerate(range(*heads)):
        columns = slice(h * HD, (h + 1) * HD)
        out = (x_ref[:, columns].astype(f32) + mixed[i * tokens : (i + 1) * tokens]).astype(bf16)
        out = jnp.where(section == sections - 1, fresh_ref[:, columns].astype(f32), out.astype(f32))
        out_ref[:, i * HD : (i + 1) * HD] = out.astype(bf16)


def first_attend(opened, q, x, fresh, pieces, flips, parts, heads, sections):
    tokens = q.shape[0]
    out = (VMEM((tokens, (heads[1] - heads[0]) * HD), bf16),)
    scratch = []
    if flips is not None:
        out = out + (VMEM((HD, tokens), bf16),) * 2
        scratch = [VMEM((2, HD, tokens), f32)]
    operands = [opened, q, x, fresh, *pieces]
    return pl.pallas_call(
        functools.partial(first_attend_kernel, sections, heads, flips, parts),
        out_shape=out,
        in_specs=[vmem] * len(operands),
        out_specs=(vmem,) * len(out),
        scratch_shapes=scratch,
        cost_estimate=cost(1000, 1000),
        compiler_params=params,
        name="first_attend",
    )(*operands)


def resident_kernel(sections, opened_ref, q_ref, keys_ref, values_ref, max_ref, sum_ref, mixed_ref):
    tokens = q_ref.shape[0]
    key_start = (sections - 1 - lax.axis_index("section")) * tokens
    q = stacked_heads(q_ref, (0, q_ref.shape[1] // HD))
    scores = masked_scores(q, keys_ref[...], opened_ref, key_start + tokens, key_start)
    top = jnp.max(scores, axis=1, keepdims=True)
    expon = jnp.exp(scores - top)
    max_ref[...] = jnp.broadcast_to(top, max_ref.shape)
    sum_ref[...] = jnp.broadcast_to(jnp.sum(expon, axis=1, keepdims=True), sum_ref.shape)
    mixed_ref[...] = dot_turned(expon.astype(bf16), values_ref[...])


def resident_attend(opened, q, keys, values, sections):
    rows = q.shape[0] * (q.shape[1] // HD)
    return pl.pallas_call(
        functools.partial(resident_kernel, sections),
        out_shape=(VMEM((rows, HD), f32),) * 3,
        in_specs=[vmem] * 4,
        out_specs=(vmem,) * 3,
        cost_estimate=cost(1000, 1000),
        compiler_params=params,
        name="resident_attend",
    )(opened, q, keys, values)


def second_attend_kernel(sections, flips, parts, x_count, opened_ref, q_ref, max_ref, sum_ref, mixed_ref, *refs):
    x_refs, refs = refs[:x_count], refs[x_count:]
    pieces, (out_ref, gather) = refs[: len(flips)], refs[len(flips) :]
    tokens, heads = q_ref.shape[0], q_ref.shape[1] // HD
    start = (sections - lax.axis_index("section")) * tokens
    keys, values = put_together(lax.axis_index("head"), pieces, flips, parts, gather)
    scores = masked_scores(stacked_heads(q_ref, (0, heads)), keys, opened_ref, start, start)
    top = jnp.maximum(jnp.max(scores, axis=1, keepdims=True), max_ref[...])
    expon = jnp.exp(scores - top)
    shrink = jnp.exp(max_ref[...] - top)
    total = jnp.sum(expon, axis=1, keepdims=True) + shrink * sum_ref[...]
    mixed = dot_turned(expon.astype(bf16), values) + shrink * mixed_ref[...]
    mixed = (mixed * (1.0 / total)).astype(bf16).astype(f32)
    x_width = x_refs[0].shape[1]
    for h in range(heads):
        x_ref, inside = x_refs[h * HD // x_width], h * HD % x_width
        out = x_ref[:, inside : inside + HD].astype(f32) + mixed[h * tokens : (h + 1) * tokens]
        out_ref[:, h * HD : (h + 1) * HD] = out.astype(bf16)


def second_attend(opened, q, xs, resident, pieces, flips, parts, sections):
    tokens = q.shape[0]
    operands = [opened, q, *resident, *xs, *pieces]
    return pl.pallas_call(
        functools.partial(second_attend_kernel, sections, flips, parts, len(xs)),
        out_shape=jax.ShapeDtypeStruct(q.shape, bf16),
        in_specs=[vmem] * len(operands),
        out_specs=vmem,
        scratch_shapes=[VMEM((2, HD, tokens), f32)],
        cost_estimate=cost(1000, 1000),
        compiler_params=params,
        name="second_attend",
    )(*operands)


def shards(entering, fresh_slice, norm_gain, w_query, w_key_value, doc_lengths):
    n = lax.axis_size("head")
    sections = lax.axis_size("section")
    own = entering[0]
    w_q, w_kv = w_query[0], w_key_value[0]
    tokens = own.shape[0]
    heads = w_q.shape[1] // HD
    paired = n == 4
    parts = 2 if paired else 1
    flips = [0, 3] if paired else list(range(n))

    def moved(array, by, flip):
        pairs = [
            (s * n + h, ((s + by) % sections) * n + (h ^ flip)) for s in range(sections) for h in range(n)
        ]
        return lax.ppermute(array, ("section", "head"), pairs)

    def after(array, *others):
        return lax.optimization_barrier((array, *others))[0]

    def exchanged(xs, places, state):
        scale, *pieces = last_kv(xs, places, gain, wkvs, choose, state[1], state[2])
        received = [moved(piece, 0, flip) for piece, flip in zip(pieces[1:], flips[1:])]
        return scale, [pieces[0], *received]

    def rest_of(array):
        every = lax.all_gather(array, "head", axis=0)
        me = lax.axis_index("head")
        return [lax.dynamic_index_in_dim(every, (me + k) % n, 0, False) for k in range(1, n)]

    def place(flip, count=1, part=0):
        return lambda me: lax.bitwise_xor(me, jnp.int32(flip)) * count + part

    following = [functools.partial(lambda k, me: lax.rem(me + k, jnp.int32(n)), k) for k in range(n)]

    if paired:
        over = moved(own, 0, 3)
        beside = moved(own, 0, 1)
        w_kv_beside = moved(w_kv, 0, 1)
    accq, own, gain, wq, wkv, choose = load(own, norm_gain, w_q, w_kv, n, flips, parts)
    if paired:
        wkvs = [wkv, w_kv_beside]
        over = after(over, accq)
        passed = moved(over, 0, 1)
        xs, places, with_q = [own, beside, over], [place(0), place(1), place(3)], [False, True, True]
        state = more_blocks(xs, places, gain, wq, wkvs, [accq], with_q)
        last, places = [passed], [place(2)]
    else:
        wkvs = [wkv]
        state = more_blocks([own], following[:1], gain, wq, wkvs, [accq], [False])
        last, places = rest_of(own), following[1:]
    scale, pieces = exchanged(last, places, state)
    opened = openings(after(doc_lengths, scale), tokens, sections)
    q = last_q(last, places, gain, wq, state[0], scale)
    half = heads // 2 if paired else heads
    sent, keys, values = first_attend(
        opened[0], q, own, fresh_slice, pieces, flips, parts, (0, half), sections
    )

    if paired:
        a1 = moved(sent, 1, 1)
        (sent,) = first_attend(
            opened[0], q, own, fresh_slice, [keys, values], None, parts, (half, heads), sections
        )
        b1 = moved(sent, 1, 1)
        b3 = moved(sent, 1, 3)
        a1 = after(a1, sent)
        a2 = moved(a1, 0, 3)
        a0 = moved(a1, 0, 1)
        state = more_blocks([a1], [place(1, 2, 0)], gain, wq, wkvs, [])
        b3, b1, *state = lax.optimization_barrier((b3, b1, *state))
        b2 = moved(b3, 0, 1)
        b0 = moved(b1, 0, 1)
        a3 = moved(a2, 0, 1)
        places = [place(0, 2, 0), place(2, 2, 0), *(place(flip, 2, 1) for flip in (3, 1, 2))]
        state = more_blocks([a0, a2, b3, b1, b2], places, gain, wq, wkvs, state)
        last, places = [a3, b0], [place(3, 2, 0), place(0, 2, 1)]
        mine = [a0, b0]
    else:
        mine = [moved(sent, 1, 0)]
        state = more_blocks(mine, following[:1], gain, wq, wkvs, [])
        last, places = rest_of(mine[0]), following[1:]
    scale, pieces = exchanged(last, places, state)
    q = last_q(last, places, gain, wq, state[0], scale)
    resident = resident_attend(opened[1], q, keys, values, sections)
    return second_attend(opened[1], q, mine, resident, pieces, flips, parts, sections)[None]


def solution(mesh):
    placed = (
        P("section", None, "head"),
        P(None, "head"),
        P("section", None),
        P("section", None, "head"),
        P("section", None, "head"),
        P(),
    )
    return jax.shard_map(
        shards, mesh=mesh, in_specs=placed, out_specs=P("section", None, "head"), check_vma=False
    )
```

```python
import functools
import math

import jax
import jax.numpy as jnp
from jax import lax
from jax.experimental import pallas as pl
from jax.experimental.pallas import tpu as pltpu
from jax.sharding import PartitionSpec as P

HD = 128
KVH = 4
GROUP = 8

epsilon = 1e-05
score_scale = math.log2(math.e) / math.sqrt(HD)
masked_score = -1e30

VMEM = pltpu.VMEM
f32 = jnp.float32
bf16 = jnp.bfloat16
vmem = pl.BlockSpec(memory_space=VMEM)
smem = pl.BlockSpec(memory_space=pltpu.SMEM)
in_hbm = pl.BlockSpec(memory_space=pltpu.HBM)
params = pltpu.CompilerParams(vmem_limit_bytes=16 * 1024 * 1024)


def resident_in(*arrays):
    return [pltpu.with_memory_space_constraint(a, VMEM) for a in arrays]


def cost(flops, moved):
    return pl.CostEstimate(flops=flops, bytes_accessed=moved, transcendentals=0)


def rows_of(block, width):
    return pl.ds(pl.multiple_of(block * width, width), width)


def from_start(start, width):
    return pl.ds(pl.multiple_of(start, HD), width)


def dot(a, b):
    return jnp.dot(a, b, preferred_element_type=f32)


def dot_turned(a, b):
    return lax.dot_general(a, b, (((1,), (1,)), ((), ())), preferred_element_type=f32)


def gained(x, gain_ref, start):
    width = x.shape[1]
    wide = x.astype(f32)
    squares = wide * wide
    ssq = squares[:, :HD]
    for c in range(HD, width, HD):
        ssq = ssq + squares[:, c : c + HD]
    return (wide * gain_ref[:, from_start(start, width)]).astype(bf16), ssq


def choose_rows(choose_ref, me, n, flips, parts):
    size, columns = choose_ref.shape[1], choose_ref.shape[2] // parts
    features = size // (2 * parts)
    shape = (features, choose_ref.shape[2])
    row = lax.broadcasted_iota(jnp.int32, shape, 0)
    col = lax.broadcasted_iota(jnp.int32, shape, 1)
    offset = col - row * (2 * KVH)
    for i, flip in enumerate(flips):
        group = lax.bitwise_xor(me, jnp.int32(flip)) * KVH // n
        for which in range(2):
            for core in range(parts):
                whose = jnp.where(lax.rem(me, jnp.int32(parts)) == core, 0, 1)
                wanted = whose * columns + group * 2 + which
                first = (which * parts + core) * features
                choose_ref[i, first : first + features, :] = jnp.where(offset == wanted, 1.0, 0.0)


def load_kernel(
    n, flips, parts, x_hbm, gain_hbm, wq_hbm, wkv_hbm, accq_ref, x_ref, gain_ref, wq_ref, wkv_ref, choose_ref, sems
):
    width = x_hbm.shape[1]
    me = lax.axis_index("head")

    def part(step):
        rows = rows_of(lax.rem(me + step, n), width)
        return pltpu.make_async_copy(wq_hbm.at[rows], wq_ref.at[rows], sems.at[step])

    small = (
        pltpu.make_async_copy(x_hbm, x_ref, sems.at[n]),
        pltpu.make_async_copy(gain_hbm, gain_ref, sems.at[n + 1]),
    )
    keys_values = pltpu.make_async_copy(wkv_hbm, wkv_ref, sems.at[n + 2])
    for copy in small:
        copy.start()
    for step in range(n):
        part(step).start()
    keys_values.start()
    choose_rows(choose_ref, me, n, flips, parts)
    for copy in small:
        copy.wait()
    normed, _ = gained(x_ref[...], gain_ref, me * width)
    part(0).wait()
    accq_ref[...] = dot(normed, wq_ref[rows_of(me, width), :])
    for step in range(1, n):
        part(step).wait()
    keys_values.wait()


def load(x, gain, wq, wkv, n, flips, parts):
    tokens, width = x.shape
    columns = wkv.shape[1]
    operands = [pltpu.with_memory_space_constraint(a, pltpu.HBM) for a in (x, gain, wq, wkv)]
    return pl.pallas_call(
        functools.partial(load_kernel, n, flips, parts),
        out_shape=(
            VMEM((tokens, wq.shape[1]), f32),
            VMEM(x.shape, bf16),
            VMEM(gain.shape, f32),
            VMEM(wq.shape, bf16),
            VMEM(wkv.shape, bf16),
            VMEM((len(flips), parts * columns // KVH, parts * columns), f32),
        ),
        in_specs=[in_hbm] * 4,
        out_specs=(vmem,) * 6,
        scratch_shapes=[pltpu.SemaphoreType.DMA((n + 3,))],
        cost_estimate=cost(10**11, 10**9),
        compiler_params=params,
        name="load_and_own_queries",
    )(*operands)


def blocks_kernel(count, wkv_count, carried, places, with_q, *refs):
    xs, refs = refs[:count], refs[count:]
    gain_ref, wq_ref = refs[:2]
    wkv_refs, refs = refs[2 : 2 + wkv_count], refs[2 + wkv_count :]
    old, outs = refs[:carried], refs[carried:]
    me = lax.axis_index("head")
    columns = wkv_refs[0].shape[1]
    q = old[0][...] if carried >= 1 else None
    kvs = [old[1][:, c * columns : (c + 1) * columns] if carried == 3 else None for c in range(wkv_count)]
    ssq = old[2][...] if carried == 3 else None

    def add(total, term):
        return term if total is None else total + term

    for i, x_ref in enumerate(xs):
        start, width = places[i](me), x_ref.shape[1]
        normed, squares = gained(x_ref[...], gain_ref, start)
        ssq = add(ssq, squares)
        rows = from_start(start, width)
        kvs = [add(kv, dot(normed, w_ref[rows, :])) for kv, w_ref in zip(kvs, wkv_refs)]
        if with_q[i]:
            q = add(q, dot(normed, wq_ref[rows, :]))
    outs[0][...] = q
    for c, kv in enumerate(kvs):
        outs[1][:, c * columns : (c + 1) * columns] = kv
    outs[2][...] = ssq


def more_blocks(xs, places, gain, wq, wkvs, state, with_q=None):
    tokens = xs[0].shape[0]
    operands = [*xs, *resident_in(gain, wq, *wkvs), *state]
    columns = len(wkvs) * wkvs[0].shape[1]
    shapes = ((tokens, wq.shape[1]), (tokens, columns), (tokens, HD))
    return pl.pallas_call(
        functools.partial(
            blocks_kernel, len(xs), len(wkvs), len(state), places, with_q or [True] * len(xs)
        ),
        out_shape=tuple(VMEM(s, f32) for s in shapes),
        in_specs=[vmem] * len(operands),
        out_specs=(vmem,) * 3,
        cost_estimate=cost(sum(2 * x.size * (wq.shape[1] + columns) for x in xs), sum(2 * x.size for x in xs)),
        compiler_params=params,
        name="more_blocks",
    )(*operands)


def last_kv_kernel(count, wkv_count, places, *refs):
    xs, refs = refs[:count], refs[count:]
    gain_ref, wkv_refs, refs = refs[0], refs[1 : 1 + wkv_count], refs[1 + wkv_count :]
    choose_ref, acckv_ref, ssq_ref, scale_ref, *pieces = refs
    me = lax.axis_index("head")
    columns = wkv_refs[0].shape[1]
    kvs = [acckv_ref[:, c * columns : (c + 1) * columns] for c in range(wkv_count)]
    ssq = ssq_ref[...]
    for i, x_ref in enumerate(xs):
        start, width = places[i](me), x_ref.shape[1]
        normed, squares = gained(x_ref[...], gain_ref, start)
        ssq = ssq + squares
        kvs = [kv + dot(normed, w_ref[from_start(start, width), :]) for kv, w_ref in zip(kvs, wkv_refs)]
    scale = lax.rsqrt(jnp.sum(ssq, axis=1, keepdims=True) / gain_ref.shape[1] + epsilon)
    scale_ref[...] = jnp.broadcast_to(scale, scale_ref.shape)
    kv = jnp.concatenate([(kv * scale).astype(bf16) for kv in kvs], axis=1)
    for i, piece in enumerate(pieces):
        piece[...] = dot_turned(choose_ref[i].astype(bf16), kv).astype(bf16)


def last_kv(xs, places, gain, wkvs, choose, acckv, ssq):
    tokens = xs[0].shape[0]
    columns = len(wkvs) * wkvs[0].shape[1]
    operands = [*xs, *resident_in(gain, *wkvs, choose), acckv, ssq]
    count = choose.shape[0]
    return pl.pallas_call(
        functools.partial(last_kv_kernel, len(xs), len(wkvs), places),
        out_shape=(VMEM((tokens, HD), f32),) + (VMEM((columns // KVH, tokens), bf16),) * count,
        in_specs=[vmem] * len(operands),
        out_specs=(vmem,) * (1 + count),
        cost_estimate=cost(sum(2 * x.size * columns for x in xs), sum(2 * x.size for x in xs)),
        compiler_params=params,
        name="last_keys_values",
    )(*operands)


def last_q_kernel(count, places, *refs):
    xs, rest = refs[:count], refs[count:]
    gain_ref, wq_ref, accq_ref, scale_ref, q_ref = rest
    me = lax.axis_index("head")
    total = accq_ref[...]
    for i, x_ref in enumerate(xs):
        start, width = places[i](me), x_ref.shape[1]
        normed, _ = gained(x_ref[...], gain_ref, start)
        total = total + dot(normed, wq_ref[from_start(start, width), :])
    q_ref[...] = (total * scale_ref[:, 0:1]).astype(bf16)


def last_q(xs, places, gain, wq, accq, scale):
    operands = [*xs, *resident_in(gain, wq), accq, scale]
    return pl.pallas_call(
        functools.partial(last_q_kernel, len(xs), places),
        out_shape=VMEM((xs[0].shape[0], wq.shape[1]), bf16),
        in_specs=[vmem] * len(operands),
        out_specs=vmem,
        cost_estimate=cost(sum(2 * x.size * wq.shape[1] for x in xs), sum(2 * x.size for x in xs)),
        compiler_params=params,
        name="last_queries",
    )(*operands)


def openings_kernel(sections, doc_ref, first_ref, second_ref):
    tokens = first_ref.shape[0]
    for turn, out_ref in enumerate((first_ref, second_ref)):
        start = (sections - 1 + turn - lax.axis_index("section")) * tokens
        here = start + lax.broadcasted_iota(jnp.int32, out_ref.shape, 0)
        opened = jnp.zeros(out_ref.shape, jnp.int32)
        end = jnp.int32(0)
        for d in range(doc_ref.shape[0]):
            end = end + doc_ref[d]
            opened = jnp.where(end <= here, end, opened)
        out_ref[...] = opened


def openings(doc_lengths, tokens, sections):
    return pl.pallas_call(
        functools.partial(openings_kernel, sections),
        out_shape=(VMEM((tokens, HD), jnp.int32),) * 2,
        in_specs=[smem],
        out_specs=(vmem,) * 2,
        compiler_params=params,
        name="openings",
    )(doc_lengths)


def stacked_heads(q_ref, heads):
    return jnp.concatenate([q_ref[:, h * HD : (h + 1) * HD] for h in range(*heads)], axis=0)


def masked_scores(q, keys, opened_ref, query_start, key_start):
    tokens, count = opened_ref.shape[0], keys.shape[1]
    here = query_start + lax.broadcasted_iota(jnp.int32, (tokens, count), 0)
    there = key_start + lax.broadcasted_iota(jnp.int32, (tokens, count), 1)
    allowed = (there >= opened_ref[:, 0:1]) & (there <= here)
    scores = jnp.where(allowed[None], dot(q, keys).reshape(-1, tokens, count), masked_score)
    return scores.reshape(-1, count)


def mixed_and_sums(expon, values):
    both = jnp.concatenate([values, jnp.ones(values.shape, bf16)], axis=0)
    both = dot_turned(expon.astype(bf16), both)
    return both[:, :HD], both[:, HD:]


def put_together(me, pieces, flips, parts, gather):
    features = pieces[0].shape[0] // 2
    for flip, piece_ref in zip(flips, pieces):
        source = lax.bitwise_xor(me, jnp.int32(flip)) // parts
        piece = piece_ref[...].astype(f32)
        gather[0, rows_of(source, features), :] = piece[:features]
        gather[1, rows_of(source, features), :] = piece[features:]
    return gather[0].astype(bf16), gather[1].astype(bf16)


def first_attend_kernel(sections, heads, flips, parts, opened_ref, q_ref, x_ref, fresh_ref, *refs):
    section = lax.axis_index("section")
    start = (sections - 1 - section) * q_ref.shape[0]
    if flips is None:
        keys_ref, values_ref, out_ref = refs
        keys, values = keys_ref[...], values_ref[...]
    else:
        pieces, (out_ref, keys_ref, values_ref, gather) = refs[: len(flips)], refs[len(flips) :]
        keys, values = put_together(lax.axis_index("head"), pieces, flips, parts, gather)
        keys_ref[...], values_ref[...] = keys, values
    tokens = q_ref.shape[0]
    scores = masked_scores(stacked_heads(q_ref, heads), keys, opened_ref, start, start)
    expon = jnp.exp2((scores - jnp.max(scores, axis=1, keepdims=True)) * score_scale)
    mixed, total = mixed_and_sums(expon, values)
    mixed = (mixed * (1.0 / total)).astype(bf16).astype(f32)
    for i, h in enumerate(range(*heads)):
        columns = slice(h * HD, (h + 1) * HD)
        out = (x_ref[:, columns].astype(f32) + mixed[i * tokens : (i + 1) * tokens]).astype(bf16)
        out = jnp.where(section == sections - 1, fresh_ref[:, columns].astype(f32), out.astype(f32))
        out_ref[:, i * HD : (i + 1) * HD] = out.astype(bf16)


def first_attend(opened, q, x, fresh, pieces, flips, parts, heads, sections):
    tokens = q.shape[0]
    out = (VMEM((tokens, (heads[1] - heads[0]) * HD), bf16),)
    scratch = []
    if flips is not None:
        out = out + (VMEM((HD, tokens), bf16),) * 2
        scratch = [VMEM((2, HD, tokens), f32)]
    operands = [opened, q, x, fresh, *pieces]
    return pl.pallas_call(
        functools.partial(first_attend_kernel, sections, heads, flips, parts),
        out_shape=out,
        in_specs=[vmem] * len(operands),
        out_specs=(vmem,) * len(out),
        scratch_shapes=scratch,
        cost_estimate=cost(1000, 1000),
        compiler_params=params,
        name="first_attend",
    )(*operands)


def resident_kernel(sections, opened_ref, q_ref, keys_ref, values_ref, max_ref, sum_ref, mixed_ref):
    tokens = q_ref.shape[0]
    key_start = (sections - 1 - lax.axis_index("section")) * tokens
    q = stacked_heads(q_ref, (0, q_ref.shape[1] // HD))
    scores = masked_scores(q, keys_ref[...], opened_ref, key_start + tokens, key_start)
    top = jnp.max(scores, axis=1, keepdims=True)
    expon = jnp.exp2((scores - top) * score_scale)
    max_ref[...] = jnp.broadcast_to(top, max_ref.shape)
    mixed_ref[...], sum_ref[...] = mixed_and_sums(expon, values_ref[...])


def resident_attend(opened, q, keys, values, sections):
    rows = q.shape[0] * (q.shape[1] // HD)
    return pl.pallas_call(
        functools.partial(resident_kernel, sections),
        out_shape=(VMEM((rows, HD), f32),) * 3,
        in_specs=[vmem] * 4,
        out_specs=(vmem,) * 3,
        cost_estimate=cost(1000, 1000),
        compiler_params=params,
        name="resident_attend",
    )(opened, q, keys, values)


def second_attend_kernel(sections, flips, parts, x_count, opened_ref, q_ref, max_ref, sum_ref, mixed_ref, *refs):
    x_refs, refs = refs[:x_count], refs[x_count:]
    pieces, (out_ref, gather) = refs[: len(flips)], refs[len(flips) :]
    tokens, heads = q_ref.shape[0], q_ref.shape[1] // HD
    start = (sections - lax.axis_index("section")) * tokens
    keys, values = put_together(lax.axis_index("head"), pieces, flips, parts, gather)
    scores = masked_scores(stacked_heads(q_ref, (0, heads)), keys, opened_ref, start, start)
    top = jnp.maximum(jnp.max(scores, axis=1, keepdims=True), max_ref[...])
    expon = jnp.exp2((scores - top) * score_scale)
    shrink = jnp.exp2((max_ref[...] - top) * score_scale)
    mixed, total = mixed_and_sums(expon, values)
    total = total + shrink * sum_ref[...]
    mixed = mixed + shrink * mixed_ref[...]
    mixed = (mixed * (1.0 / total)).astype(bf16).astype(f32)
    where = [(x_ref, inside) for x_ref in x_refs for inside in range(0, x_ref.shape[1], HD)]
    for h, (x_ref, inside) in enumerate(where):
        out = x_ref[:, inside : inside + HD].astype(f32) + mixed[h * tokens : (h + 1) * tokens]
        out_ref[:, h * HD : (h + 1) * HD] = out.astype(bf16)


def second_attend(opened, q, xs, resident, pieces, flips, parts, sections):
    tokens = q.shape[0]
    operands = [opened, q, *resident, *xs, *pieces]
    return pl.pallas_call(
        functools.partial(second_attend_kernel, sections, flips, parts, len(xs)),
        out_shape=jax.ShapeDtypeStruct(q.shape, bf16),
        in_specs=[vmem] * len(operands),
        out_specs=vmem,
        scratch_shapes=[VMEM((2, HD, tokens), f32)],
        cost_estimate=cost(1000, 1000),
        compiler_params=params,
        name="second_attend",
    )(*operands)


def shards(entering, fresh_slice, norm_gain, w_query, w_key_value, doc_lengths):
    n = lax.axis_size("head")
    sections = lax.axis_size("section")
    own = entering[0]
    w_q, w_kv = w_query[0], w_key_value[0]
    tokens, width = own.shape
    heads = w_q.shape[1] // HD
    paired = n == 4
    parts = 2 if paired else 1
    flips = [0, 3] if paired else list(range(n))

    def moved(array, by, flip):
        pairs = [
            (s * n + h, ((s + by) % sections) * n + (h ^ flip)) for s in range(sections) for h in range(n)
        ]
        return lax.ppermute(array, ("section", "head"), pairs)

    def after(array, *others):
        return lax.optimization_barrier((array, *others))[0]

    def exchanged(xs, places, state):
        scale, *pieces = last_kv(xs, places, gain, wkvs, choose, state[1], state[2])
        received = [moved(piece, 0, flip) for piece, flip in zip(pieces[1:], flips[1:])]
        return scale, [pieces[0], *received]

    def rest_of(array):
        every = lax.all_gather(array, "head", axis=0)
        me = lax.axis_index("head")
        return [lax.dynamic_index_in_dim(every, (me + k) % n, 0, False) for k in range(1, n)]

    def place(flip, offset=0):
        return lambda me: lax.bitwise_xor(me, jnp.int32(flip)) * width + offset

    following = [functools.partial(lambda k, me: lax.rem(me + k, jnp.int32(n)) * width, k) for k in range(n)]

    if paired:
        over = moved(own, 0, 3)
        beside = moved(own, 0, 1)
        w_kv_beside = moved(w_kv, 0, 1)
    accq, own, gain, wq, wkv, choose = load(own, norm_gain, w_q, w_kv, n, flips, parts)
    if paired:
        wkvs = [wkv, w_kv_beside]
        over = after(over, accq)
        passed = moved(over, 0, 1)
        xs, places, with_q = [own, beside, over], [place(0), place(1), place(3)], [False, True, True]
        state = more_blocks(xs, places, gain, wq, wkvs, [accq], with_q)
        last, places = [passed], [place(2)]
    else:
        wkvs = [wkv]
        state = more_blocks([own], following[:1], gain, wq, wkvs, [accq], [False])
        last, places = rest_of(own), following[1:]
    scale, pieces = exchanged(last, places, state)
    opened = openings(after(doc_lengths, scale), tokens, sections)
    q = last_q(last, places, gain, wq, state[0], scale)
    part = heads // 2 if paired else heads
    split = part * HD
    sent, keys, values = first_attend(
        opened[0], q, own, fresh_slice, pieces, flips, parts, (0, part), sections
    )

    if paired:
        a1 = moved(sent, 1, 1)
        (sent,) = first_attend(
            opened[0], q, own, fresh_slice, [keys, values], None, parts, (part, heads), sections
        )
        b1 = moved(sent, 1, 1)
        b3 = moved(sent, 1, 3)
        a1 = after(a1, sent)
        a2 = moved(a1, 0, 3)
        a0 = moved(a1, 0, 1)
        state = more_blocks([a1], [place(1)], gain, wq, wkvs, [])
        b3, b1, *state = lax.optimization_barrier((b3, b1, *state))
        b2 = moved(b3, 0, 1)
        b0 = moved(b1, 0, 1)
        a3 = moved(a2, 0, 1)
        places = [place(0), place(2), *(place(flip, split) for flip in (3, 1, 2))]
        state = more_blocks([a0, a2, b3, b1, b2], places, gain, wq, wkvs, state)
        last, places = [a3, b0], [place(3), place(0, split)]
        mine = [a0, b0]
    else:
        mine = [moved(sent, 1, 0)]
        state = more_blocks(mine, following[:1], gain, wq, wkvs, [])
        last, places = rest_of(mine[0]), following[1:]
    scale, pieces = exchanged(last, places, state)
    q = last_q(last, places, gain, wq, state[0], scale)
    resident = resident_attend(opened[1], q, keys, values, sections)
    return second_attend(opened[1], q, mine, resident, pieces, flips, parts, sections)[None]


def solution(mesh):
    placed = (
        P("section", None, "head"),
        P(None, "head"),
        P("section", None),
        P("section", None, "head"),
        P("section", None, "head"),
        P(),
    )
    return jax.shard_map(
        shards, mesh=mesh, in_specs=placed, out_specs=P("section", None, "head"), check_vma=False
    )
```

```python
import functools
import math

import jax
import jax.numpy as jnp
from jax import lax
from jax.experimental import pallas as pl
from jax.experimental.pallas import tpu as pltpu
from jax.sharding import PartitionSpec as P

HD = 128
KVH = 4
GROUP = 8

epsilon = 1e-05
score_scale = math.log2(math.e) / math.sqrt(HD)
masked_score = -1e30

VMEM = pltpu.VMEM
f32 = jnp.float32
bf16 = jnp.bfloat16
vmem = pl.BlockSpec(memory_space=VMEM)
smem = pl.BlockSpec(memory_space=pltpu.SMEM)
in_hbm = pl.BlockSpec(memory_space=pltpu.HBM)
params = pltpu.CompilerParams(vmem_limit_bytes=16 * 1024 * 1024)


def resident_in(*arrays):
    return [pltpu.with_memory_space_constraint(a, VMEM) for a in arrays]


def cost(flops, moved):
    return pl.CostEstimate(flops=flops, bytes_accessed=moved, transcendentals=0)


def rows_of(block, width):
    return pl.ds(pl.multiple_of(block * width, width), width)


def from_start(start, width):
    return pl.ds(pl.multiple_of(start, HD), width)


def dot(a, b):
    return jnp.dot(a, b, preferred_element_type=f32)


def dot_turned(a, b):
    return lax.dot_general(a, b, (((1,), (1,)), ((), ())), preferred_element_type=f32)


def picked(x_ref, fresh_ref, offset, first):
    wide = x_ref[...].astype(f32)
    if fresh_ref is None:
        return wide
    return jnp.where(first, fresh_ref[:, offset : offset + wide.shape[1]].astype(f32), wide)


def blocks_of(refs, count, offsets):
    xs, rest = refs[:count], refs[count:]
    if offsets is None:
        return [(x, None, 0) for x in xs], rest
    return list(zip(xs, rest[:count], offsets)), rest[count:]


def gained(wide, gain_ref, start):
    width = wide.shape[1]
    squares = wide * wide
    ssq = squares[:, :HD]
    for c in range(HD, width, HD):
        ssq = ssq + squares[:, c : c + HD]
    return (wide * gain_ref[:, from_start(start, width)]).astype(bf16), ssq


def choose_rows(choose_ref, me, n, flips, parts):
    size, columns = choose_ref.shape[1], choose_ref.shape[2] // parts
    features = size // (2 * parts)
    shape = (features, choose_ref.shape[2])
    row = lax.broadcasted_iota(jnp.int32, shape, 0)
    col = lax.broadcasted_iota(jnp.int32, shape, 1)
    offset = col - row * (2 * KVH)
    for i, flip in enumerate(flips):
        group = lax.bitwise_xor(me, jnp.int32(flip)) * KVH // n
        for which in range(2):
            for core in range(parts):
                whose = jnp.where(lax.rem(me, jnp.int32(parts)) == core, 0, 1)
                wanted = whose * columns + group * 2 + which
                first = (which * parts + core) * features
                choose_ref[i, first : first + features, :] = jnp.where(offset == wanted, 1.0, 0.0)


def load_kernel(
    n, flips, parts, x_hbm, gain_hbm, wq_hbm, wkv_hbm, accq_ref, x_ref, gain_ref, wq_ref, wkv_ref, choose_ref, sems
):
    width = x_hbm.shape[1]
    me = lax.axis_index("head")

    def part(step):
        rows = rows_of(lax.rem(me + step, n), width)
        return pltpu.make_async_copy(wq_hbm.at[rows], wq_ref.at[rows], sems.at[step])

    small = (
        pltpu.make_async_copy(x_hbm, x_ref, sems.at[n]),
        pltpu.make_async_copy(gain_hbm, gain_ref, sems.at[n + 1]),
    )
    keys_values = pltpu.make_async_copy(wkv_hbm, wkv_ref, sems.at[n + 2])
    for copy in small:
        copy.start()
    for step in range(n):
        part(step).start()
    keys_values.start()
    choose_rows(choose_ref, me, n, flips, parts)
    for copy in small:
        copy.wait()
    normed, _ = gained(x_ref[...].astype(f32), gain_ref, me * width)
    part(0).wait()
    accq_ref[...] = dot(normed, wq_ref[rows_of(me, width), :])
    for step in range(1, n):
        part(step).wait()
    keys_values.wait()


def load(x, gain, wq, wkv, n, flips, parts):
    tokens, width = x.shape
    columns = wkv.shape[1]
    operands = [pltpu.with_memory_space_constraint(a, pltpu.HBM) for a in (x, gain, wq, wkv)]
    return pl.pallas_call(
        functools.partial(load_kernel, n, flips, parts),
        out_shape=(
            VMEM((tokens, wq.shape[1]), f32),
            VMEM(x.shape, bf16),
            VMEM(gain.shape, f32),
            VMEM(wq.shape, bf16),
            VMEM(wkv.shape, bf16),
            VMEM((len(flips), parts * columns // KVH, parts * columns), f32),
        ),
        in_specs=[in_hbm] * 4,
        out_specs=(vmem,) * 6,
        scratch_shapes=[pltpu.SemaphoreType.DMA((n + 3,))],
        cost_estimate=cost(10**11, 10**9),
        compiler_params=params,
        name="load_and_own_queries",
    )(*operands)


def blocks_kernel(count, wkv_count, carried, places, offsets, with_q, *refs):
    blocks, refs = blocks_of(refs, count, offsets)
    first = lax.axis_index("section") == 0
    gain_ref, wq_ref = refs[:2]
    wkv_refs, refs = refs[2 : 2 + wkv_count], refs[2 + wkv_count :]
    old, outs = refs[:carried], refs[carried:]
    me = lax.axis_index("head")
    columns = wkv_refs[0].shape[1]
    q = old[0][...] if carried >= 1 else None
    kvs = [old[1][:, c * columns : (c + 1) * columns] if carried == 3 else None for c in range(wkv_count)]
    ssq = old[2][...] if carried == 3 else None

    def add(total, term):
        return term if total is None else total + term

    for i, block in enumerate(blocks):
        start, width = places[i](me), block[0].shape[1]
        normed, squares = gained(picked(*block, first), gain_ref, start)
        ssq = add(ssq, squares)
        rows = from_start(start, width)
        kvs = [add(kv, dot(normed, w_ref[rows, :])) for kv, w_ref in zip(kvs, wkv_refs)]
        if with_q[i]:
            q = add(q, dot(normed, wq_ref[rows, :]))
    outs[0][...] = q
    for c, kv in enumerate(kvs):
        outs[1][:, c * columns : (c + 1) * columns] = kv
    outs[2][...] = ssq


def more_blocks(xs, places, gain, wq, wkvs, state, with_q=None, fresh=(), offsets=None):
    tokens = xs[0].shape[0]
    operands = [*xs, *fresh, *resident_in(gain, wq, *wkvs), *state]
    columns = len(wkvs) * wkvs[0].shape[1]
    shapes = ((tokens, wq.shape[1]), (tokens, columns), (tokens, HD))
    return pl.pallas_call(
        functools.partial(
            blocks_kernel, len(xs), len(wkvs), len(state), places, offsets, with_q or [True] * len(xs)
        ),
        out_shape=tuple(VMEM(s, f32) for s in shapes),
        in_specs=[vmem] * len(operands),
        out_specs=(vmem,) * 3,
        cost_estimate=cost(sum(2 * x.size * (wq.shape[1] + columns) for x in xs), sum(2 * x.size for x in xs)),
        compiler_params=params,
        name="more_blocks",
    )(*operands)


def last_kv_kernel(count, wkv_count, places, offsets, *refs):
    blocks, refs = blocks_of(refs, count, offsets)
    first = lax.axis_index("section") == 0
    gain_ref, wkv_refs, refs = refs[0], refs[1 : 1 + wkv_count], refs[1 + wkv_count :]
    choose_ref, acckv_ref, ssq_ref, scale_ref, *pieces = refs
    me = lax.axis_index("head")
    columns = wkv_refs[0].shape[1]
    kvs = [acckv_ref[:, c * columns : (c + 1) * columns] for c in range(wkv_count)]
    ssq = ssq_ref[...]
    for i, block in enumerate(blocks):
        start, width = places[i](me), block[0].shape[1]
        normed, squares = gained(picked(*block, first), gain_ref, start)
        ssq = ssq + squares
        kvs = [kv + dot(normed, w_ref[from_start(start, width), :]) for kv, w_ref in zip(kvs, wkv_refs)]
    scale = lax.rsqrt(jnp.sum(ssq, axis=1, keepdims=True) / gain_ref.shape[1] + epsilon)
    scale_ref[...] = jnp.broadcast_to(scale, scale_ref.shape)
    kv = jnp.concatenate([(kv * scale).astype(bf16) for kv in kvs], axis=1)
    for i, piece in enumerate(pieces):
        piece[...] = dot_turned(choose_ref[i].astype(bf16), kv).astype(bf16)


def last_kv(xs, places, gain, wkvs, choose, acckv, ssq, fresh=(), offsets=None):
    tokens = xs[0].shape[0]
    columns = len(wkvs) * wkvs[0].shape[1]
    operands = [*xs, *fresh, *resident_in(gain, *wkvs, choose), acckv, ssq]
    count = choose.shape[0]
    return pl.pallas_call(
        functools.partial(last_kv_kernel, len(xs), len(wkvs), places, offsets),
        out_shape=(VMEM((tokens, HD), f32),) + (VMEM((columns // KVH, tokens), bf16),) * count,
        in_specs=[vmem] * len(operands),
        out_specs=(vmem,) * (1 + count),
        cost_estimate=cost(sum(2 * x.size * columns for x in xs), sum(2 * x.size for x in xs)),
        compiler_params=params,
        name="last_keys_values",
    )(*operands)


def last_q_kernel(count, places, offsets, *refs):
    blocks, rest = blocks_of(refs, count, offsets)
    first = lax.axis_index("section") == 0
    gain_ref, wq_ref, accq_ref, scale_ref, q_ref = rest
    me = lax.axis_index("head")
    total = accq_ref[...]
    for i, block in enumerate(blocks):
        start, width = places[i](me), block[0].shape[1]
        normed, _ = gained(picked(*block, first), gain_ref, start)
        total = total + dot(normed, wq_ref[from_start(start, width), :])
    q_ref[...] = (total * scale_ref[:, 0:1]).astype(bf16)


def last_q(xs, places, gain, wq, accq, scale, fresh=(), offsets=None):
    operands = [*xs, *fresh, *resident_in(gain, wq), accq, scale]
    return pl.pallas_call(
        functools.partial(last_q_kernel, len(xs), places, offsets),
        out_shape=VMEM((xs[0].shape[0], wq.shape[1]), bf16),
        in_specs=[vmem] * len(operands),
        out_specs=vmem,
        cost_estimate=cost(sum(2 * x.size * wq.shape[1] for x in xs), sum(2 * x.size for x in xs)),
        compiler_params=params,
        name="last_queries",
    )(*operands)


def openings_kernel(sections, doc_ref, first_ref, second_ref):
    tokens = first_ref.shape[0]
    for turn, out_ref in enumerate((first_ref, second_ref)):
        start = (sections - 1 + turn - lax.axis_index("section")) * tokens
        here = start + lax.broadcasted_iota(jnp.int32, out_ref.shape, 0)
        opened = jnp.zeros(out_ref.shape, jnp.int32)
        end = jnp.int32(0)
        for d in range(doc_ref.shape[0]):
            end = end + doc_ref[d]
            opened = jnp.where(end <= here, end, opened)
        out_ref[...] = opened


def openings(doc_lengths, tokens, sections):
    return pl.pallas_call(
        functools.partial(openings_kernel, sections),
        out_shape=(VMEM((tokens, HD), jnp.int32),) * 2,
        in_specs=[smem],
        out_specs=(vmem,) * 2,
        compiler_params=params,
        name="openings",
    )(doc_lengths)


def stacked_heads(q_ref, heads):
    return jnp.concatenate([q_ref[:, h * HD : (h + 1) * HD] for h in range(*heads)], axis=0)


def masked_scores(q, keys, opened_ref, query_start, key_start):
    tokens, count = opened_ref.shape[0], keys.shape[1]
    here = query_start + lax.broadcasted_iota(jnp.int32, (tokens, count), 0)
    there = key_start + lax.broadcasted_iota(jnp.int32, (tokens, count), 1)
    allowed = (there >= opened_ref[:, 0:1]) & (there <= here)
    scores = jnp.where(allowed[None], dot(q, keys).reshape(-1, tokens, count), masked_score)
    return scores.reshape(-1, count)


def mixed_and_sums(expon, values):
    both = jnp.concatenate([values, jnp.ones(values.shape, bf16)], axis=0)
    both = dot_turned(expon.astype(bf16), both)
    return both[:, :HD], both[:, HD:]


def put_together(me, pieces, flips, parts, gather):
    features = pieces[0].shape[0] // 2
    for flip, piece_ref in zip(flips, pieces):
        source = lax.bitwise_xor(me, jnp.int32(flip)) // parts
        piece = piece_ref[...].astype(f32)
        gather[0, rows_of(source, features), :] = piece[:features]
        gather[1, rows_of(source, features), :] = piece[features:]
    return gather[0].astype(bf16), gather[1].astype(bf16)


def first_attend_kernel(sections, heads, flips, parts, opened_ref, q_ref, x_ref, *refs):
    start = (sections - 1 - lax.axis_index("section")) * q_ref.shape[0]
    if flips is None:
        keys_ref, values_ref, out_ref = refs
        keys, values = keys_ref[...], values_ref[...]
    else:
        pieces, (out_ref, keys_ref, values_ref, gather) = refs[: len(flips)], refs[len(flips) :]
        keys, values = put_together(lax.axis_index("head"), pieces, flips, parts, gather)
        keys_ref[...], values_ref[...] = keys, values
    tokens = q_ref.shape[0]
    scores = masked_scores(stacked_heads(q_ref, heads), keys, opened_ref, start, start)
    expon = jnp.exp2((scores - jnp.max(scores, axis=1, keepdims=True)) * score_scale)
    mixed, total = mixed_and_sums(expon, values)
    mixed = (mixed * (1.0 / total)).astype(bf16).astype(f32)
    for i, h in enumerate(range(*heads)):
        columns = slice(h * HD, (h + 1) * HD)
        out = x_ref[:, columns].astype(f32) + mixed[i * tokens : (i + 1) * tokens]
        out_ref[:, i * HD : (i + 1) * HD] = out.astype(bf16)


def first_attend(opened, q, x, pieces, flips, parts, heads, sections):
    tokens = q.shape[0]
    out = (VMEM((tokens, (heads[1] - heads[0]) * HD), bf16),)
    scratch = []
    if flips is not None:
        out = out + (VMEM((HD, tokens), bf16),) * 2
        scratch = [VMEM((2, HD, tokens), f32)]
    operands = [opened, q, x, *pieces]
    return pl.pallas_call(
        functools.partial(first_attend_kernel, sections, heads, flips, parts),
        out_shape=out,
        in_specs=[vmem] * len(operands),
        out_specs=(vmem,) * len(out),
        scratch_shapes=scratch,
        cost_estimate=cost(10**10, 1000),
        compiler_params=params,
        name="first_attend",
    )(*operands)


def resident_kernel(sections, opened_ref, q_ref, keys_ref, values_ref, max_ref, sum_ref, mixed_ref):
    tokens = q_ref.shape[0]
    key_start = (sections - 1 - lax.axis_index("section")) * tokens
    q = stacked_heads(q_ref, (0, q_ref.shape[1] // HD))
    scores = masked_scores(q, keys_ref[...], opened_ref, key_start + tokens, key_start)
    top = jnp.max(scores, axis=1, keepdims=True)
    expon = jnp.exp2((scores - top) * score_scale)
    max_ref[...] = jnp.broadcast_to(top, max_ref.shape)
    mixed_ref[...], sum_ref[...] = mixed_and_sums(expon, values_ref[...])


def resident_attend(opened, q, keys, values, sections):
    rows = q.shape[0] * (q.shape[1] // HD)
    return pl.pallas_call(
        functools.partial(resident_kernel, sections),
        out_shape=(VMEM((rows, HD), f32),) * 3,
        in_specs=[vmem] * 4,
        out_specs=(vmem,) * 3,
        cost_estimate=cost(10**10, 1000),
        compiler_params=params,
        name="resident_attend",
    )(opened, q, keys, values)


def second_attend_kernel(
    sections, flips, parts, x_count, with_fresh, opened_ref, q_ref, max_ref, sum_ref, mixed_ref, *refs
):
    x_refs, refs = refs[:x_count], refs[x_count:]
    fresh_ref, refs = (refs[0], refs[1:]) if with_fresh else (None, refs)
    first = lax.axis_index("section") == 0
    pieces, (out_ref, gather) = refs[: len(flips)], refs[len(flips) :]
    tokens, heads = q_ref.shape[0], q_ref.shape[1] // HD
    start = (sections - lax.axis_index("section")) * tokens
    keys, values = put_together(lax.axis_index("head"), pieces, flips, parts, gather)
    scores = masked_scores(stacked_heads(q_ref, (0, heads)), keys, opened_ref, start, start)
    top = jnp.maximum(jnp.max(scores, axis=1, keepdims=True), max_ref[...])
    expon = jnp.exp2((scores - top) * score_scale)
    shrink = jnp.exp2((max_ref[...] - top) * score_scale)
    mixed, total = mixed_and_sums(expon, values)
    total = total + shrink * sum_ref[...]
    mixed = mixed + shrink * mixed_ref[...]
    mixed = (mixed * (1.0 / total)).astype(bf16).astype(f32)
    where = [(x_ref, inside) for x_ref in x_refs for inside in range(0, x_ref.shape[1], HD)]
    for h, (x_ref, inside) in enumerate(where):
        x = picked(x_ref.at[:, inside : inside + HD], fresh_ref, h * HD, first)
        out = x + mixed[h * tokens : (h + 1) * tokens]
        out_ref[:, h * HD : (h + 1) * HD] = out.astype(bf16)


def second_attend(opened, q, xs, fresh, resident, pieces, flips, parts, sections):
    tokens = q.shape[0]
    operands = [opened, q, *resident, *xs, *fresh, *pieces]
    return pl.pallas_call(
        functools.partial(second_attend_kernel, sections, flips, parts, len(xs), len(fresh) == 1),
        out_shape=jax.ShapeDtypeStruct(q.shape, bf16),
        in_specs=[vmem] * len(operands),
        out_specs=vmem,
        scratch_shapes=[VMEM((2, HD, tokens), f32)],
        cost_estimate=cost(10**10, 1000),
        compiler_params=params,
        name="second_attend",
    )(*operands)


def shards(entering, fresh_slice, norm_gain, w_query, w_key_value, doc_lengths):
    n = lax.axis_size("head")
    sections = lax.axis_size("section")
    own = entering[0]
    w_q, w_kv = w_query[0], w_key_value[0]
    tokens, width = own.shape
    heads = w_q.shape[1] // HD
    paired = n == 4
    parts = 2 if paired else 1
    flips = [0, 3] if paired else list(range(n))

    def moved(array, by, flip, among=None):
        pairs = [
            (s * n + h, (s + by) * n + (h ^ flip))
            for s in among or range(sections - by)
            for h in range(n)
        ]
        return lax.ppermute(array, ("section", "head"), pairs)

    def after(array, *others):
        return lax.optimization_barrier((array, *others))[0]

    def exchanged(xs, places, state, *fresh):
        scale, *pieces = last_kv(xs, places, gain, wkvs, choose, state[1], state[2], *fresh)
        received = [moved(piece, 0, flip) for piece, flip in zip(pieces[1:], flips[1:])]
        return scale, [pieces[0], *received]

    def rest_of(array):
        every = lax.all_gather(array, "head", axis=0)
        me = lax.axis_index("head")
        return [lax.dynamic_index_in_dim(every, (me + k) % n, 0, False) for k in range(1, n)]

    def place(flip, offset=0):
        return lambda me: lax.bitwise_xor(me, jnp.int32(flip)) * width + offset

    following = [functools.partial(lambda k, me: lax.rem(me + k, jnp.int32(n)) * width, k) for k in range(n)]

    if paired:
        over = moved(own, 0, 3)
        beside = moved(own, 0, 1)
        w_kv_beside = moved(w_kv, 0, 1)
    accq, own, gain, wq, wkv, choose = load(own, norm_gain, w_q, w_kv, n, flips, parts)
    opened = openings(after(doc_lengths, accq), tokens, sections)
    if paired:
        wkvs = [wkv, w_kv_beside]
        over, *opened = lax.optimization_barrier((over, *opened))
        passed = moved(over, 0, 1)
        xs, places, with_q = [own, beside, over], [place(0), place(1), place(3)], [False, True, True]
        state = more_blocks(xs, places, gain, wq, wkvs, [accq], with_q)
        last, places = [passed], [place(2)]
    else:
        wkvs = [wkv]
        state = more_blocks([own], following[:1], gain, wq, wkvs, [accq], [False])
        last, places = rest_of(own), following[1:]
    scale, pieces = exchanged(last, places, state)
    q = last_q(last, places, gain, wq, state[0], scale)
    part = heads // 2 if paired else heads
    split = part * HD
    sent, keys, values = first_attend(opened[0], q, own, pieces, flips, parts, (0, part), sections)

    if paired:
        rest, start = range(1, sections), range(1)
        f0 = fresh_slice
        f3 = moved(after(f0, scale), 0, 3, start)
        a1 = moved(sent, 1, 1)
        (sent,) = first_attend(
            opened[0], q, own, [keys, values], None, parts, (part, heads), sections
        )
        f1 = moved(after(f0, scale), 0, 1, start)
        b1 = moved(sent, 1, 1)
        b3 = moved(sent, 1, 3)
        a1 = after(a1, sent)
        a2 = moved(a1, 0, 3, rest)
        a0 = moved(a1, 0, 1, rest)
        state = more_blocks([a1], [place(1)], gain, wq, wkvs, [], None, [f1], [0])
        f3 = after(f3, sent)
        f2 = moved(f3, 0, 1, start)
        b3, b1, *state = lax.optimization_barrier((b3, b1, *state))
        b2 = moved(b3, 0, 1, rest)
        b0 = moved(b1, 0, 1, rest)
        a3 = moved(a2, 0, 1, rest)
        places = [place(0), place(2), *(place(flip, split) for flip in (3, 1, 2))]
        state = more_blocks(
            [a0, a2, b3, b1, b2], places, gain, wq, wkvs, state, None,
            [f0, f2, f3, f1, f2], [0, 0, split, split, split],
        )
        last, places = [a3, b0], [place(3), place(0, split)]
        mine, fresh, own_fresh = [a0, b0], ([f3, f0], [0, split]), [f0]
    else:
        mine = [jnp.where(lax.axis_index("section") == 0, fresh_slice, moved(sent, 1, 0))]
        state = more_blocks(mine, following[:1], gain, wq, wkvs, [])
        last, places = rest_of(mine[0]), following[1:]
        fresh, own_fresh = (), []
    scale, pieces = exchanged(last, places, state, *fresh)
    q = last_q(last, places, gain, wq, state[0], scale, *fresh)
    resident = resident_attend(opened[1], q, keys, values, sections)
    return second_attend(opened[1], q, mine, own_fresh, resident, pieces, flips, parts, sections)[None]


def solution(mesh):
    placed = (
        P("section", None, "head"),
        P(None, "head"),
        P("section", None),
        P("section", None, "head"),
        P("section", None, "head"),
        P(),
    )
    return jax.shard_map(
        shards, mesh=mesh, in_specs=placed, out_specs=P("section", None, "head"), check_vma=False
    )
```

```python
import functools
import math

import jax
import jax.numpy as jnp
from jax import lax
from jax.experimental import pallas as pl
from jax.experimental.pallas import tpu as pltpu
from jax.sharding import PartitionSpec as P

HD = 128
KVH = 4
GROUP = 8

epsilon = 1e-05
score_scale = math.log2(math.e) / math.sqrt(HD)
masked_score = -1e30

VMEM = pltpu.VMEM
f32 = jnp.float32
bf16 = jnp.bfloat16
vmem = pl.BlockSpec(memory_space=VMEM)
smem = pl.BlockSpec(memory_space=pltpu.SMEM)
in_hbm = pl.BlockSpec(memory_space=pltpu.HBM)
params = pltpu.CompilerParams(vmem_limit_bytes=16 * 1024 * 1024)


def resident_in(*arrays):
    return [pltpu.with_memory_space_constraint(a, VMEM) for a in arrays]


def cost(flops, moved):
    return pl.CostEstimate(flops=flops, bytes_accessed=moved, transcendentals=0)


def rows_of(block, width):
    return pl.ds(pl.multiple_of(block * width, width), width)


def from_start(start, width):
    return pl.ds(pl.multiple_of(start, HD), width)


def dot(a, b):
    return jnp.dot(a, b, preferred_element_type=f32)


def dot_turned(a, b):
    return lax.dot_general(a, b, (((1,), (1,)), ((), ())), preferred_element_type=f32)


def gained(x, gain_ref, start):
    width = x.shape[1]
    wide = x.astype(f32)
    squares = wide * wide
    ssq = squares[:, :HD]
    for c in range(HD, width, HD):
        ssq = ssq + squares[:, c : c + HD]
    return (wide * gain_ref[:, from_start(start, width)]).astype(bf16), ssq


def choose_rows(choose_ref, me, n, flips, parts):
    size, columns = choose_ref.shape[1], choose_ref.shape[2] // parts
    features = size // (2 * parts)
    shape = (features, choose_ref.shape[2])
    row = lax.broadcasted_iota(jnp.int32, shape, 0)
    col = lax.broadcasted_iota(jnp.int32, shape, 1)
    offset = col - row * (2 * KVH)
    for i, flip in enumerate(flips):
        group = lax.bitwise_xor(me, jnp.int32(flip)) * KVH // n
        for which in range(2):
            for core in range(parts):
                whose = jnp.where(lax.rem(me, jnp.int32(parts)) == core, 0, 1)
                wanted = whose * columns + group * 2 + which
                first = (which * parts + core) * features
                choose_ref[i, first : first + features, :] = jnp.where(offset == wanted, 1.0, 0.0)


def load_kernel(
    n, flips, parts, x_hbm, gain_hbm, wq_hbm, wkv_hbm, accq_ref, x_ref, gain_ref, wq_ref, wkv_ref, choose_ref, sems
):
    width = x_hbm.shape[1]
    me = lax.axis_index("head")

    def part(step):
        rows = rows_of(lax.rem(me + step, n), width)
        return pltpu.make_async_copy(wq_hbm.at[rows], wq_ref.at[rows], sems.at[step])

    small = (
        pltpu.make_async_copy(x_hbm, x_ref, sems.at[n]),
        pltpu.make_async_copy(gain_hbm, gain_ref, sems.at[n + 1]),
    )
    keys_values = pltpu.make_async_copy(wkv_hbm, wkv_ref, sems.at[n + 2])
    for copy in small:
        copy.start()
    for step in range(n):
        part(step).start()
    keys_values.start()
    choose_rows(choose_ref, me, n, flips, parts)
    for copy in small:
        copy.wait()
    normed, _ = gained(x_ref[...], gain_ref, me * width)
    part(0).wait()
    accq_ref[...] = dot(normed, wq_ref[rows_of(me, width), :])
    for step in range(1, n):
        part(step).wait()
    keys_values.wait()


def load(x, gain, wq, wkv, n, flips, parts):
    tokens, width = x.shape
    columns = wkv.shape[1]
    operands = [pltpu.with_memory_space_constraint(a, pltpu.HBM) for a in (x, gain, wq, wkv)]
    return pl.pallas_call(
        functools.partial(load_kernel, n, flips, parts),
        out_shape=(
            VMEM((tokens, wq.shape[1]), f32),
            VMEM(x.shape, bf16),
            VMEM(gain.shape, f32),
            VMEM(wq.shape, bf16),
            VMEM(wkv.shape, bf16),
            VMEM((len(flips), parts * columns // KVH, parts * columns), f32),
        ),
        in_specs=[in_hbm] * 4,
        out_specs=(vmem,) * 6,
        scratch_shapes=[pltpu.SemaphoreType.DMA((n + 3,))],
        cost_estimate=cost(10**11, 10**9),
        compiler_params=params,
        name="load_and_own_queries",
    )(*operands)


def blocks_kernel(count, wkv_count, carried, places, with_q, *refs):
    xs, refs = refs[:count], refs[count:]
    gain_ref, wq_ref = refs[:2]
    wkv_refs, refs = refs[2 : 2 + wkv_count], refs[2 + wkv_count :]
    old, outs = refs[:carried], refs[carried:]
    me = lax.axis_index("head")
    columns = wkv_refs[0].shape[1]
    q = old[0][...] if carried >= 1 else None
    kvs = [old[1][:, c * columns : (c + 1) * columns] if carried == 3 else None for c in range(wkv_count)]
    ssq = old[2][...] if carried == 3 else None

    def add(total, term):
        return term if total is None else total + term

    for i, x_ref in enumerate(xs):
        start, width = places[i](me), x_ref.shape[1]
        normed, squares = gained(x_ref[...], gain_ref, start)
        ssq = add(ssq, squares)
        rows = from_start(start, width)
        kvs = [add(kv, dot(normed, w_ref[rows, :])) for kv, w_ref in zip(kvs, wkv_refs)]
        if with_q[i]:
            q = add(q, dot(normed, wq_ref[rows, :]))
    outs[0][...] = q
    for c, kv in enumerate(kvs):
        outs[1][:, c * columns : (c + 1) * columns] = kv
    outs[2][...] = ssq


def more_blocks(xs, places, gain, wq, wkvs, state, with_q=None):
    tokens = xs[0].shape[0]
    operands = [*xs, *resident_in(gain, wq, *wkvs), *state]
    columns = len(wkvs) * wkvs[0].shape[1]
    shapes = ((tokens, wq.shape[1]), (tokens, columns), (tokens, HD))
    return pl.pallas_call(
        functools.partial(
            blocks_kernel, len(xs), len(wkvs), len(state), places, with_q or [True] * len(xs)
        ),
        out_shape=tuple(VMEM(s, f32) for s in shapes),
        in_specs=[vmem] * len(operands),
        out_specs=(vmem,) * 3,
        cost_estimate=cost(sum(2 * x.size * (wq.shape[1] + columns) for x in xs), sum(2 * x.size for x in xs)),
        compiler_params=params,
        name="more_blocks",
    )(*operands)


def last_kv_kernel(count, wkv_count, places, *refs):
    xs, refs = refs[:count], refs[count:]
    gain_ref, wkv_refs, refs = refs[0], refs[1 : 1 + wkv_count], refs[1 + wkv_count :]
    choose_ref, acckv_ref, ssq_ref, scale_ref, *pieces = refs
    me = lax.axis_index("head")
    columns = wkv_refs[0].shape[1]
    kvs = [acckv_ref[:, c * columns : (c + 1) * columns] for c in range(wkv_count)]
    ssq = ssq_ref[...]
    for i, x_ref in enumerate(xs):
        start, width = places[i](me), x_ref.shape[1]
        normed, squares = gained(x_ref[...], gain_ref, start)
        ssq = ssq + squares
        kvs = [kv + dot(normed, w_ref[from_start(start, width), :]) for kv, w_ref in zip(kvs, wkv_refs)]
    scale = lax.rsqrt(jnp.sum(ssq, axis=1, keepdims=True) / gain_ref.shape[1] + epsilon)
    scale_ref[...] = jnp.broadcast_to(scale, scale_ref.shape)
    kv = jnp.concatenate([(kv * scale).astype(bf16) for kv in kvs], axis=1)
    for i, piece in enumerate(pieces):
        piece[...] = dot_turned(choose_ref[i].astype(bf16), kv).astype(bf16)


def last_kv(xs, places, gain, wkvs, choose, acckv, ssq):
    tokens = xs[0].shape[0]
    columns = len(wkvs) * wkvs[0].shape[1]
    operands = [*xs, *resident_in(gain, *wkvs, choose), acckv, ssq]
    count = choose.shape[0]
    return pl.pallas_call(
        functools.partial(last_kv_kernel, len(xs), len(wkvs), places),
        out_shape=(VMEM((tokens, HD), f32),) + (VMEM((columns // KVH, tokens), bf16),) * count,
        in_specs=[vmem] * len(operands),
        out_specs=(vmem,) * (1 + count),
        cost_estimate=cost(sum(2 * x.size * columns for x in xs), sum(2 * x.size for x in xs)),
        compiler_params=params,
        name="last_keys_values",
    )(*operands)


def last_q_kernel(count, places, *refs):
    xs, rest = refs[:count], refs[count:]
    gain_ref, wq_ref, accq_ref, scale_ref, *rest = rest
    me = lax.axis_index("head")
    total = accq_ref[...]
    for i, x_ref in enumerate(xs):
        start, width = places[i](me), x_ref.shape[1]
        normed, _ = gained(x_ref[...], gain_ref, start)
        total = total + dot(normed, wq_ref[from_start(start, width), :])
    q = (total * scale_ref[:, 0:1]).astype(bf16)
    if len(rest) == 1:
        rest[0][...] = q
        return
    piece_ref, fresh_ref, q_ref, bundle_ref = rest
    q_ref[...] = q
    late = bundle_ref.shape[1] - HD
    last = lax.axis_index("section") == lax.axis_size("section") - 1
    sent = jnp.where(last, fresh_ref[:, -late:].astype(f32), q[:, -late:].astype(f32))
    bundle_ref[:, :late] = sent.astype(bf16)
    bundle_ref[:, late:] = piece_ref[...]


def last_q(xs, places, gain, wq, accq, scale, bundled=(), late=0):
    operands = [*xs, *resident_in(gain, wq), accq, scale, *bundled]
    tokens = xs[0].shape[0]
    out = [VMEM((tokens, wq.shape[1]), bf16)]
    if bundled:
        out.append(VMEM((tokens, late + HD), bf16))
    return pl.pallas_call(
        functools.partial(last_q_kernel, len(xs), places),
        out_shape=tuple(out),
        in_specs=[vmem] * len(operands),
        out_specs=(vmem,) * len(out),
        cost_estimate=cost(sum(2 * x.size * wq.shape[1] for x in xs), sum(2 * x.size for x in xs)),
        compiler_params=params,
        name="last_queries",
    )(*operands)


def openings_kernel(sections, doc_ref, first_ref, second_ref):
    tokens = first_ref.shape[0]
    for turn, out_ref in enumerate((first_ref, second_ref)):
        start = (sections - 1 + turn - lax.axis_index("section")) * tokens
        here = start + lax.broadcasted_iota(jnp.int32, out_ref.shape, 0)
        opened = jnp.zeros(out_ref.shape, jnp.int32)
        end = jnp.int32(0)
        for d in range(doc_ref.shape[0]):
            end = end + doc_ref[d]
            opened = jnp.where(end <= here, end, opened)
        out_ref[...] = opened


def openings(doc_lengths, tokens, sections):
    return pl.pallas_call(
        functools.partial(openings_kernel, sections),
        out_shape=(VMEM((tokens, HD), jnp.int32),) * 2,
        in_specs=[smem],
        out_specs=(vmem,) * 2,
        compiler_params=params,
        name="openings",
    )(doc_lengths)


def stacked_heads(q_ref, heads):
    return jnp.concatenate([q_ref[:, h * HD : (h + 1) * HD] for h in range(*heads)], axis=0)


def masked_scores(q, keys, opened_ref, query_start, key_start):
    tokens, count = opened_ref.shape[0], keys.shape[1]
    here = query_start + lax.broadcasted_iota(jnp.int32, (tokens, count), 0)
    there = key_start + lax.broadcasted_iota(jnp.int32, (tokens, count), 1)
    allowed = (there >= opened_ref[:, 0:1]) & (there <= here)
    scores = jnp.where(allowed[None], dot(q, keys).reshape(-1, tokens, count), masked_score)
    return scores.reshape(-1, count)


def mixed_and_sums(expon, values):
    both = jnp.concatenate([values, jnp.ones(values.shape, bf16)], axis=0)
    both = dot_turned(expon.astype(bf16), both)
    return both[:, :HD], both[:, HD:]


def put_together(me, pieces, flips, parts, gather):
    features = pieces[0].shape[0] // 2
    for flip, piece_ref in zip(flips, pieces):
        source = lax.bitwise_xor(me, jnp.int32(flip)) // parts
        piece = piece_ref[...].astype(f32)
        gather[0, rows_of(source, features), :] = piece[:features]
        gather[1, rows_of(source, features), :] = piece[features:]
    return gather[0].astype(bf16), gather[1].astype(bf16)


def peer_attend_kernel(sections, flips, parts, opened_ref, bundle_ref, x_ref, piece_ref, out_ref, gather):
    section = lax.axis_index("section")
    tokens, width = out_ref.shape
    start = (sections - 1 - section) * tokens
    pieces = [piece_ref, bundle_ref.at[:, width:]]
    keys, values = put_together(lax.axis_index("head"), pieces, flips, parts, gather)
    q = stacked_heads(bundle_ref, (0, width // HD))
    scores = masked_scores(q, keys, opened_ref, start, start)
    expon = jnp.exp2((scores - jnp.max(scores, axis=1, keepdims=True)) * score_scale)
    mixed, total = mixed_and_sums(expon, values)
    mixed = (mixed * (1.0 / total)).astype(bf16).astype(f32)
    for h in range(width // HD):
        columns = slice(h * HD, (h + 1) * HD)
        x = x_ref[:, x_ref.shape[1] - width + h * HD : x_ref.shape[1] - width + (h + 1) * HD].astype(f32)
        out = (x + mixed[h * tokens : (h + 1) * tokens]).astype(bf16).astype(f32)
        out = jnp.where(section == sections - 1, bundle_ref[:, columns].astype(f32), out)
        out_ref[:, columns] = out.astype(bf16)


def peer_attend(opened, bundle, x, piece, flips, parts, sections):
    tokens, width = x.shape[0], bundle.shape[1] - HD
    return pl.pallas_call(
        functools.partial(peer_attend_kernel, sections, flips, parts),
        out_shape=VMEM((tokens, width), bf16),
        in_specs=[vmem] * 4,
        out_specs=vmem,
        scratch_shapes=[VMEM((2, HD, tokens), f32)],
        cost_estimate=cost(1000, 1000),
        compiler_params=params,
        name="peer_attend",
    )(opened, bundle, x, piece)


def first_attend_kernel(sections, heads, flips, parts, opened_ref, q_ref, x_ref, fresh_ref, *refs):
    section = lax.axis_index("section")
    start = (sections - 1 - section) * q_ref.shape[0]
    if flips is None:
        keys_ref, values_ref, out_ref = refs
        keys, values = keys_ref[...], values_ref[...]
    else:
        pieces, (out_ref, keys_ref, values_ref, gather) = refs[: len(flips)], refs[len(flips) :]
        keys, values = put_together(lax.axis_index("head"), pieces, flips, parts, gather)
        keys_ref[...], values_ref[...] = keys, values
    tokens = q_ref.shape[0]
    scores = masked_scores(stacked_heads(q_ref, heads), keys, opened_ref, start, start)
    expon = jnp.exp2((scores - jnp.max(scores, axis=1, keepdims=True)) * score_scale)
    mixed, total = mixed_and_sums(expon, values)
    mixed = (mixed * (1.0 / total)).astype(bf16).astype(f32)
    for i, h in enumerate(range(*heads)):
        columns = slice(h * HD, (h + 1) * HD)
        out = (x_ref[:, columns].astype(f32) + mixed[i * tokens : (i + 1) * tokens]).astype(bf16)
        out = jnp.where(section == sections - 1, fresh_ref[:, columns].astype(f32), out.astype(f32))
        out_ref[:, i * HD : (i + 1) * HD] = out.astype(bf16)


def first_attend(opened, q, x, fresh, pieces, flips, parts, heads, sections):
    tokens = q.shape[0]
    out = (VMEM((tokens, (heads[1] - heads[0]) * HD), bf16),)
    scratch = []
    if flips is not None:
        out = out + (VMEM((HD, tokens), bf16),) * 2
        scratch = [VMEM((2, HD, tokens), f32)]
    operands = [opened, q, x, fresh, *pieces]
    return pl.pallas_call(
        functools.partial(first_attend_kernel, sections, heads, flips, parts),
        out_shape=out,
        in_specs=[vmem] * len(operands),
        out_specs=(vmem,) * len(out),
        scratch_shapes=scratch,
        cost_estimate=cost(10**10, 1000),
        compiler_params=params,
        name="first_attend",
    )(*operands)


def resident_kernel(sections, opened_ref, q_ref, keys_ref, values_ref, max_ref, sum_ref, mixed_ref):
    tokens = q_ref.shape[0]
    key_start = (sections - 1 - lax.axis_index("section")) * tokens
    q = stacked_heads(q_ref, (0, q_ref.shape[1] // HD))
    scores = masked_scores(q, keys_ref[...], opened_ref, key_start + tokens, key_start)
    top = jnp.max(scores, axis=1, keepdims=True)
    expon = jnp.exp2((scores - top) * score_scale)
    max_ref[...] = jnp.broadcast_to(top, max_ref.shape)
    mixed_ref[...], sum_ref[...] = mixed_and_sums(expon, values_ref[...])


def resident_attend(opened, q, keys, values, sections):
    rows = q.shape[0] * (q.shape[1] // HD)
    return pl.pallas_call(
        functools.partial(resident_kernel, sections),
        out_shape=(VMEM((rows, HD), f32),) * 3,
        in_specs=[vmem] * 4,
        out_specs=(vmem,) * 3,
        cost_estimate=cost(1000, 1000),
        compiler_params=params,
        name="resident_attend",
    )(opened, q, keys, values)


def second_attend_kernel(sections, flips, parts, x_count, opened_ref, q_ref, max_ref, sum_ref, mixed_ref, *refs):
    x_refs, refs = refs[:x_count], refs[x_count:]
    pieces, (out_ref, gather) = refs[: len(flips)], refs[len(flips) :]
    tokens, heads = q_ref.shape[0], q_ref.shape[1] // HD
    start = (sections - lax.axis_index("section")) * tokens
    keys, values = put_together(lax.axis_index("head"), pieces, flips, parts, gather)
    scores = masked_scores(stacked_heads(q_ref, (0, heads)), keys, opened_ref, start, start)
    top = jnp.maximum(jnp.max(scores, axis=1, keepdims=True), max_ref[...])
    expon = jnp.exp2((scores - top) * score_scale)
    shrink = jnp.exp2((max_ref[...] - top) * score_scale)
    mixed, total = mixed_and_sums(expon, values)
    total = total + shrink * sum_ref[...]
    mixed = mixed + shrink * mixed_ref[...]
    mixed = (mixed * (1.0 / total)).astype(bf16).astype(f32)
    where = [(x_ref, inside) for x_ref in x_refs for inside in range(0, x_ref.shape[1], HD)]
    for h, (x_ref, inside) in enumerate(where):
        out = x_ref[:, inside : inside + HD].astype(f32) + mixed[h * tokens : (h + 1) * tokens]
        out_ref[:, h * HD : (h + 1) * HD] = out.astype(bf16)


def second_attend(opened, q, xs, resident, pieces, flips, parts, sections):
    tokens = q.shape[0]
    operands = [opened, q, *resident, *xs, *pieces]
    return pl.pallas_call(
        functools.partial(second_attend_kernel, sections, flips, parts, len(xs)),
        out_shape=jax.ShapeDtypeStruct(q.shape, bf16),
        in_specs=[vmem] * len(operands),
        out_specs=vmem,
        scratch_shapes=[VMEM((2, HD, tokens), f32)],
        cost_estimate=cost(1000, 1000),
        compiler_params=params,
        name="second_attend",
    )(*operands)


def shards(entering, fresh_slice, norm_gain, w_query, w_key_value, doc_lengths):
    n = lax.axis_size("head")
    sections = lax.axis_size("section")
    own = entering[0]
    w_q, w_kv = w_query[0], w_key_value[0]
    tokens, width = own.shape
    heads = w_q.shape[1] // HD
    paired = n == 4
    parts = 2 if paired else 1
    flips = [0, 3] if paired else list(range(n))

    def moved(array, by, flip):
        pairs = [
            (s * n + h, ((s + by) % sections) * n + (h ^ flip)) for s in range(sections) for h in range(n)
        ]
        return lax.ppermute(array, ("section", "head"), pairs)

    def after(array, *others):
        return lax.optimization_barrier((array, *others))[0]

    def exchanged(xs, places, state):
        scale, *pieces = last_kv(xs, places, gain, wkvs, choose, state[1], state[2])
        received = [moved(piece, 0, flip) for piece, flip in zip(pieces[1:], flips[1:])]
        return scale, [pieces[0], *received], pieces

    def rest_of(array):
        every = lax.all_gather(array, "head", axis=0)
        me = lax.axis_index("head")
        return [lax.dynamic_index_in_dim(every, (me + k) % n, 0, False) for k in range(1, n)]

    def place(flip, offset=0):
        return lambda me: lax.bitwise_xor(me, jnp.int32(flip)) * width + offset

    following = [functools.partial(lambda k, me: lax.rem(me + k, jnp.int32(n)) * width, k) for k in range(n)]

    if paired:
        over = moved(own, 0, 3)
        beside = moved(own, 0, 1)
        w_kv_beside = moved(w_kv, 0, 1)
    accq, own, gain, wq, wkv, choose = load(own, norm_gain, w_q, w_kv, n, flips, parts)
    opened = openings(after(doc_lengths, accq), tokens, sections)
    if paired:
        wkvs = [wkv, w_kv_beside]
        over, *opened = lax.optimization_barrier((over, *opened))
        passed = moved(over, 0, 1)
        xs, places, with_q = [own, beside, over], [place(0), place(1), place(3)], [False, True, True]
        state = more_blocks(xs, places, gain, wq, wkvs, [accq], with_q)
        last, places = [passed], [place(2)]
    else:
        wkvs = [wkv]
        state = more_blocks([own], following[:1], gain, wq, wkvs, [accq], [False])
        last, places = rest_of(own), following[1:]
    scale, pieces, made = exchanged(last, places, state)
    part = heads // 2 if paired else heads
    split = part * HD
    if paired:
        q, bundle = last_q(last, places, gain, wq, state[0], scale, [made[0], fresh_slice], width - split)
        bundle = moved(bundle, 0, 3)
    else:
        (q,) = last_q(last, places, gain, wq, state[0], scale)
    sent, keys, values = first_attend(
        opened[0], q, own, fresh_slice, pieces, flips, parts, (0, part), sections
    )

    if paired:
        a1 = moved(sent, 1, 1)
        (sent,) = first_attend(
            opened[0], q, own, fresh_slice, [keys, values], None, parts, (part, heads), sections
        )
        b1 = moved(sent, 1, 1)
        bundle = after(bundle, sent)
        peers = peer_attend(opened[0], bundle, over, made[1], flips, parts, sections)
        b2 = moved(peers, 1, 1)
        a1 = after(a1, peers)
        a2 = moved(a1, 0, 3)
        a0 = moved(a1, 0, 1)
        state = more_blocks([a1], [place(1)], gain, wq, wkvs, [])
        b2, b1, *state = lax.optimization_barrier((b2, b1, *state))
        b3 = moved(b2, 0, 1)
        b0 = moved(b1, 0, 1)
        a3 = moved(a2, 0, 1)
        places = [place(0), place(2), *(place(flip, split) for flip in (2, 1, 3))]
        state = more_blocks([a0, a2, b2, b1, b3], places, gain, wq, wkvs, state)
        last, places = [a3, b0], [place(3), place(0, split)]
        mine = [a0, b0]
    else:
        mine = [moved(sent, 1, 0)]
        state = more_blocks(mine, following[:1], gain, wq, wkvs, [])
        last, places = rest_of(mine[0]), following[1:]
    scale, pieces, _ = exchanged(last, places, state)
    (q,) = last_q(last, places, gain, wq, state[0], scale)
    resident = resident_attend(opened[1], q, keys, values, sections)
    return second_attend(opened[1], q, mine, resident, pieces, flips, parts, sections)[None]


def solution(mesh):
    placed = (
        P("section", None, "head"),
        P(None, "head"),
        P("section", None),
        P("section", None, "head"),
        P("section", None, "head"),
        P(),
    )
    return jax.shard_map(
        shards, mesh=mesh, in_specs=placed, out_specs=P("section", None, "head"), check_vma=False
    )
```

```python
import functools
import math

import jax
import jax.numpy as jnp
from jax import lax
from jax.experimental import pallas as pl
from jax.experimental.pallas import tpu as pltpu
from jax.sharding import PartitionSpec as P

HD = 128
KVH = 4
GROUP = 8

epsilon = 1e-05
score_scale = math.log2(math.e) / math.sqrt(HD)
masked_score = -1e30

VMEM = pltpu.VMEM
f32 = jnp.float32
bf16 = jnp.bfloat16
vmem = pl.BlockSpec(memory_space=VMEM)
smem = pl.BlockSpec(memory_space=pltpu.SMEM)
in_hbm = pl.BlockSpec(memory_space=pltpu.HBM)
params = pltpu.CompilerParams(vmem_limit_bytes=16 * 1024 * 1024)


def resident_in(*arrays):
    return [pltpu.with_memory_space_constraint(a, VMEM) for a in arrays]


def cost(flops, moved):
    return pl.CostEstimate(flops=flops, bytes_accessed=moved, transcendentals=0)


def rows_of(block, width):
    return pl.ds(pl.multiple_of(block * width, width), width)


def from_start(start, width):
    return pl.ds(pl.multiple_of(start, HD), width)


def dot(a, b):
    return jnp.dot(a, b, preferred_element_type=f32)


def dot_turned(a, b):
    return lax.dot_general(a, b, (((1,), (1,)), ((), ())), preferred_element_type=f32)


def gained(x, gain_ref, start):
    width = x.shape[1]
    wide = x.astype(f32)
    squares = wide * wide
    ssq = squares[:, :HD]
    for c in range(HD, width, HD):
        ssq = ssq + squares[:, c : c + HD]
    return (wide * gain_ref[:, from_start(start, width)]).astype(bf16), ssq


def choose_rows(choose_ref, me, n, flips, parts):
    size, columns = choose_ref.shape[1], choose_ref.shape[2] // parts
    features = size // (2 * parts)
    shape = (features, choose_ref.shape[2])
    row = lax.broadcasted_iota(jnp.int32, shape, 0)
    col = lax.broadcasted_iota(jnp.int32, shape, 1)
    offset = col - row * (2 * KVH)
    for i, flip in enumerate(flips):
        group = lax.bitwise_xor(me, jnp.int32(flip)) * KVH // n
        for which in range(2):
            for core in range(parts):
                whose = jnp.where(lax.rem(me, jnp.int32(parts)) == core, 0, 1)
                wanted = whose * columns + group * 2 + which
                first = (which * parts + core) * features
                choose_ref[i, first : first + features, :] = jnp.where(offset == wanted, 1.0, 0.0)


def load_kernel(
    n, flips, parts, x_hbm, gain_hbm, wq_hbm, wkv_hbm, accq_ref, x_ref, gain_ref, wq_ref, wkv_ref, choose_ref, sems
):
    width = x_hbm.shape[1]
    me = lax.axis_index("head")

    def part(step):
        rows = rows_of(lax.rem(me + step, n), width)
        return pltpu.make_async_copy(wq_hbm.at[rows], wq_ref.at[rows], sems.at[step])

    small = (
        pltpu.make_async_copy(x_hbm, x_ref, sems.at[n]),
        pltpu.make_async_copy(gain_hbm, gain_ref, sems.at[n + 1]),
    )
    keys_values = pltpu.make_async_copy(wkv_hbm, wkv_ref, sems.at[n + 2])
    for copy in small:
        copy.start()
    for step in range(n):
        part(step).start()
    keys_values.start()
    choose_rows(choose_ref, me, n, flips, parts)
    for copy in small:
        copy.wait()
    normed, _ = gained(x_ref[...], gain_ref, me * width)
    part(0).wait()
    accq_ref[...] = dot(normed, wq_ref[rows_of(me, width), :])
    for step in range(1, n):
        part(step).wait()
    keys_values.wait()


def load(x, gain, wq, wkv, n, flips, parts):
    tokens, width = x.shape
    columns = wkv.shape[1]
    operands = [pltpu.with_memory_space_constraint(a, pltpu.HBM) for a in (x, gain, wq, wkv)]
    return pl.pallas_call(
        functools.partial(load_kernel, n, flips, parts),
        out_shape=(
            VMEM((tokens, wq.shape[1]), f32),
            VMEM(x.shape, bf16),
            VMEM(gain.shape, f32),
            VMEM(wq.shape, bf16),
            VMEM(wkv.shape, bf16),
            VMEM((len(flips), parts * columns // KVH, parts * columns), f32),
        ),
        in_specs=[in_hbm] * 4,
        out_specs=(vmem,) * 6,
        scratch_shapes=[pltpu.SemaphoreType.DMA((n + 3,))],
        cost_estimate=cost(10**11, 10**9),
        compiler_params=params,
        name="load_and_own_queries",
    )(*operands)


def blocks_kernel(count, wkv_count, carried, places, with_q, *refs):
    xs, refs = refs[:count], refs[count:]
    gain_ref, wq_ref = refs[:2]
    wkv_refs, refs = refs[2 : 2 + wkv_count], refs[2 + wkv_count :]
    old, outs = refs[:carried], refs[carried:]
    me = lax.axis_index("head")
    columns = wkv_refs[0].shape[1]
    q = old[0][...] if carried >= 1 else None
    kvs = [old[1][:, c * columns : (c + 1) * columns] if carried == 3 else None for c in range(wkv_count)]
    ssq = old[2][...] if carried == 3 else None

    def add(total, term):
        return term if total is None else total + term

    for i, x_ref in enumerate(xs):
        start, width = places[i](me), x_ref.shape[1]
        normed, squares = gained(x_ref[...], gain_ref, start)
        ssq = add(ssq, squares)
        rows = from_start(start, width)
        kvs = [add(kv, dot(normed, w_ref[rows, :])) for kv, w_ref in zip(kvs, wkv_refs)]
        if with_q[i]:
            q = add(q, dot(normed, wq_ref[rows, :]))
    outs[0][...] = q
    for c, kv in enumerate(kvs):
        outs[1][:, c * columns : (c + 1) * columns] = kv
    outs[2][...] = ssq


def more_blocks(xs, places, gain, wq, wkvs, state, with_q=None):
    tokens = xs[0].shape[0]
    operands = [*xs, *resident_in(gain, wq, *wkvs), *state]
    columns = len(wkvs) * wkvs[0].shape[1]
    shapes = ((tokens, wq.shape[1]), (tokens, columns), (tokens, HD))
    return pl.pallas_call(
        functools.partial(
            blocks_kernel, len(xs), len(wkvs), len(state), places, with_q or [True] * len(xs)
        ),
        out_shape=tuple(VMEM(s, f32) for s in shapes),
        in_specs=[vmem] * len(operands),
        out_specs=(vmem,) * 3,
        cost_estimate=cost(sum(2 * x.size * (wq.shape[1] + columns) for x in xs), sum(2 * x.size for x in xs)),
        compiler_params=params,
        name="more_blocks",
    )(*operands)


def last_kv_kernel(count, wkv_count, places, *refs):
    xs, refs = refs[:count], refs[count:]
    gain_ref, wkv_refs, refs = refs[0], refs[1 : 1 + wkv_count], refs[1 + wkv_count :]
    choose_ref, acckv_ref, ssq_ref, scale_ref, *pieces = refs
    me = lax.axis_index("head")
    columns = wkv_refs[0].shape[1]
    kvs = [acckv_ref[:, c * columns : (c + 1) * columns] for c in range(wkv_count)]
    ssq = ssq_ref[...]
    for i, x_ref in enumerate(xs):
        start, width = places[i](me), x_ref.shape[1]
        normed, squares = gained(x_ref[...], gain_ref, start)
        ssq = ssq + squares
        kvs = [kv + dot(normed, w_ref[from_start(start, width), :]) for kv, w_ref in zip(kvs, wkv_refs)]
    scale = lax.rsqrt(jnp.sum(ssq, axis=1, keepdims=True) / gain_ref.shape[1] + epsilon)
    scale_ref[...] = jnp.broadcast_to(scale, scale_ref.shape)
    kv = jnp.concatenate([(kv * scale).astype(bf16) for kv in kvs], axis=1)
    for i, piece in enumerate(pieces):
        piece[...] = dot_turned(choose_ref[i].astype(bf16), kv).astype(bf16)


def last_kv(xs, places, gain, wkvs, choose, acckv, ssq):
    tokens = xs[0].shape[0]
    columns = len(wkvs) * wkvs[0].shape[1]
    operands = [*xs, *resident_in(gain, *wkvs, choose), acckv, ssq]
    count = choose.shape[0]
    return pl.pallas_call(
        functools.partial(last_kv_kernel, len(xs), len(wkvs), places),
        out_shape=(VMEM((tokens, HD), f32),) + (VMEM((columns // KVH, tokens), bf16),) * count,
        in_specs=[vmem] * len(operands),
        out_specs=(vmem,) * (1 + count),
        cost_estimate=cost(sum(2 * x.size * columns for x in xs), sum(2 * x.size for x in xs)),
        compiler_params=params,
        name="last_keys_values",
    )(*operands)


def last_q_kernel(count, places, *refs):
    xs, rest = refs[:count], refs[count:]
    gain_ref, wq_ref, accq_ref, scale_ref, *rest = rest
    me = lax.axis_index("head")
    total = accq_ref[...]
    for i, x_ref in enumerate(xs):
        start, width = places[i](me), x_ref.shape[1]
        normed, _ = gained(x_ref[...], gain_ref, start)
        total = total + dot(normed, wq_ref[from_start(start, width), :])
    q = (total * scale_ref[:, 0:1]).astype(bf16)
    if len(rest) == 1:
        rest[0][...] = q
        return
    piece_ref, fresh_ref, q_ref, bundle_ref = rest
    q_ref[...] = q
    late = bundle_ref.shape[1] - HD
    last = lax.axis_index("section") == lax.axis_size("section") - 1
    sent = jnp.where(last, fresh_ref[:, -late:].astype(f32), q[:, -late:].astype(f32))
    bundle_ref[:, :late] = sent.astype(bf16)
    bundle_ref[:, late:] = piece_ref[...]


def last_q(xs, places, gain, wq, accq, scale, bundled=(), late=0):
    operands = [*xs, *resident_in(gain, wq), accq, scale, *bundled]
    tokens = xs[0].shape[0]
    out = [VMEM((tokens, wq.shape[1]), bf16)]
    if bundled:
        out.append(VMEM((tokens, late + HD), bf16))
    return pl.pallas_call(
        functools.partial(last_q_kernel, len(xs), places),
        out_shape=tuple(out),
        in_specs=[vmem] * len(operands),
        out_specs=(vmem,) * len(out),
        cost_estimate=cost(sum(2 * x.size * wq.shape[1] for x in xs), sum(2 * x.size for x in xs)),
        compiler_params=params,
        name="last_queries",
    )(*operands)


def openings_kernel(sections, doc_ref, first_ref, second_ref):
    tokens = first_ref.shape[0]
    for turn, out_ref in enumerate((first_ref, second_ref)):
        start = (sections - 1 + turn - lax.axis_index("section")) * tokens
        here = start + lax.broadcasted_iota(jnp.int32, out_ref.shape, 0)
        opened = jnp.zeros(out_ref.shape, jnp.int32)
        end = jnp.int32(0)
        for d in range(doc_ref.shape[0]):
            end = end + doc_ref[d]
            opened = jnp.where(end <= here, end, opened)
        out_ref[...] = opened


def openings(doc_lengths, tokens, sections):
    return pl.pallas_call(
        functools.partial(openings_kernel, sections),
        out_shape=(VMEM((tokens, HD), jnp.int32),) * 2,
        in_specs=[smem],
        out_specs=(vmem,) * 2,
        compiler_params=params,
        name="openings",
    )(doc_lengths)


def stacked_heads(q_ref, heads):
    return jnp.concatenate([q_ref[:, h * HD : (h + 1) * HD] for h in range(*heads)], axis=0)


def masked_scores(q, keys, opened_ref, query_start, key_start):
    tokens, count = opened_ref.shape[0], keys.shape[1]
    here = query_start + lax.broadcasted_iota(jnp.int32, (tokens, count), 0)
    there = key_start + lax.broadcasted_iota(jnp.int32, (tokens, count), 1)
    allowed = (there >= opened_ref[:, 0:1]) & (there <= here)
    scores = jnp.where(allowed[None], dot(q, keys).reshape(-1, tokens, count), masked_score)
    return scores.reshape(-1, count)


def mixed_and_sums(expon, values):
    both = jnp.concatenate([values, jnp.ones(values.shape, bf16)], axis=0)
    both = dot_turned(expon.astype(bf16), both)
    return both[:, :HD], both[:, HD:]


def put_together(me, pieces, flips, parts, gather):
    features = pieces[0].shape[0] // 2
    for flip, piece_ref in zip(flips, pieces):
        source = lax.bitwise_xor(me, jnp.int32(flip)) // parts
        piece = piece_ref[...].astype(f32)
        gather[0, rows_of(source, features), :] = piece[:features]
        gather[1, rows_of(source, features), :] = piece[features:]
    return gather[0].astype(bf16), gather[1].astype(bf16)


def peer_attend_kernel(sections, flips, parts, opened_ref, bundle_ref, x_ref, piece_ref, out_ref, gather):
    section = lax.axis_index("section")
    tokens, width = out_ref.shape
    start = (sections - 1 - section) * tokens
    pieces = [piece_ref, bundle_ref.at[:, width:]]
    keys, values = put_together(lax.axis_index("head"), pieces, flips, parts, gather)
    q = stacked_heads(bundle_ref, (0, width // HD))
    scores = masked_scores(q, keys, opened_ref, start, start)
    expon = jnp.exp2((scores - jnp.max(scores, axis=1, keepdims=True)) * score_scale)
    mixed, total = mixed_and_sums(expon, values)
    mixed = (mixed * (1.0 / total)).astype(bf16).astype(f32)
    for h in range(width // HD):
        columns = slice(h * HD, (h + 1) * HD)
        x = x_ref[:, x_ref.shape[1] - width + h * HD : x_ref.shape[1] - width + (h + 1) * HD].astype(f32)
        out = (x + mixed[h * tokens : (h + 1) * tokens]).astype(bf16).astype(f32)
        out = jnp.where(section == sections - 1, bundle_ref[:, columns].astype(f32), out)
        out_ref[:, columns] = out.astype(bf16)


def peer_attend(opened, bundle, x, piece, flips, parts, sections):
    tokens, width = x.shape[0], bundle.shape[1] - HD
    return pl.pallas_call(
        functools.partial(peer_attend_kernel, sections, flips, parts),
        out_shape=VMEM((tokens, width), bf16),
        in_specs=[vmem] * 4,
        out_specs=vmem,
        scratch_shapes=[VMEM((2, HD, tokens), f32)],
        cost_estimate=cost(1000, 1000),
        compiler_params=params,
        name="peer_attend",
    )(opened, bundle, x, piece)


def first_attend_kernel(sections, heads, flips, parts, opened_ref, q_ref, x_ref, fresh_ref, *refs):
    section = lax.axis_index("section")
    start = (sections - 1 - section) * q_ref.shape[0]
    if flips is None:
        keys_ref, values_ref, out_ref = refs
        keys, values = keys_ref[...], values_ref[...]
    else:
        pieces, (out_ref, keys_ref, values_ref, gather) = refs[: len(flips)], refs[len(flips) :]
        keys, values = put_together(lax.axis_index("head"), pieces, flips, parts, gather)
        keys_ref[...], values_ref[...] = keys, values
    tokens = q_ref.shape[0]
    scores = masked_scores(stacked_heads(q_ref, heads), keys, opened_ref, start, start)
    expon = jnp.exp2((scores - jnp.max(scores, axis=1, keepdims=True)) * score_scale)
    mixed, total = mixed_and_sums(expon, values)
    mixed = (mixed * (1.0 / total)).astype(bf16).astype(f32)
    for i, h in enumerate(range(*heads)):
        columns = slice(h * HD, (h + 1) * HD)
        out = (x_ref[:, columns].astype(f32) + mixed[i * tokens : (i + 1) * tokens]).astype(bf16)
        out = jnp.where(section == sections - 1, fresh_ref[:, columns].astype(f32), out.astype(f32))
        out_ref[:, i * HD : (i + 1) * HD] = out.astype(bf16)


def first_attend(opened, q, x, fresh, pieces, flips, parts, heads, sections):
    tokens = q.shape[0]
    out = (VMEM((tokens, (heads[1] - heads[0]) * HD), bf16),)
    scratch = []
    if flips is not None:
        out = out + (VMEM((HD, tokens), bf16),) * 2
        scratch = [VMEM((2, HD, tokens), f32)]
    operands = [opened, q, x, fresh, *pieces]
    return pl.pallas_call(
        functools.partial(first_attend_kernel, sections, heads, flips, parts),
        out_shape=out,
        in_specs=[vmem] * len(operands),
        out_specs=(vmem,) * len(out),
        scratch_shapes=scratch,
        cost_estimate=cost(10**10, 1000),
        compiler_params=params,
        name="first_attend",
    )(*operands)


def resident_kernel(sections, opened_ref, q_ref, keys_ref, values_ref, max_ref, sum_ref, mixed_ref):
    tokens = q_ref.shape[0]
    key_start = (sections - 1 - lax.axis_index("section")) * tokens
    q = stacked_heads(q_ref, (0, q_ref.shape[1] // HD))
    scores = masked_scores(q, keys_ref[...], opened_ref, key_start + tokens, key_start)
    top = jnp.max(scores, axis=1, keepdims=True)
    expon = jnp.exp2((scores - top) * score_scale)
    max_ref[...] = jnp.broadcast_to(top, max_ref.shape)
    mixed_ref[...], sum_ref[...] = mixed_and_sums(expon, values_ref[...])


def resident_attend(opened, q, keys, values, sections):
    rows = q.shape[0] * (q.shape[1] // HD)
    return pl.pallas_call(
        functools.partial(resident_kernel, sections),
        out_shape=(VMEM((rows, HD), f32),) * 3,
        in_specs=[vmem] * 4,
        out_specs=(vmem,) * 3,
        cost_estimate=cost(1000, 1000),
        compiler_params=params,
        name="resident_attend",
    )(opened, q, keys, values)


def second_attend_kernel(sections, flips, parts, x_count, opened_ref, q_ref, max_ref, sum_ref, mixed_ref, *refs):
    x_refs, refs = refs[:x_count], refs[x_count:]
    pieces, (out_ref, gather) = refs[: len(flips)], refs[len(flips) :]
    tokens, heads = q_ref.shape[0], q_ref.shape[1] // HD
    start = (sections - lax.axis_index("section")) * tokens
    keys, values = put_together(lax.axis_index("head"), pieces, flips, parts, gather)
    scores = masked_scores(stacked_heads(q_ref, (0, heads)), keys, opened_ref, start, start)
    top = jnp.maximum(jnp.max(scores, axis=1, keepdims=True), max_ref[...])
    expon = jnp.exp2((scores - top) * score_scale)
    shrink = jnp.exp2((max_ref[...] - top) * score_scale)
    mixed, total = mixed_and_sums(expon, values)
    total = total + shrink * sum_ref[...]
    mixed = mixed + shrink * mixed_ref[...]
    mixed = (mixed * (1.0 / total)).astype(bf16).astype(f32)
    where = [(x_ref, inside) for x_ref in x_refs for inside in range(0, x_ref.shape[1], HD)]
    for h, (x_ref, inside) in enumerate(where):
        out = x_ref[:, inside : inside + HD].astype(f32) + mixed[h * tokens : (h + 1) * tokens]
        out_ref[:, h * HD : (h + 1) * HD] = out.astype(bf16)


def second_attend(opened, q, xs, resident, pieces, flips, parts, sections):
    tokens = q.shape[0]
    operands = [opened, q, *resident, *xs, *pieces]
    return pl.pallas_call(
        functools.partial(second_attend_kernel, sections, flips, parts, len(xs)),
        out_shape=jax.ShapeDtypeStruct(q.shape, bf16),
        in_specs=[vmem] * len(operands),
        out_specs=vmem,
        scratch_shapes=[VMEM((2, HD, tokens), f32)],
        cost_estimate=cost(1000, 1000),
        compiler_params=params,
        name="second_attend",
    )(*operands)


def shards(entering, fresh_slice, norm_gain, w_query, w_key_value, doc_lengths):
    n = lax.axis_size("head")
    sections = lax.axis_size("section")
    own = entering[0]
    w_q, w_kv = w_query[0], w_key_value[0]
    tokens, width = own.shape
    heads = w_q.shape[1] // HD
    paired = n == 4
    parts = 2 if paired else 1
    flips = [0, 3] if paired else list(range(n))

    def moved(array, by, flip):
        pairs = [
            (s * n + h, ((s + by) % sections) * n + (h ^ flip)) for s in range(sections) for h in range(n)
        ]
        return lax.ppermute(array, ("section", "head"), pairs)

    def after(array, *others):
        return lax.optimization_barrier((array, *others))[0]

    def exchanged(xs, places, state):
        scale, *pieces = last_kv(xs, places, gain, wkvs, choose, state[1], state[2])
        received = [moved(piece, 0, flip) for piece, flip in zip(pieces[1:], flips[1:])]
        return scale, [pieces[0], *received], pieces

    def rest_of(array):
        every = lax.all_gather(array, "head", axis=0)
        me = lax.axis_index("head")
        return [lax.dynamic_index_in_dim(every, (me + k) % n, 0, False) for k in range(1, n)]

    def place(flip, offset=0):
        return lambda me: lax.bitwise_xor(me, jnp.int32(flip)) * width + offset

    following = [functools.partial(lambda k, me: lax.rem(me + k, jnp.int32(n)) * width, k) for k in range(n)]

    if paired:
        over = moved(own, 0, 3)
        beside = moved(own, 0, 1)
        w_kv_beside = moved(w_kv, 0, 1)
    accq, own, gain, wq, wkv, choose = load(own, norm_gain, w_q, w_kv, n, flips, parts)
    opened = openings(after(doc_lengths, accq), tokens, sections)
    if paired:
        wkvs = [wkv, w_kv_beside]
        over, *opened = lax.optimization_barrier((over, *opened))
        passed = moved(over, 0, 1)
        xs, places, with_q = [own, beside, over], [place(0), place(1), place(3)], [False, True, True]
        state = more_blocks(xs, places, gain, wq, wkvs, [accq], with_q)
        last, places = [passed], [place(2)]
    else:
        wkvs = [wkv]
        state = more_blocks([own], following[:1], gain, wq, wkvs, [accq], [False])
        last, places = rest_of(own), following[1:]
    scale, pieces, made = exchanged(last, places, state)
    part = heads // 2 if paired else heads
    split = part * HD
    if paired:
        q, bundle = last_q(last, places, gain, wq, state[0], scale, [made[0], fresh_slice], width - split)
        bundle = moved(bundle, 0, 3)
    else:
        (q,) = last_q(last, places, gain, wq, state[0], scale)
    sent, keys, values = first_attend(
        opened[0], q, own, fresh_slice, pieces, flips, parts, (0, part), sections
    )

    if paired:
        a1 = moved(sent, 1, 1)
        (sent,) = first_attend(
            opened[0], q, own, fresh_slice, [keys, values], None, parts, (part, heads), sections
        )
        b1 = moved(sent, 1, 1)
        bundle = after(bundle, sent)
        peers = peer_attend(opened[0], bundle, over, made[1], flips, parts, sections)
        b2 = moved(peers, 1, 1)
        a1 = after(a1, peers)
        a2 = moved(a1, 0, 3)
        a0 = moved(a1, 0, 1)
        state = more_blocks([a1], [place(1)], gain, wq, wkvs, [])
        b1, *state = lax.optimization_barrier((b1, *state))
        b0 = moved(b1, 0, 1)
        state = more_blocks([b1], [place(1, split)], gain, wq, wkvs, state)
        b2, *state = lax.optimization_barrier((b2, *state))
        b3 = moved(b2, 0, 1)
        a3 = moved(a2, 0, 1)
        state = more_blocks([a0, a2, b2], [place(0), place(2), place(2, split)], gain, wq, wkvs, state)
        last, places = [a3, b0, b3], [place(3), place(0, split), place(3, split)]
        mine = [a0, b0]
    else:
        mine = [moved(sent, 1, 0)]
        state = more_blocks(mine, following[:1], gain, wq, wkvs, [])
        last, places = rest_of(mine[0]), following[1:]
    scale, pieces, _ = exchanged(last, places, state)
    (q,) = last_q(last, places, gain, wq, state[0], scale)
    resident = resident_attend(opened[1], q, keys, values, sections)
    return second_attend(opened[1], q, mine, resident, pieces, flips, parts, sections)[None]


def solution(mesh):
    placed = (
        P("section", None, "head"),
        P(None, "head"),
        P("section", None),
        P("section", None, "head"),
        P("section", None, "head"),
        P(),
    )
    return jax.shard_map(
        shards, mesh=mesh, in_specs=placed, out_specs=P("section", None, "head"), check_vma=False
    )
```

```python
import functools
import math

import jax
import jax.numpy as jnp
from jax import lax
from jax.experimental import pallas as pl
from jax.experimental.pallas import tpu as pltpu
from jax.sharding import PartitionSpec as P

HD = 128
KVH = 4
GROUP = 8

epsilon = 1e-05
score_scale = math.log2(math.e) / math.sqrt(HD)
masked_score = -1e30

VMEM = pltpu.VMEM
f32 = jnp.float32
bf16 = jnp.bfloat16
vmem = pl.BlockSpec(memory_space=VMEM)
smem = pl.BlockSpec(memory_space=pltpu.SMEM)
in_hbm = pl.BlockSpec(memory_space=pltpu.HBM)
params = pltpu.CompilerParams(vmem_limit_bytes=16 * 1024 * 1024)


def resident_in(*arrays):
    return [pltpu.with_memory_space_constraint(a, VMEM) for a in arrays]


def cost(flops, moved):
    return pl.CostEstimate(flops=flops, bytes_accessed=moved, transcendentals=0)


def rows_of(block, width):
    return pl.ds(pl.multiple_of(block * width, width), width)


def from_start(start, width):
    return pl.ds(pl.multiple_of(start, HD), width)


def dot(a, b):
    return jnp.dot(a, b, preferred_element_type=f32)


def dot_turned(a, b):
    return lax.dot_general(a, b, (((1,), (1,)), ((), ())), preferred_element_type=f32)


def gained(x, gain_ref, start):
    width = x.shape[1]
    wide = x.astype(f32)
    squares = wide * wide
    ssq = squares[:, :HD]
    for c in range(HD, width, HD):
        ssq = ssq + squares[:, c : c + HD]
    return (wide * gain_ref[:, from_start(start, width)]).astype(bf16), ssq


def choose_rows(choose_ref, me, n, flips, parts):
    size, columns = choose_ref.shape[1], choose_ref.shape[2] // parts
    features = size // (2 * parts)
    shape = (features, choose_ref.shape[2])
    row = lax.broadcasted_iota(jnp.int32, shape, 0)
    col = lax.broadcasted_iota(jnp.int32, shape, 1)
    offset = col - row * (2 * KVH)
    for i, flip in enumerate(flips):
        group = lax.bitwise_xor(me, jnp.int32(flip)) * KVH // n
        for which in range(2):
            for core in range(parts):
                whose = jnp.where(lax.rem(me, jnp.int32(parts)) == core, 0, 1)
                wanted = whose * columns + group * 2 + which
                first = (which * parts + core) * features
                choose_ref[i, first : first + features, :] = jnp.where(offset == wanted, 1.0, 0.0)


def paired_selection(me, columns):
    row = lax.broadcasted_iota(jnp.int32, (columns, columns // 2), 0)
    col = lax.broadcasted_iota(jnp.int32, (columns, columns // 2), 1)
    quarter = columns // 8
    piece, which = col // (2 * quarter), col // quarter % 2
    group = lax.bitwise_xor(3 * piece, jnp.broadcast_to(me, col.shape))
    return jnp.where(row == col % quarter * (2 * KVH) + group * 2 + which, 1.0, 0.0).astype(bf16)


def select_into(out_ref, wkv_ref, me):
    select = paired_selection(me, wkv_ref.shape[1])
    size = wkv_ref.shape[0] // 4
    for first in range(0, wkv_ref.shape[0], size):
        out_ref[first : first + size, :] = dot(wkv_ref[first : first + size, :], select).astype(bf16)


def select_kernel(wkv_ref, out_ref):
    select_into(out_ref, wkv_ref, lax.axis_index("head"))


def selected(wkv):
    return pl.pallas_call(
        select_kernel,
        out_shape=VMEM((wkv.shape[0], wkv.shape[1] // 2), bf16),
        in_specs=[vmem],
        out_specs=vmem,
        cost_estimate=cost(1000, 1000),
        compiler_params=params,
        name="selected_columns",
    )(*resident_in(wkv))


def paired_turn(me, side):
    row = lax.broadcasted_iota(jnp.int32, (side, side), 0)
    col = lax.broadcasted_iota(jnp.int32, (side, side), 1)
    quarter = side // 8
    piece, which, core = row // (4 * quarter), row // (2 * quarter) % 2, row // quarter % 2
    whose = lax.bitwise_xor(core, jnp.broadcast_to(lax.rem(me, jnp.int32(2)), core.shape))
    wanted = whose * (4 * quarter) + piece * (2 * quarter) + which * quarter + row % quarter
    return jnp.where(col == wanted, 1.0, 0.0)


def load_kernel(
    n, flips, parts, x_hbm, gain_hbm, wq_hbm, wkv_hbm, accq_ref, x_ref, gain_ref, wq_ref, choose_ref, *rest
):
    selected_ref, wkv_ref, sems = rest if parts == 2 else (None, *rest)
    width = x_hbm.shape[1]
    me = lax.axis_index("head")

    def part(step):
        rows = rows_of(lax.rem(me + step, n), width)
        return pltpu.make_async_copy(wq_hbm.at[rows], wq_ref.at[rows], sems.at[step])

    small = (
        pltpu.make_async_copy(x_hbm, x_ref, sems.at[n]),
        pltpu.make_async_copy(gain_hbm, gain_ref, sems.at[n + 1]),
    )
    keys_values = pltpu.make_async_copy(wkv_hbm, wkv_ref, sems.at[n + 2])
    for copy in small:
        copy.start()
    keys_values.start()
    for step in range(n):
        part(step).start()
    columns = wkv_hbm.shape[1]
    if parts == 2:
        choose_ref[0] = paired_turn(me, columns)
    else:
        choose_rows(choose_ref, me, n, flips, parts)
    for copy in small:
        copy.wait()
    normed, _ = gained(x_ref[...].astype(f32), gain_ref, me * width)
    keys_values.wait()
    if parts == 2:
        select_into(selected_ref, wkv_ref, me)
    part(0).wait()
    accq_ref[...] = dot(normed, wq_ref[rows_of(me, width), :])
    for step in range(1, n):
        part(step).wait()


def load(x, gain, wq, wkv, n, flips, parts):
    tokens, width = x.shape
    columns = wkv.shape[1]
    operands = [pltpu.with_memory_space_constraint(a, pltpu.HBM) for a in (x, gain, wq, wkv)]
    return pl.pallas_call(
        functools.partial(load_kernel, n, flips, parts),
        out_shape=(
            VMEM((tokens, wq.shape[1]), f32),
            VMEM(x.shape, bf16),
            VMEM(gain.shape, f32),
            VMEM(wq.shape, bf16),
            VMEM((1, columns, columns) if parts == 2 else (len(flips), columns // KVH, columns), f32),
        )
        + (VMEM((wkv.shape[0], columns // parts), bf16),),
        in_specs=[in_hbm] * 4,
        out_specs=(vmem,) * 6,
        scratch_shapes=[VMEM(wkv.shape, bf16)] * (parts - 1) + [pltpu.SemaphoreType.DMA((n + 3,))],
        cost_estimate=cost(10**11, 10**9),
        compiler_params=params,
        name="load_and_own_queries",
    )(*operands)


def blocks_kernel(count, wkv_count, carried, places, with_q, *refs):
    xs, refs = refs[:count], refs[count:]
    gain_ref, wq_ref = refs[:2]
    wkv_refs, refs = refs[2 : 2 + wkv_count], refs[2 + wkv_count :]
    old, outs = refs[:carried], refs[carried:]
    me = lax.axis_index("head")
    columns = wkv_refs[0].shape[1]
    q = old[0][...] if carried >= 1 else None
    kvs = [old[1][:, c * columns : (c + 1) * columns] if carried == 3 else None for c in range(wkv_count)]
    ssq = old[2][...] if carried == 3 else None

    def add(total, term):
        return term if total is None else total + term

    for i, x_ref in enumerate(xs):
        start, width = places[i](me), x_ref.shape[1]
        normed, squares = gained(x_ref[...], gain_ref, start)
        ssq = add(ssq, squares)
        rows = from_start(start, width)
        kvs = [add(kv, dot(normed, w_ref[rows, :])) for kv, w_ref in zip(kvs, wkv_refs)]
        if with_q[i]:
            q = add(q, dot(normed, wq_ref[rows, :]))
    outs[0][...] = q
    for c, kv in enumerate(kvs):
        outs[1][:, c * columns : (c + 1) * columns] = kv
    outs[2][...] = ssq


def more_blocks(xs, places, gain, wq, wkvs, state, with_q=None):
    tokens = xs[0].shape[0]
    operands = [*xs, *resident_in(gain, wq, *wkvs), *state]
    columns = len(wkvs) * wkvs[0].shape[1]
    shapes = ((tokens, wq.shape[1]), (tokens, columns), (tokens, HD))
    return pl.pallas_call(
        functools.partial(
            blocks_kernel, len(xs), len(wkvs), len(state), places, with_q or [True] * len(xs)
        ),
        out_shape=tuple(VMEM(s, f32) for s in shapes),
        in_specs=[vmem] * len(operands),
        out_specs=(vmem,) * 3,
        cost_estimate=cost(sum(2 * x.size * (wq.shape[1] + columns) for x in xs), sum(2 * x.size for x in xs)),
        compiler_params=params,
        name="more_blocks",
    )(*operands)


def last_kv_kernel(count, wkv_count, places, *refs):
    xs, refs = refs[:count], refs[count:]
    gain_ref, wkv_refs, refs = refs[0], refs[1 : 1 + wkv_count], refs[1 + wkv_count :]
    choose_ref, acckv_ref, ssq_ref, scale_ref, *pieces = refs
    me = lax.axis_index("head")
    columns = wkv_refs[0].shape[1]
    kvs = [acckv_ref[:, c * columns : (c + 1) * columns] for c in range(wkv_count)]
    ssq = ssq_ref[...]
    for i, x_ref in enumerate(xs):
        start, width = places[i](me), x_ref.shape[1]
        normed, squares = gained(x_ref[...], gain_ref, start)
        ssq = ssq + squares
        kvs = [kv + dot(normed, w_ref[from_start(start, width), :]) for kv, w_ref in zip(kvs, wkv_refs)]
    scale = lax.rsqrt(jnp.sum(ssq, axis=1, keepdims=True) / gain_ref.shape[1] + epsilon)
    scale_ref[...] = jnp.broadcast_to(scale, scale_ref.shape)
    kv = jnp.concatenate([(kv * scale).astype(bf16) for kv in kvs], axis=1)
    if wkv_count == 2:
        turned = dot_turned(choose_ref[0].astype(bf16), kv).astype(bf16)
        pieces[0][...], pieces[1][...] = turned[: kv.shape[1] // 2], turned[kv.shape[1] // 2 :]
        return
    for i, piece in enumerate(pieces):
        piece[...] = dot_turned(choose_ref[i].astype(bf16), kv).astype(bf16)


def last_kv(xs, places, gain, wkvs, choose, acckv, ssq):
    tokens = xs[0].shape[0]
    columns = len(wkvs) * wkvs[0].shape[1]
    operands = [*xs, *resident_in(gain, *wkvs, choose), acckv, ssq]
    count, size = (2, columns // 2) if len(wkvs) == 2 else choose.shape[:2]
    return pl.pallas_call(
        functools.partial(last_kv_kernel, len(xs), len(wkvs), places),
        out_shape=(VMEM((tokens, HD), f32),) + (VMEM((size, tokens), bf16),) * count,
        in_specs=[vmem] * len(operands),
        out_specs=(vmem,) * (1 + count),
        cost_estimate=cost(sum(2 * x.size * columns for x in xs), sum(2 * x.size for x in xs)),
        compiler_params=params,
        name="last_keys_values",
    )(*operands)


def last_q_kernel(count, places, *refs):
    xs, rest = refs[:count], refs[count:]
    gain_ref, wq_ref, accq_ref, scale_ref, *rest = rest
    me = lax.axis_index("head")
    total = accq_ref[...]
    for i, x_ref in enumerate(xs):
        start, width = places[i](me), x_ref.shape[1]
        normed, _ = gained(x_ref[...], gain_ref, start)
        total = total + dot(normed, wq_ref[from_start(start, width), :])
    q = (total * scale_ref[:, 0:1]).astype(bf16)
    if len(rest) == 1:
        rest[0][...] = q
        return
    piece_ref, fresh_ref, q_ref, bundle_ref = rest
    q_ref[...] = q
    late = bundle_ref.shape[1] - HD
    last = lax.axis_index("section") == lax.axis_size("section") - 1
    sent = jnp.where(last, fresh_ref[:, -late:].astype(f32), q[:, -late:].astype(f32))
    bundle_ref[:, :late] = sent.astype(bf16)
    bundle_ref[:, late:] = piece_ref[...]


def last_q(xs, places, gain, wq, accq, scale, bundled=(), late=0):
    operands = [*xs, *resident_in(gain, wq), accq, scale, *bundled]
    tokens = xs[0].shape[0]
    out = [VMEM((tokens, wq.shape[1]), bf16)]
    if bundled:
        out.append(VMEM((tokens, late + HD), bf16))
    return pl.pallas_call(
        functools.partial(last_q_kernel, len(xs), places),
        out_shape=tuple(out),
        in_specs=[vmem] * len(operands),
        out_specs=(vmem,) * len(out),
        cost_estimate=cost(sum(2 * x.size * wq.shape[1] for x in xs), sum(2 * x.size for x in xs)),
        compiler_params=params,
        name="last_queries",
    )(*operands)


def openings_kernel(sections, doc_ref, first_ref, second_ref):
    tokens = first_ref.shape[0]
    for turn, out_ref in enumerate((first_ref, second_ref)):
        start = (sections - 1 + turn - lax.axis_index("section")) * tokens
        here = start + lax.broadcasted_iota(jnp.int32, out_ref.shape, 0)
        opened = jnp.zeros(out_ref.shape, jnp.int32)
        end = jnp.int32(0)
        for d in range(doc_ref.shape[0]):
            end = end + doc_ref[d]
            opened = jnp.where(end <= here, end, opened)
        out_ref[...] = opened


def openings(doc_lengths, tokens, sections):
    return pl.pallas_call(
        functools.partial(openings_kernel, sections),
        out_shape=(VMEM((tokens, HD), jnp.int32),) * 2,
        in_specs=[smem],
        out_specs=(vmem,) * 2,
        compiler_params=params,
        name="openings",
    )(doc_lengths)


def stacked_heads(q_ref, heads):
    return jnp.concatenate([q_ref[:, h * HD : (h + 1) * HD] for h in range(*heads)], axis=0)


def masked_scores(q, keys, opened_ref, query_start, key_start):
    tokens, count = opened_ref.shape[0], keys.shape[1]
    here = query_start + lax.broadcasted_iota(jnp.int32, (tokens, count), 0)
    there = key_start + lax.broadcasted_iota(jnp.int32, (tokens, count), 1)
    allowed = (there >= opened_ref[:, 0:1]) & (there <= here)
    scores = jnp.where(allowed[None], dot(q, keys).reshape(-1, tokens, count), masked_score)
    return scores.reshape(-1, count)


def mixed_and_sums(expon, values):
    both = jnp.concatenate([values, jnp.ones(values.shape, bf16)], axis=0)
    both = dot_turned(expon.astype(bf16), both)
    return both[:, :HD], both[:, HD:]


def put_together(me, pieces, flips, parts, gather):
    features = pieces[0].shape[0] // 2
    for flip, piece_ref in zip(flips, pieces):
        source = lax.bitwise_xor(me, jnp.int32(flip)) // parts
        piece = piece_ref[...].astype(f32)
        gather[0, rows_of(source, features), :] = piece[:features]
        gather[1, rows_of(source, features), :] = piece[features:]
    return gather[0].astype(bf16), gather[1].astype(bf16)


def peer_attend_kernel(sections, flips, parts, opened_ref, bundle_ref, x_ref, piece_ref, out_ref, gather):
    section = lax.axis_index("section")
    tokens, width = out_ref.shape
    start = (sections - 1 - section) * tokens
    pieces = [piece_ref, bundle_ref.at[:, width:]]
    keys, values = put_together(lax.axis_index("head"), pieces, flips, parts, gather)
    q = stacked_heads(bundle_ref, (0, width // HD))
    scores = masked_scores(q, keys, opened_ref, start, start)
    expon = jnp.exp2((scores - jnp.max(scores, axis=1, keepdims=True)) * score_scale)
    mixed, total = mixed_and_sums(expon, values)
    mixed = (mixed * (1.0 / total)).astype(bf16).astype(f32)
    for h in range(width // HD):
        columns = slice(h * HD, (h + 1) * HD)
        x = x_ref[:, x_ref.shape[1] - width + h * HD : x_ref.shape[1] - width + (h + 1) * HD].astype(f32)
        out = (x + mixed[h * tokens : (h + 1) * tokens]).astype(bf16).astype(f32)
        out = jnp.where(section == sections - 1, bundle_ref[:, columns].astype(f32), out)
        out_ref[:, columns] = out.astype(bf16)


def peer_attend(opened, bundle, x, piece, flips, parts, sections):
    tokens, width = x.shape[0], bundle.shape[1] - HD
    return pl.pallas_call(
        functools.partial(peer_attend_kernel, sections, flips, parts),
        out_shape=VMEM((tokens, width), bf16),
        in_specs=[vmem] * 4,
        out_specs=vmem,
        scratch_shapes=[VMEM((2, HD, tokens), f32)],
        cost_estimate=cost(1000, 1000),
        compiler_params=params,
        name="peer_attend",
    )(opened, bundle, x, piece)


def first_attend_kernel(sections, heads, flips, parts, opened_ref, q_ref, x_ref, fresh_ref, *refs):
    section = lax.axis_index("section")
    start = (sections - 1 - section) * q_ref.shape[0]
    if flips is None:
        keys_ref, values_ref, out_ref = refs
        keys, values = keys_ref[...], values_ref[...]
    else:
        pieces, (out_ref, keys_ref, values_ref, gather) = refs[: len(flips)], refs[len(flips) :]
        keys, values = put_together(lax.axis_index("head"), pieces, flips, parts, gather)
        keys_ref[...], values_ref[...] = keys, values
    tokens = q_ref.shape[0]
    scores = masked_scores(stacked_heads(q_ref, heads), keys, opened_ref, start, start)
    expon = jnp.exp2((scores - jnp.max(scores, axis=1, keepdims=True)) * score_scale)
    mixed, total = mixed_and_sums(expon, values)
    mixed = (mixed * (1.0 / total)).astype(bf16).astype(f32)
    for i, h in enumerate(range(*heads)):
        columns = slice(h * HD, (h + 1) * HD)
        out = (x_ref[:, columns].astype(f32) + mixed[i * tokens : (i + 1) * tokens]).astype(bf16)
        out = jnp.where(section == sections - 1, fresh_ref[:, columns].astype(f32), out.astype(f32))
        out_ref[:, i * HD : (i + 1) * HD] = out.astype(bf16)


def first_attend(opened, q, x, fresh, pieces, flips, parts, heads, sections):
    tokens = q.shape[0]
    out = (VMEM((tokens, (heads[1] - heads[0]) * HD), bf16),)
    scratch = []
    if flips is not None:
        out = out + (VMEM((HD, tokens), bf16),) * 2
        scratch = [VMEM((2, HD, tokens), f32)]
    operands = [opened, q, x, fresh, *pieces]
    return pl.pallas_call(
        functools.partial(first_attend_kernel, sections, heads, flips, parts),
        out_shape=out,
        in_specs=[vmem] * len(operands),
        out_specs=(vmem,) * len(out),
        scratch_shapes=scratch,
        cost_estimate=cost(10**10, 1000),
        compiler_params=params,
        name="first_attend",
    )(*operands)


def resident_kernel(sections, opened_ref, q_ref, keys_ref, values_ref, max_ref, sum_ref, mixed_ref):
    tokens = q_ref.shape[0]
    key_start = (sections - 1 - lax.axis_index("section")) * tokens
    q = stacked_heads(q_ref, (0, q_ref.shape[1] // HD))
    scores = masked_scores(q, keys_ref[...], opened_ref, key_start + tokens, key_start)
    top = jnp.max(scores, axis=1, keepdims=True)
    expon = jnp.exp2((scores - top) * score_scale)
    max_ref[...] = jnp.broadcast_to(top, max_ref.shape)
    mixed_ref[...], sum_ref[...] = mixed_and_sums(expon, values_ref[...])


def resident_attend(opened, q, keys, values, sections):
    rows = q.shape[0] * (q.shape[1] // HD)
    return pl.pallas_call(
        functools.partial(resident_kernel, sections),
        out_shape=(VMEM((rows, HD), f32),) * 3,
        in_specs=[vmem] * 4,
        out_specs=(vmem,) * 3,
        cost_estimate=cost(1000, 1000),
        compiler_params=params,
        name="resident_attend",
    )(opened, q, keys, values)


def second_attend_kernel(sections, flips, parts, x_count, opened_ref, q_ref, max_ref, sum_ref, mixed_ref, *refs):
    x_refs, refs = refs[:x_count], refs[x_count:]
    pieces, (out_ref, gather) = refs[: len(flips)], refs[len(flips) :]
    tokens, heads = q_ref.shape[0], q_ref.shape[1] // HD
    start = (sections - lax.axis_index("section")) * tokens
    keys, values = put_together(lax.axis_index("head"), pieces, flips, parts, gather)
    scores = masked_scores(stacked_heads(q_ref, (0, heads)), keys, opened_ref, start, start)
    top = jnp.maximum(jnp.max(scores, axis=1, keepdims=True), max_ref[...])
    expon = jnp.exp2((scores - top) * score_scale)
    shrink = jnp.exp2((max_ref[...] - top) * score_scale)
    mixed, total = mixed_and_sums(expon, values)
    total = total + shrink * sum_ref[...]
    mixed = mixed + shrink * mixed_ref[...]
    mixed = (mixed * (1.0 / total)).astype(bf16).astype(f32)
    where = [(x_ref, inside) for x_ref in x_refs for inside in range(0, x_ref.shape[1], HD)]
    for h, (x_ref, inside) in enumerate(where):
        out = x_ref[:, inside : inside + HD].astype(f32) + mixed[h * tokens : (h + 1) * tokens]
        out_ref[:, h * HD : (h + 1) * HD] = out.astype(bf16)


def second_attend(opened, q, xs, resident, pieces, flips, parts, sections):
    tokens = q.shape[0]
    operands = [opened, q, *resident, *xs, *pieces]
    return pl.pallas_call(
        functools.partial(second_attend_kernel, sections, flips, parts, len(xs)),
        out_shape=jax.ShapeDtypeStruct(q.shape, bf16),
        in_specs=[vmem] * len(operands),
        out_specs=vmem,
        scratch_shapes=[VMEM((2, HD, tokens), f32)],
        cost_estimate=cost(1000, 1000),
        compiler_params=params,
        name="second_attend",
    )(*operands)


def shards(entering, fresh_slice, norm_gain, w_query, w_key_value, doc_lengths):
    n = lax.axis_size("head")
    sections = lax.axis_size("section")
    own = entering[0]
    w_q, w_kv = w_query[0], w_key_value[0]
    tokens, width = own.shape
    heads = w_q.shape[1] // HD
    paired = n == 4
    parts = 2 if paired else 1
    flips = [0, 3] if paired else list(range(n))

    def moved(array, by, flip):
        pairs = [
            (s * n + h, ((s + by) % sections) * n + (h ^ flip)) for s in range(sections) for h in range(n)
        ]
        return lax.ppermute(array, ("section", "head"), pairs)

    def after(array, *others):
        return lax.optimization_barrier((array, *others))[0]

    def exchanged(xs, places, state):
        scale, *pieces = last_kv(xs, places, gain, wkvs, choose, state[1], state[2])
        received = [moved(piece, 0, flip) for piece, flip in zip(pieces[1:], flips[1:])]
        return scale, [pieces[0], *received], pieces

    def rest_of(array):
        every = lax.all_gather(array, "head", axis=0)
        me = lax.axis_index("head")
        return [lax.dynamic_index_in_dim(every, (me + k) % n, 0, False) for k in range(1, n)]

    def place(flip, offset=0):
        return lambda me: lax.bitwise_xor(me, jnp.int32(flip)) * width + offset

    following = [functools.partial(lambda k, me: lax.rem(me + k, jnp.int32(n)) * width, k) for k in range(n)]

    if paired:
        over = moved(own, 0, 3)
        beside = moved(own, 0, 1)
        w_kv_beside = moved(w_kv, 0, 1)
    accq, own, gain, wq, choose, wkv = load(own, norm_gain, w_q, w_kv, n, flips, parts)
    opened = openings(after(doc_lengths, accq), tokens, sections)
    if paired:
        wkvs = [wkv, selected(after(w_kv_beside, accq))]
        over, wkvs[1], *opened = lax.optimization_barrier((over, wkvs[1], *opened))
        passed = moved(over, 0, 1)
        xs, places, with_q = [own, beside, over], [place(0), place(1), place(3)], [False, True, True]
        state = more_blocks(xs, places, gain, wq, wkvs, [accq], with_q)
        last, places = [passed], [place(2)]
    else:
        wkvs = [wkv]
        state = more_blocks([own], following[:1], gain, wq, wkvs, [accq], [False])
        last, places = rest_of(own), following[1:]
    scale, pieces, made = exchanged(last, places, state)
    part = heads // 2 if paired else heads
    split = part * HD
    if paired:
        q, bundle = last_q(last, places, gain, wq, state[0], scale, [made[0], fresh_slice], width - split)
        bundle = moved(bundle, 0, 3)
    else:
        (q,) = last_q(last, places, gain, wq, state[0], scale)
    sent, keys, values = first_attend(
        opened[0], q, own, fresh_slice, pieces, flips, parts, (0, part), sections
    )

    if paired:
        a1 = moved(sent, 1, 1)
        (sent,) = first_attend(
            opened[0], q, own, fresh_slice, [keys, values], None, parts, (part, heads), sections
        )
        b1 = moved(sent, 1, 1)
        bundle = after(bundle, sent)
        peers = peer_attend(opened[0], bundle, over, made[1], flips, parts, sections)
        b2 = moved(peers, 1, 1)
        a1 = after(a1, peers)
        a2 = moved(a1, 0, 3)
        a0 = moved(a1, 0, 1)
        state = more_blocks([a1], [place(1)], gain, wq, wkvs, [])
        b1, *state = lax.optimization_barrier((b1, *state))
        b0 = moved(b1, 0, 1)
        state = more_blocks([b1], [place(1, split)], gain, wq, wkvs, state)
        b2, *state = lax.optimization_barrier((b2, *state))
        b3 = moved(b2, 0, 1)
        a3 = moved(a2, 0, 1)
        state = more_blocks([a0, a2, b2], [place(0), place(2), place(2, split)], gain, wq, wkvs, state)
        last, places = [a3, b0, b3], [place(3), place(0, split), place(3, split)]
        mine = [a0, b0]
    else:
        mine = [moved(sent, 1, 0)]
        state = more_blocks(mine, following[:1], gain, wq, wkvs, [])
        last, places = rest_of(mine[0]), following[1:]
    scale, pieces, _ = exchanged(last, places, state)
    (q,) = last_q(last, places, gain, wq, state[0], scale)
    resident = resident_attend(opened[1], q, keys, values, sections)
    return second_attend(opened[1], q, mine, resident, pieces, flips, parts, sections)[None]


def solution(mesh):
    placed = (
        P("section", None, "head"),
        P(None, "head"),
        P("section", None),
        P("section", None, "head"),
        P("section", None, "head"),
        P(),
    )
    return jax.shard_map(
        shards, mesh=mesh, in_specs=placed, out_specs=P("section", None, "head"), check_vma=False
    )
```

```python
import functools
import math

import jax
import jax.numpy as jnp
from jax import lax
from jax.experimental import pallas as pl
from jax.experimental.pallas import tpu as pltpu
from jax.sharding import PartitionSpec as P

HD = 128
KVH = 4
GROUP = 8

epsilon = 1e-05
score_scale = math.log2(math.e) / math.sqrt(HD)
masked_score = -1e30

VMEM = pltpu.VMEM
f32 = jnp.float32
bf16 = jnp.bfloat16
vmem = pl.BlockSpec(memory_space=VMEM)
smem = pl.BlockSpec(memory_space=pltpu.SMEM)
in_hbm = pl.BlockSpec(memory_space=pltpu.HBM)
params = pltpu.CompilerParams(vmem_limit_bytes=16 * 1024 * 1024)


def resident_in(*arrays):
    return [pltpu.with_memory_space_constraint(a, VMEM) for a in arrays]


def cost(flops, moved):
    return pl.CostEstimate(flops=flops, bytes_accessed=moved, transcendentals=0)


def rows_of(block, width):
    return pl.ds(pl.multiple_of(block * width, width), width)


def from_start(start, width):
    return pl.ds(pl.multiple_of(start, HD), width)


def dot(a, b):
    return jnp.dot(a, b, preferred_element_type=f32)


def dot_turned(a, b):
    return lax.dot_general(a, b, (((1,), (1,)), ((), ())), preferred_element_type=f32)


def squares_by_lane(wide):
    squares = wide * wide
    ssq = squares[:, :HD]
    for c in range(HD, wide.shape[1], HD):
        ssq = ssq + squares[:, c : c + HD]
    return ssq


def choose_rows(choose_ref, me, n, flips, parts):
    size, columns = choose_ref.shape[1], choose_ref.shape[2] // parts
    features = size // (2 * parts)
    shape = (features, choose_ref.shape[2])
    row = lax.broadcasted_iota(jnp.int32, shape, 0)
    col = lax.broadcasted_iota(jnp.int32, shape, 1)
    offset = col - row * (2 * KVH)
    for i, flip in enumerate(flips):
        group = lax.bitwise_xor(me, jnp.int32(flip)) * KVH // n
        for which in range(2):
            for core in range(parts):
                whose = jnp.where(lax.rem(me, jnp.int32(parts)) == core, 0, 1)
                wanted = whose * columns + group * 2 + which
                first = (which * parts + core) * features
                choose_ref[i, first : first + features, :] = jnp.where(offset == wanted, 1.0, 0.0)


def load_kernel(
    n, flips, parts, x_hbm, gain_hbm, wq_hbm, wkv_hbm, x_ref, gain_ref, wq_ref, wkv_ref, choose_ref, sems
):
    width = x_hbm.shape[1]
    me = lax.axis_index("head")

    def part(step):
        rows = rows_of(lax.rem(me + step, n), width)
        return pltpu.make_async_copy(wq_hbm.at[rows], wq_ref.at[rows], sems.at[step])

    small = (
        pltpu.make_async_copy(x_hbm, x_ref, sems.at[n]),
        pltpu.make_async_copy(gain_hbm, gain_ref, sems.at[n + 1]),
    )
    keys_values = pltpu.make_async_copy(wkv_hbm, wkv_ref, sems.at[n + 2])
    for copy in small:
        copy.start()
    for step in range(n):
        part(step).start()
    keys_values.start()
    choose_rows(choose_ref, me, n, flips, parts)
    for copy in (*small, keys_values):
        copy.wait()
    for step in range(n):
        part(step).wait()


def load(x, gain, wq, wkv, n, flips, parts):
    tokens, width = x.shape
    columns = wkv.shape[1]
    operands = [pltpu.with_memory_space_constraint(a, pltpu.HBM) for a in (x, gain, wq, wkv)]
    return pl.pallas_call(
        functools.partial(load_kernel, n, flips, parts),
        out_shape=(
            VMEM(x.shape, bf16),
            VMEM(gain.shape, f32),
            VMEM(wq.shape, bf16),
            VMEM(wkv.shape, bf16),
            VMEM((len(flips), parts * columns // KVH, parts * columns), f32),
        ),
        in_specs=[in_hbm] * 4,
        out_specs=(vmem,) * 5,
        scratch_shapes=[pltpu.SemaphoreType.DMA((n + 3,))],
        cost_estimate=cost(10**11, 10**9),
        compiler_params=params,
        name="load",
    )(*operands)


def keys_values_kernel(count, wkv_count, places, *refs):
    xs, refs = refs[:count], refs[count:]
    gain_ref, wkv_refs, refs = refs[0], refs[1 : 1 + wkv_count], refs[1 + wkv_count :]
    choose_ref, normed_ref, *pieces = refs
    me = lax.axis_index("head")
    ssq = squares_by_lane(xs[0][...].astype(f32))
    for x_ref in xs[1:]:
        ssq = ssq + squares_by_lane(x_ref[...].astype(f32))
    scale = lax.rsqrt(jnp.sum(ssq, axis=1, keepdims=True) / gain_ref.shape[1] + epsilon)
    kvs, at = [None] * wkv_count, 0
    for place, x_ref in zip(places, xs):
        width = x_ref.shape[1]
        rows = from_start(place(me), width)
        normed = (x_ref[...].astype(f32) * scale * gain_ref[:, rows]).astype(bf16)
        normed_ref[:, at : at + width] = normed
        at += width
        terms = [dot(normed, w_ref[rows, :]) for w_ref in wkv_refs]
        kvs = [term if kv is None else kv + term for kv, term in zip(kvs, terms)]
    kv = jnp.concatenate([kv.astype(bf16) for kv in kvs], axis=1)
    for i, piece in enumerate(pieces):
        piece[...] = dot_turned(choose_ref[i].astype(bf16), kv).astype(bf16)


def keys_values(xs, places, gain, wkvs, choose):
    tokens, width = xs[0].shape[0], sum(x.shape[1] for x in xs)
    columns = len(wkvs) * wkvs[0].shape[1]
    operands = [*xs, *resident_in(gain, *wkvs, choose)]
    count = choose.shape[0]
    return pl.pallas_call(
        functools.partial(keys_values_kernel, len(xs), len(wkvs), places),
        out_shape=(VMEM((tokens, width), bf16),) + (VMEM((columns // KVH, tokens), bf16),) * count,
        in_specs=[vmem] * len(operands),
        out_specs=(vmem,) * (1 + count),
        cost_estimate=cost(2 * tokens * width * columns, 2 * tokens * width),
        compiler_params=params,
        name="keys_values",
    )(*operands)


def queries_kernel(widths, places, normed_ref, wq_ref, *refs):
    me = lax.axis_index("head")
    total, at = None, 0
    for place, width in zip(places, widths):
        term = dot(normed_ref[:, at : at + width], wq_ref[from_start(place(me), width), :])
        total = term if total is None else total + term
        at += width
    q = total.astype(bf16)
    if len(refs) == 1:
        refs[0][...] = q
        return
    piece_ref, fresh_ref, q_ref, bundle_ref = refs
    q_ref[...] = q
    late = bundle_ref.shape[1] - HD
    last = lax.axis_index("section") == lax.axis_size("section") - 1
    sent = jnp.where(last, fresh_ref[:, -late:].astype(f32), q[:, -late:].astype(f32))
    bundle_ref[:, :late] = sent.astype(bf16)
    bundle_ref[:, late:] = piece_ref[...]


def queries(normed, widths, places, wq, bundled=(), late=0):
    tokens = normed.shape[0]
    operands = [normed, *resident_in(wq), *bundled]
    out = [VMEM((tokens, wq.shape[1]), bf16)]
    if bundled:
        out.append(VMEM((tokens, late + HD), bf16))
    return pl.pallas_call(
        functools.partial(queries_kernel, widths, places),
        out_shape=tuple(out),
        in_specs=[vmem] * len(operands),
        out_specs=(vmem,) * len(out),
        cost_estimate=cost(1000, 1000),
        compiler_params=params,
        name="queries",
    )(*operands)


def openings_kernel(sections, doc_ref, first_ref, second_ref):
    tokens = first_ref.shape[0]
    for turn, out_ref in enumerate((first_ref, second_ref)):
        start = (sections - 1 + turn - lax.axis_index("section")) * tokens
        here = start + lax.broadcasted_iota(jnp.int32, out_ref.shape, 0)
        opened = jnp.zeros(out_ref.shape, jnp.int32)
        end = jnp.int32(0)
        for d in range(doc_ref.shape[0]):
            end = end + doc_ref[d]
            opened = jnp.where(end <= here, end, opened)
        out_ref[...] = opened


def openings(doc_lengths, tokens, sections):
    return pl.pallas_call(
        functools.partial(openings_kernel, sections),
        out_shape=(VMEM((tokens, HD), jnp.int32),) * 2,
        in_specs=[smem],
        out_specs=(vmem,) * 2,
        compiler_params=params,
        name="openings",
    )(doc_lengths)


def stacked_heads(q_ref, heads):
    return jnp.concatenate([q_ref[:, h * HD : (h + 1) * HD] for h in range(*heads)], axis=0)


def masked_scores(q, keys, opened_ref, query_start, key_start):
    tokens, count = opened_ref.shape[0], keys.shape[1]
    here = query_start + lax.broadcasted_iota(jnp.int32, (tokens, count), 0)
    there = key_start + lax.broadcasted_iota(jnp.int32, (tokens, count), 1)
    allowed = (there >= opened_ref[:, 0:1]) & (there <= here)
    scores = jnp.where(allowed[None], dot(q, keys).reshape(-1, tokens, count), masked_score)
    return scores.reshape(-1, count)


def mixed_and_sums(expon, values):
    both = jnp.concatenate([values, jnp.ones(values.shape, bf16)], axis=0)
    both = dot_turned(expon.astype(bf16), both)
    return both[:, :HD], both[:, HD:]


def put_together(me, pieces, flips, parts, gather):
    features = pieces[0].shape[0] // 2
    for flip, piece_ref in zip(flips, pieces):
        source = lax.bitwise_xor(me, jnp.int32(flip)) // parts
        piece = piece_ref[...].astype(f32)
        gather[0, rows_of(source, features), :] = piece[:features]
        gather[1, rows_of(source, features), :] = piece[features:]
    return gather[0].astype(bf16), gather[1].astype(bf16)


def peer_attend_kernel(sections, flips, parts, opened_ref, bundle_ref, x_ref, piece_ref, out_ref, gather):
    section = lax.axis_index("section")
    tokens, width = out_ref.shape
    start = (sections - 1 - section) * tokens
    pieces = [piece_ref, bundle_ref.at[:, width:]]
    keys, values = put_together(lax.axis_index("head"), pieces, flips, parts, gather)
    q = stacked_heads(bundle_ref, (0, width // HD))
    scores = masked_scores(q, keys, opened_ref, start, start)
    expon = jnp.exp2((scores - jnp.max(scores, axis=1, keepdims=True)) * score_scale)
    mixed, total = mixed_and_sums(expon, values)
    mixed = (mixed * (1.0 / total)).astype(bf16).astype(f32)
    for h in range(width // HD):
        columns = slice(h * HD, (h + 1) * HD)
        x = x_ref[:, x_ref.shape[1] - width + h * HD : x_ref.shape[1] - width + (h + 1) * HD].astype(f32)
        out = (x + mixed[h * tokens : (h + 1) * tokens]).astype(bf16).astype(f32)
        out = jnp.where(section == sections - 1, bundle_ref[:, columns].astype(f32), out)
        out_ref[:, columns] = out.astype(bf16)


def peer_attend(opened, bundle, x, piece, flips, parts, sections):
    tokens, width = x.shape[0], bundle.shape[1] - HD
    return pl.pallas_call(
        functools.partial(peer_attend_kernel, sections, flips, parts),
        out_shape=VMEM((tokens, width), bf16),
        in_specs=[vmem] * 4,
        out_specs=vmem,
        scratch_shapes=[VMEM((2, HD, tokens), f32)],
        cost_estimate=cost(1000, 1000),
        compiler_params=params,
        name="peer_attend",
    )(opened, bundle, x, piece)


def first_attend_kernel(sections, heads, flips, parts, opened_ref, q_ref, x_ref, fresh_ref, *refs):
    section = lax.axis_index("section")
    start = (sections - 1 - section) * q_ref.shape[0]
    if flips is None:
        keys_ref, values_ref, out_ref = refs
        keys, values = keys_ref[...], values_ref[...]
    else:
        pieces, (out_ref, keys_ref, values_ref, gather) = refs[: len(flips)], refs[len(flips) :]
        keys, values = put_together(lax.axis_index("head"), pieces, flips, parts, gather)
        keys_ref[...], values_ref[...] = keys, values
    tokens = q_ref.shape[0]
    scores = masked_scores(stacked_heads(q_ref, heads), keys, opened_ref, start, start)
    expon = jnp.exp2((scores - jnp.max(scores, axis=1, keepdims=True)) * score_scale)
    mixed, total = mixed_and_sums(expon, values)
    mixed = (mixed * (1.0 / total)).astype(bf16).astype(f32)
    for i, h in enumerate(range(*heads)):
        columns = slice(h * HD, (h + 1) * HD)
        out = (x_ref[:, columns].astype(f32) + mixed[i * tokens : (i + 1) * tokens]).astype(bf16)
        out = jnp.where(section == sections - 1, fresh_ref[:, columns].astype(f32), out.astype(f32))
        out_ref[:, i * HD : (i + 1) * HD] = out.astype(bf16)


def first_attend(opened, q, x, fresh, pieces, flips, parts, heads, sections):
    tokens = q.shape[0]
    out = (VMEM((tokens, (heads[1] - heads[0]) * HD), bf16),)
    scratch = []
    if flips is not None:
        out = out + (VMEM((HD, tokens), bf16),) * 2
        scratch = [VMEM((2, HD, tokens), f32)]
    operands = [opened, q, x, fresh, *pieces]
    return pl.pallas_call(
        functools.partial(first_attend_kernel, sections, heads, flips, parts),
        out_shape=out,
        in_specs=[vmem] * len(operands),
        out_specs=(vmem,) * len(out),
        scratch_shapes=scratch,
        cost_estimate=cost(10**10, 1000),
        compiler_params=params,
        name="first_attend",
    )(*operands)


def resident_kernel(sections, opened_ref, q_ref, keys_ref, values_ref, max_ref, sum_ref, mixed_ref):
    tokens = q_ref.shape[0]
    key_start = (sections - 1 - lax.axis_index("section")) * tokens
    q = stacked_heads(q_ref, (0, q_ref.shape[1] // HD))
    scores = masked_scores(q, keys_ref[...], opened_ref, key_start + tokens, key_start)
    top = jnp.max(scores, axis=1, keepdims=True)
    expon = jnp.exp2((scores - top) * score_scale)
    max_ref[...] = jnp.broadcast_to(top, max_ref.shape)
    mixed_ref[...], sum_ref[...] = mixed_and_sums(expon, values_ref[...])


def resident_attend(opened, q, keys, values, sections):
    rows = q.shape[0] * (q.shape[1] // HD)
    return pl.pallas_call(
        functools.partial(resident_kernel, sections),
        out_shape=(VMEM((rows, HD), f32),) * 3,
        in_specs=[vmem] * 4,
        out_specs=(vmem,) * 3,
        cost_estimate=cost(1000, 1000),
        compiler_params=params,
        name="resident_attend",
    )(opened, q, keys, values)


def second_attend_kernel(sections, flips, parts, x_count, opened_ref, q_ref, max_ref, sum_ref, mixed_ref, *refs):
    x_refs, refs = refs[:x_count], refs[x_count:]
    pieces, (out_ref, gather) = refs[: len(flips)], refs[len(flips) :]
    tokens, heads = q_ref.shape[0], q_ref.shape[1] // HD
    start = (sections - lax.axis_index("section")) * tokens
    keys, values = put_together(lax.axis_index("head"), pieces, flips, parts, gather)
    scores = masked_scores(stacked_heads(q_ref, (0, heads)), keys, opened_ref, start, start)
    top = jnp.maximum(jnp.max(scores, axis=1, keepdims=True), max_ref[...])
    expon = jnp.exp2((scores - top) * score_scale)
    shrink = jnp.exp2((max_ref[...] - top) * score_scale)
    mixed, total = mixed_and_sums(expon, values)
    total = total + shrink * sum_ref[...]
    mixed = mixed + shrink * mixed_ref[...]
    mixed = (mixed * (1.0 / total)).astype(bf16).astype(f32)
    where = [(x_ref, inside) for x_ref in x_refs for inside in range(0, x_ref.shape[1], HD)]
    for h, (x_ref, inside) in enumerate(where):
        out = x_ref[:, inside : inside + HD].astype(f32) + mixed[h * tokens : (h + 1) * tokens]
        out_ref[:, h * HD : (h + 1) * HD] = out.astype(bf16)


def second_attend(opened, q, xs, resident, pieces, flips, parts, sections):
    tokens = q.shape[0]
    operands = [opened, q, *resident, *xs, *pieces]
    return pl.pallas_call(
        functools.partial(second_attend_kernel, sections, flips, parts, len(xs)),
        out_shape=jax.ShapeDtypeStruct(q.shape, bf16),
        in_specs=[vmem] * len(operands),
        out_specs=vmem,
        scratch_shapes=[VMEM((2, HD, tokens), f32)],
        cost_estimate=cost(1000, 1000),
        compiler_params=params,
        name="second_attend",
    )(*operands)


def shards(entering, fresh_slice, norm_gain, w_query, w_key_value, doc_lengths):
    n = lax.axis_size("head")
    sections = lax.axis_size("section")
    own = entering[0]
    w_q, w_kv = w_query[0], w_key_value[0]
    tokens, width = own.shape
    heads = w_q.shape[1] // HD
    paired = n == 4
    parts = 2 if paired else 1
    flips = [0, 3] if paired else list(range(n))

    def moved(array, by, flip):
        pairs = [
            (s * n + h, ((s + by) % sections) * n + (h ^ flip)) for s in range(sections) for h in range(n)
        ]
        return lax.ppermute(array, ("section", "head"), pairs)

    def after(array, *others):
        return lax.optimization_barrier((array, *others))[0]

    def exchanged(xs, places):
        normed, *pieces = keys_values(xs, places, gain, wkvs, choose)
        received = [moved(piece, 0, flip) for piece, flip in zip(pieces[1:], flips[1:])]
        return normed, [pieces[0], *received], pieces, [x.shape[1] for x in xs]

    def rest_of(array):
        every = lax.all_gather(array, "head", axis=0)
        me = lax.axis_index("head")
        return [lax.dynamic_index_in_dim(every, (me + k) % n, 0, False) for k in range(1, n)]

    def place(flip, offset=0):
        return lambda me: lax.bitwise_xor(me, jnp.int32(flip)) * width + offset

    following = [functools.partial(lambda k, me: lax.rem(me + k, jnp.int32(n)) * width, k) for k in range(n)]

    if paired:
        over = moved(own, 0, 3)
        beside = moved(own, 0, 1)
        w_kv_beside = moved(w_kv, 0, 1)
    own, gain, wq, wkv, choose = load(own, norm_gain, w_q, w_kv, n, flips, parts)
    opened = openings(after(doc_lengths, gain), tokens, sections)
    if paired:
        wkvs = [wkv, w_kv_beside]
        over, *opened = lax.optimization_barrier((over, *opened))
        passed = moved(over, 0, 1)
        xs, places = [own, beside, over, passed], [place(0), place(1), place(3), place(2)]
    else:
        wkvs = [wkv]
        xs, places = [own, *rest_of(own)], following
    normed, pieces, made, widths = exchanged(xs, places)
    part = heads // 2 if paired else heads
    split = part * HD
    if paired:
        q, bundle = queries(normed, widths, places, wq, [made[0], fresh_slice], width - split)
        bundle = moved(bundle, 0, 3)
    else:
        (q,) = queries(normed, widths, places, wq)
    sent, keys, values = first_attend(
        opened[0], q, own, fresh_slice, pieces, flips, parts, (0, part), sections
    )

    if paired:
        a1 = moved(sent, 1, 1)
        (sent,) = first_attend(
            opened[0], q, own, fresh_slice, [keys, values], None, parts, (part, heads), sections
        )
        b1 = moved(sent, 1, 1)
        bundle = after(bundle, sent)
        peers = peer_attend(opened[0], bundle, over, made[1], flips, parts, sections)
        b2 = moved(peers, 1, 1)
        a1 = after(a1, peers)
        a2 = moved(a1, 0, 3)
        a0 = moved(a1, 0, 1)
        b0 = moved(b1, 0, 1)
        b3 = moved(b2, 0, 1)
        a3 = moved(a2, 0, 1)
        xs = [a1, a0, b1, b0, a2, b2, a3, b3]
        places = [place(1), place(0), place(1, split), place(0, split)]
        places += [place(2), place(2, split), place(3), place(3, split)]
        mine = [a0, b0]
    else:
        mine = [jnp.where(lax.axis_index("section") == 0, fresh_slice, moved(sent, 1, 0))]
        xs, places = [*mine, *rest_of(mine[0])], following
    normed, pieces, _, widths = exchanged(xs, places)
    (q,) = queries(normed, widths, places, wq)
    resident = resident_attend(opened[1], q, keys, values, sections)
    return second_attend(opened[1], q, mine, resident, pieces, flips, parts, sections)[None]


def solution(mesh):
    placed = (
        P("section", None, "head"),
        P(None, "head"),
        P("section", None),
        P("section", None, "head"),
        P("section", None, "head"),
        P(),
    )
    return jax.shard_map(
        shards, mesh=mesh, in_specs=placed, out_specs=P("section", None, "head"), check_vma=False
    )
```

```python
import functools
import math

import jax
import jax.numpy as jnp
from jax import lax
from jax.experimental import pallas as pl
from jax.experimental.pallas import tpu as pltpu
from jax.sharding import PartitionSpec as P

HD = 128
KVH = 4
GROUP = 8

epsilon = 1e-05
score_scale = math.log2(math.e) / math.sqrt(HD)
masked_score = -1e30

VMEM = pltpu.VMEM
f32 = jnp.float32
bf16 = jnp.bfloat16
vmem = pl.BlockSpec(memory_space=VMEM)
smem = pl.BlockSpec(memory_space=pltpu.SMEM)
in_hbm = pl.BlockSpec(memory_space=pltpu.HBM)
params = pltpu.CompilerParams(vmem_limit_bytes=16 * 1024 * 1024)


def resident_in(*arrays):
    return [pltpu.with_memory_space_constraint(a, VMEM) for a in arrays]


def cost(flops, moved):
    return pl.CostEstimate(flops=flops, bytes_accessed=moved, transcendentals=0)


def rows_of(block, width):
    return pl.ds(pl.multiple_of(block * width, width), width)


def from_start(start, width):
    return pl.ds(pl.multiple_of(start, HD), width)


def dot(a, b):
    return jnp.dot(a, b, preferred_element_type=f32)


def dot_turned(a, b):
    return lax.dot_general(a, b, (((1,), (1,)), ((), ())), preferred_element_type=f32)


def squares_by_lane(wide):
    squares = wide * wide
    ssq = squares[:, :HD]
    for c in range(HD, wide.shape[1], HD):
        ssq = ssq + squares[:, c : c + HD]
    return ssq


def choose_rows(choose_ref, me, n, flips, parts):
    size, columns = choose_ref.shape[1], choose_ref.shape[2] // parts
    features = size // (2 * parts)
    shape = (features, choose_ref.shape[2])
    row = lax.broadcasted_iota(jnp.int32, shape, 0)
    col = lax.broadcasted_iota(jnp.int32, shape, 1)
    offset = col - row * (2 * KVH)
    for i, flip in enumerate(flips):
        group = lax.bitwise_xor(me, jnp.int32(flip)) * KVH // n
        for which in range(2):
            for core in range(parts):
                whose = jnp.where(lax.rem(me, jnp.int32(parts)) == core, 0, 1)
                wanted = whose * columns + group * 2 + which
                first = (which * parts + core) * features
                choose_ref[i, first : first + features, :] = jnp.where(offset == wanted, 1.0, 0.0)


def load_kernel(
    n, flips, parts, x_hbm, gain_hbm, wq_hbm, wkv_hbm, x_ref, gain_ref, wq_ref, wkv_ref, choose_ref, sems
):
    width = x_hbm.shape[1]
    me = lax.axis_index("head")

    def part(step):
        rows = rows_of(lax.rem(me + step, n), width)
        return pltpu.make_async_copy(wq_hbm.at[rows], wq_ref.at[rows], sems.at[step])

    small = (
        pltpu.make_async_copy(x_hbm, x_ref, sems.at[n]),
        pltpu.make_async_copy(gain_hbm, gain_ref, sems.at[n + 1]),
    )
    keys_values = pltpu.make_async_copy(wkv_hbm, wkv_ref, sems.at[n + 2])
    for copy in small:
        copy.start()
    for step in range(n):
        part(step).start()
    keys_values.start()
    choose_rows(choose_ref, me, n, flips, parts)
    for copy in (*small, keys_values):
        copy.wait()
    for step in range(n):
        part(step).wait()


def load(x, gain, wq, wkv, n, flips, parts):
    tokens, width = x.shape
    columns = wkv.shape[1]
    operands = [pltpu.with_memory_space_constraint(a, pltpu.HBM) for a in (x, gain, wq, wkv)]
    return pl.pallas_call(
        functools.partial(load_kernel, n, flips, parts),
        out_shape=(
            VMEM(x.shape, bf16),
            VMEM(gain.shape, f32),
            VMEM(wq.shape, bf16),
            VMEM(wkv.shape, bf16),
            VMEM((len(flips), parts * columns // KVH, parts * columns), f32),
        ),
        in_specs=[in_hbm] * 4,
        out_specs=(vmem,) * 5,
        scratch_shapes=[pltpu.SemaphoreType.DMA((n + 3,))],
        cost_estimate=cost(10**11, 10**9),
        compiler_params=params,
        name="load",
    )(*operands)


def squares_kernel(count, *refs):
    ssq = squares_by_lane(refs[0][...].astype(f32))
    for x_ref in refs[1:count]:
        ssq = ssq + squares_by_lane(x_ref[...].astype(f32))
    for old_ref in refs[count:-1]:
        ssq = ssq + old_ref[...]
    refs[-1][...] = ssq


def squares(xs, old=()):
    operands = [*xs, *old]
    return pl.pallas_call(
        functools.partial(squares_kernel, len(xs)),
        out_shape=VMEM((xs[0].shape[0], HD), f32),
        in_specs=[vmem] * len(operands),
        out_specs=vmem,
        cost_estimate=cost(sum(2560 * x.size for x in xs), sum(2 * x.size for x in xs)),
        compiler_params=params,
        name="squares",
    )(*operands)


def keys_values_kernel(count, wkv_count, squared, places, *refs):
    xs, refs = refs[:count], refs[count:]
    gain_ref, wkv_refs, refs = refs[0], refs[1 : 1 + wkv_count], refs[1 + wkv_count :]
    choose_ref, ssq_ref, normed_ref, *pieces = refs
    me = lax.axis_index("head")
    ssq = ssq_ref[...]
    for x_ref in xs[squared:]:
        ssq = ssq + squares_by_lane(x_ref[...].astype(f32))
    scale = lax.rsqrt(jnp.sum(ssq, axis=1, keepdims=True) / gain_ref.shape[1] + epsilon)
    kvs, at = [None] * wkv_count, 0
    for place, x_ref in zip(places, xs):
        width = x_ref.shape[1]
        rows = from_start(place(me), width)
        normed = (x_ref[...].astype(f32) * scale * gain_ref[:, rows]).astype(bf16)
        normed_ref[:, at : at + width] = normed
        at += width
        terms = [dot(normed, w_ref[rows, :]) for w_ref in wkv_refs]
        kvs = [term if kv is None else kv + term for kv, term in zip(kvs, terms)]
    kv = jnp.concatenate([kv.astype(bf16) for kv in kvs], axis=1)
    for i, piece in enumerate(pieces):
        piece[...] = dot_turned(choose_ref[i].astype(bf16), kv).astype(bf16)


def keys_values(xs, places, gain, wkvs, choose, ssq, squared):
    tokens, width = xs[0].shape[0], sum(x.shape[1] for x in xs)
    columns = len(wkvs) * wkvs[0].shape[1]
    operands = [*xs, *resident_in(gain, *wkvs, choose), ssq]
    count = choose.shape[0]
    return pl.pallas_call(
        functools.partial(keys_values_kernel, len(xs), len(wkvs), squared, places),
        out_shape=(VMEM((tokens, width), bf16),) + (VMEM((columns // KVH, tokens), bf16),) * count,
        in_specs=[vmem] * len(operands),
        out_specs=(vmem,) * (1 + count),
        cost_estimate=cost(2 * tokens * width * columns, 2 * tokens * width),
        compiler_params=params,
        name="keys_values",
    )(*operands)


def queries_kernel(widths, places, normed_ref, wq_ref, *refs):
    me = lax.axis_index("head")
    total, at = None, 0
    for place, width in zip(places, widths):
        term = dot(normed_ref[:, at : at + width], wq_ref[from_start(place(me), width), :])
        total = term if total is None else total + term
        at += width
    q = total.astype(bf16)
    if len(refs) == 1:
        refs[0][...] = q
        return
    piece_ref, fresh_ref, q_ref, bundle_ref = refs
    q_ref[...] = q
    late = bundle_ref.shape[1] - HD
    last = lax.axis_index("section") == lax.axis_size("section") - 1
    sent = jnp.where(last, fresh_ref[:, -late:].astype(f32), q[:, -late:].astype(f32))
    bundle_ref[:, :late] = sent.astype(bf16)
    bundle_ref[:, late:] = piece_ref[...]


def queries(normed, widths, places, wq, bundled=(), late=0):
    tokens = normed.shape[0]
    operands = [normed, *resident_in(wq), *bundled]
    out = [VMEM((tokens, wq.shape[1]), bf16)]
    if bundled:
        out.append(VMEM((tokens, late + HD), bf16))
    return pl.pallas_call(
        functools.partial(queries_kernel, widths, places),
        out_shape=tuple(out),
        in_specs=[vmem] * len(operands),
        out_specs=(vmem,) * len(out),
        cost_estimate=cost(2 * normed.size * wq.shape[1], 2 * normed.size),
        compiler_params=params,
        name="queries",
    )(*operands)


def openings_kernel(sections, doc_ref, first_ref, second_ref):
    tokens = first_ref.shape[0]
    for turn, out_ref in enumerate((first_ref, second_ref)):
        start = (sections - 1 + turn - lax.axis_index("section")) * tokens
        here = start + lax.broadcasted_iota(jnp.int32, out_ref.shape, 0)
        opened = jnp.zeros(out_ref.shape, jnp.int32)
        end = jnp.int32(0)
        for d in range(doc_ref.shape[0]):
            end = end + doc_ref[d]
            opened = jnp.where(end <= here, end, opened)
        out_ref[...] = opened


def openings(doc_lengths, tokens, sections):
    return pl.pallas_call(
        functools.partial(openings_kernel, sections),
        out_shape=(VMEM((tokens, HD), jnp.int32),) * 2,
        in_specs=[smem],
        out_specs=(vmem,) * 2,
        compiler_params=params,
        name="openings",
    )(doc_lengths)


def stacked_heads(q_ref, heads):
    return jnp.concatenate([q_ref[:, h * HD : (h + 1) * HD] for h in range(*heads)], axis=0)


def masked_scores(q, keys, opened_ref, query_start, key_start):
    tokens, count = opened_ref.shape[0], keys.shape[1]
    here = query_start + lax.broadcasted_iota(jnp.int32, (tokens, count), 0)
    there = key_start + lax.broadcasted_iota(jnp.int32, (tokens, count), 1)
    allowed = (there >= opened_ref[:, 0:1]) & (there <= here)
    scores = jnp.where(allowed[None], dot(q, keys).reshape(-1, tokens, count), masked_score)
    return scores.reshape(-1, count)


def mixed_and_sums(expon, values):
    both = jnp.concatenate([values, jnp.ones(values.shape, bf16)], axis=0)
    both = dot_turned(expon.astype(bf16), both)
    return both[:, :HD], both[:, HD:]


def put_together(me, pieces, flips, parts, gather):
    features = pieces[0].shape[0] // 2
    for flip, piece_ref in zip(flips, pieces):
        source = lax.bitwise_xor(me, jnp.int32(flip)) // parts
        piece = piece_ref[...].astype(f32)
        gather[0, rows_of(source, features), :] = piece[:features]
        gather[1, rows_of(source, features), :] = piece[features:]
    return gather[0].astype(bf16), gather[1].astype(bf16)


def peer_attend_kernel(sections, flips, parts, opened_ref, bundle_ref, x_ref, piece_ref, out_ref, gather):
    section = lax.axis_index("section")
    tokens, width = out_ref.shape
    start = (sections - 1 - section) * tokens
    pieces = [piece_ref, bundle_ref.at[:, width:]]
    keys, values = put_together(lax.axis_index("head"), pieces, flips, parts, gather)
    q = stacked_heads(bundle_ref, (0, width // HD))
    scores = masked_scores(q, keys, opened_ref, start, start)
    expon = jnp.exp2((scores - jnp.max(scores, axis=1, keepdims=True)) * score_scale)
    mixed, total = mixed_and_sums(expon, values)
    mixed = (mixed * (1.0 / total)).astype(bf16).astype(f32)
    for h in range(width // HD):
        columns = slice(h * HD, (h + 1) * HD)
        x = x_ref[:, x_ref.shape[1] - width + h * HD : x_ref.shape[1] - width + (h + 1) * HD].astype(f32)
        out = (x + mixed[h * tokens : (h + 1) * tokens]).astype(bf16).astype(f32)
        out = jnp.where(section == sections - 1, bundle_ref[:, columns].astype(f32), out)
        out_ref[:, columns] = out.astype(bf16)


def peer_attend(opened, bundle, x, piece, flips, parts, sections):
    tokens, width = x.shape[0], bundle.shape[1] - HD
    return pl.pallas_call(
        functools.partial(peer_attend_kernel, sections, flips, parts),
        out_shape=VMEM((tokens, width), bf16),
        in_specs=[vmem] * 4,
        out_specs=vmem,
        scratch_shapes=[VMEM((2, HD, tokens), f32)],
        cost_estimate=cost(1000, 1000),
        compiler_params=params,
        name="peer_attend",
    )(opened, bundle, x, piece)


def first_attend_kernel(sections, heads, flips, parts, opened_ref, q_ref, x_ref, fresh_ref, *refs):
    section = lax.axis_index("section")
    start = (sections - 1 - section) * q_ref.shape[0]
    if flips is None:
        keys_ref, values_ref, out_ref = refs
        keys, values = keys_ref[...], values_ref[...]
    else:
        pieces, (out_ref, keys_ref, values_ref, gather) = refs[: len(flips)], refs[len(flips) :]
        keys, values = put_together(lax.axis_index("head"), pieces, flips, parts, gather)
        keys_ref[...], values_ref[...] = keys, values
    tokens = q_ref.shape[0]
    scores = masked_scores(stacked_heads(q_ref, heads), keys, opened_ref, start, start)
    expon = jnp.exp2((scores - jnp.max(scores, axis=1, keepdims=True)) * score_scale)
    mixed, total = mixed_and_sums(expon, values)
    mixed = (mixed * (1.0 / total)).astype(bf16).astype(f32)
    for i, h in enumerate(range(*heads)):
        columns = slice(h * HD, (h + 1) * HD)
        out = (x_ref[:, columns].astype(f32) + mixed[i * tokens : (i + 1) * tokens]).astype(bf16)
        out = jnp.where(section == sections - 1, fresh_ref[:, columns].astype(f32), out.astype(f32))
        out_ref[:, i * HD : (i + 1) * HD] = out.astype(bf16)


def first_attend(opened, q, x, fresh, pieces, flips, parts, heads, sections):
    tokens = q.shape[0]
    out = (VMEM((tokens, (heads[1] - heads[0]) * HD), bf16),)
    scratch = []
    if flips is not None:
        out = out + (VMEM((HD, tokens), bf16),) * 2
        scratch = [VMEM((2, HD, tokens), f32)]
    operands = [opened, q, x, fresh, *pieces]
    return pl.pallas_call(
        functools.partial(first_attend_kernel, sections, heads, flips, parts),
        out_shape=out,
        in_specs=[vmem] * len(operands),
        out_specs=(vmem,) * len(out),
        scratch_shapes=scratch,
        cost_estimate=cost(10**10, 1000),
        compiler_params=params,
        name="first_attend",
    )(*operands)


def resident_kernel(sections, opened_ref, q_ref, keys_ref, values_ref, max_ref, sum_ref, mixed_ref):
    tokens = q_ref.shape[0]
    key_start = (sections - 1 - lax.axis_index("section")) * tokens
    q = stacked_heads(q_ref, (0, q_ref.shape[1] // HD))
    scores = masked_scores(q, keys_ref[...], opened_ref, key_start + tokens, key_start)
    top = jnp.max(scores, axis=1, keepdims=True)
    expon = jnp.exp2((scores - top) * score_scale)
    max_ref[...] = jnp.broadcast_to(top, max_ref.shape)
    mixed_ref[...], sum_ref[...] = mixed_and_sums(expon, values_ref[...])


def resident_attend(opened, q, keys, values, sections):
    rows = q.shape[0] * (q.shape[1] // HD)
    return pl.pallas_call(
        functools.partial(resident_kernel, sections),
        out_shape=(VMEM((rows, HD), f32),) * 3,
        in_specs=[vmem] * 4,
        out_specs=(vmem,) * 3,
        cost_estimate=cost(1000, 1000),
        compiler_params=params,
        name="resident_attend",
    )(opened, q, keys, values)


def second_attend_kernel(sections, flips, parts, x_count, opened_ref, q_ref, max_ref, sum_ref, mixed_ref, *refs):
    x_refs, refs = refs[:x_count], refs[x_count:]
    pieces, (out_ref, gather) = refs[: len(flips)], refs[len(flips) :]
    tokens, heads = q_ref.shape[0], q_ref.shape[1] // HD
    start = (sections - lax.axis_index("section")) * tokens
    keys, values = put_together(lax.axis_index("head"), pieces, flips, parts, gather)
    scores = masked_scores(stacked_heads(q_ref, (0, heads)), keys, opened_ref, start, start)
    top = jnp.maximum(jnp.max(scores, axis=1, keepdims=True), max_ref[...])
    expon = jnp.exp2((scores - top) * score_scale)
    shrink = jnp.exp2((max_ref[...] - top) * score_scale)
    mixed, total = mixed_and_sums(expon, values)
    total = total + shrink * sum_ref[...]
    mixed = mixed + shrink * mixed_ref[...]
    mixed = (mixed * (1.0 / total)).astype(bf16).astype(f32)
    where = [(x_ref, inside) for x_ref in x_refs for inside in range(0, x_ref.shape[1], HD)]
    for h, (x_ref, inside) in enumerate(where):
        out = x_ref[:, inside : inside + HD].astype(f32) + mixed[h * tokens : (h + 1) * tokens]
        out_ref[:, h * HD : (h + 1) * HD] = out.astype(bf16)


def second_attend(opened, q, xs, resident, pieces, flips, parts, sections):
    tokens = q.shape[0]
    operands = [opened, q, *resident, *xs, *pieces]
    return pl.pallas_call(
        functools.partial(second_attend_kernel, sections, flips, parts, len(xs)),
        out_shape=jax.ShapeDtypeStruct(q.shape, bf16),
        in_specs=[vmem] * len(operands),
        out_specs=vmem,
        scratch_shapes=[VMEM((2, HD, tokens), f32)],
        cost_estimate=cost(1000, 1000),
        compiler_params=params,
        name="second_attend",
    )(*operands)


def shards(entering, fresh_slice, norm_gain, w_query, w_key_value, doc_lengths):
    n = lax.axis_size("head")
    sections = lax.axis_size("section")
    own = entering[0]
    w_q, w_kv = w_query[0], w_key_value[0]
    tokens, width = own.shape
    heads = w_q.shape[1] // HD
    paired = n == 4
    parts = 2 if paired else 1
    flips = [0, 3] if paired else list(range(n))

    def moved(array, by, flip):
        pairs = [
            (s * n + h, ((s + by) % sections) * n + (h ^ flip)) for s in range(sections) for h in range(n)
        ]
        return lax.ppermute(array, ("section", "head"), pairs)

    def after(array, *others):
        return lax.optimization_barrier((array, *others))[0]

    def exchanged(xs, places, ssq, squared):
        normed, *pieces = keys_values(xs, places, gain, wkvs, choose, ssq, squared)
        received = [moved(piece, 0, flip) for piece, flip in zip(pieces[1:], flips[1:])]
        return normed, [pieces[0], *received], pieces, [x.shape[1] for x in xs]

    def rest_of(array):
        every = lax.all_gather(array, "head", axis=0)
        me = lax.axis_index("head")
        return [lax.dynamic_index_in_dim(every, (me + k) % n, 0, False) for k in range(1, n)]

    def place(flip, offset=0):
        return lambda me: lax.bitwise_xor(me, jnp.int32(flip)) * width + offset

    following = [functools.partial(lambda k, me: lax.rem(me + k, jnp.int32(n)) * width, k) for k in range(n)]

    if paired:
        over = moved(own, 0, 3)
        beside = moved(own, 0, 1)
        w_kv_beside = moved(w_kv, 0, 1)
    own, gain, wq, wkv, choose = load(own, norm_gain, w_q, w_kv, n, flips, parts)
    opened = openings(after(doc_lengths, gain), tokens, sections)
    if paired:
        wkvs = [wkv, w_kv_beside]
        over, *opened = lax.optimization_barrier((over, *opened))
        passed = moved(over, 0, 1)
        xs, places = [own, beside, over, passed], [place(0), place(1), place(3), place(2)]
        ssq, squared = squares([own, beside, over]), 3
    else:
        wkvs = [wkv]
        xs, places = [own, *rest_of(own)], following
        ssq, squared = squares([own]), 1
    normed, pieces, made, widths = exchanged(xs, places, ssq, squared)
    part = heads // 2 if paired else heads
    split = part * HD
    if paired:
        q, bundle = queries(normed, widths, places, wq, [made[0], fresh_slice], width - split)
        bundle = moved(bundle, 0, 3)
    else:
        (q,) = queries(normed, widths, places, wq)
    sent, keys, values = first_attend(
        opened[0], q, own, fresh_slice, pieces, flips, parts, (0, part), sections
    )

    if paired:
        a1 = moved(sent, 1, 1)
        (sent,) = first_attend(
            opened[0], q, own, fresh_slice, [keys, values], None, parts, (part, heads), sections
        )
        b1 = moved(sent, 1, 1)
        bundle = after(bundle, sent)
        peers = peer_attend(opened[0], bundle, over, made[1], flips, parts, sections)
        b2 = moved(peers, 1, 1)
        a1 = after(a1, peers)
        a2 = moved(a1, 0, 3)
        a0 = moved(a1, 0, 1)
        ssq = squares([a1])
        b1, ssq = lax.optimization_barrier((b1, ssq))
        b0 = moved(b1, 0, 1)
        ssq = squares([b1], [ssq])
        b2, ssq = lax.optimization_barrier((b2, ssq))
        b3 = moved(b2, 0, 1)
        a3 = moved(a2, 0, 1)
        ssq, squared = squares([a0, a2, b2], [ssq]), 5
        xs = [a1, b1, a0, a2, b2, a3, b0, b3]
        places = [place(1), place(1, split), place(0), place(2), place(2, split)]
        places += [place(3), place(0, split), place(3, split)]
        mine = [a0, b0]
    else:
        mine = [jnp.where(lax.axis_index("section") == 0, fresh_slice, moved(sent, 1, 0))]
        xs, places = [*mine, *rest_of(mine[0])], following
        ssq, squared = squares(mine), 1
    normed, pieces, _, widths = exchanged(xs, places, ssq, squared)
    (q,) = queries(normed, widths, places, wq)
    resident = resident_attend(opened[1], q, keys, values, sections)
    return second_attend(opened[1], q, mine, resident, pieces, flips, parts, sections)[None]


def solution(mesh):
    placed = (
        P("section", None, "head"),
        P(None, "head"),
        P("section", None),
        P("section", None, "head"),
        P("section", None, "head"),
        P(),
    )
    return jax.shard_map(
        shards, mesh=mesh, in_specs=placed, out_specs=P("section", None, "head"), check_vma=False
    )
```
